32 devices in a mesh: seq: 16 (over z, y, core), hd: 2 (over x).
Axes of the slice: x: 2, y: 2, z: 4, core: 2. Of those that a mesh axis runs over, the one named last changes fastest.
Arguments:
- tokens: bfloat16 [24576, 768], P(('seq', 'hd')), may hold values from -6 to 6
- image_ids: int32 [24576], P(('seq', 'hd')), may hold values from 0 to 11, as said below
- keep_masks: int32 [16, 12, 2], P('seq'), may hold values 0 or 1
- ln1_gain: float32 [768], replicated, may hold values from 0.5 to 1.5
- ln1_bias: float32 [768], replicated, may hold values from -4 to 4
- w_qkv: bfloat16 [768, 2304], replicated, may hold values from -0.21875 to 0.21875
- qv_bias: float32 [1536], replicated, may hold values from -6 to 6
- w_out: bfloat16 [768, 768], replicated, may hold values from -0.875 to 0.875
- b_out: float32 [768], replicated, may hold values from -4 to 4
- ln2_gain: float32 [768], replicated, may hold values from 0.5 to 1.5
- ln2_bias: float32 [768], replicated, may hold values from -4 to 4
- w_fc1: bfloat16 [768, 3072], replicated, may hold values from -0.21875 to 0.21875
- b_fc1: float32 [3072], replicated, may hold values from -6 to 6
- w_fc2: bfloat16 [3072, 768], replicated, may hold values from -0.109375 to 0.109375
- b_fc2: float32 [768], replicated, may hold values from -4 to 4
- cotangent: bfloat16 [24576, 768], P(('seq', 'hd')), may hold values from -6 to 6
Outputs:
- mixed: bfloat16 [24576, 768], P(('seq', 'hd'))
- grad_tokens: float32 [24576, 768], P(('seq', 'hd'))
- grad_ln1_gain: float32 [768], P(('seq', 'hd'))
- grad_ln1_bias: float32 [768], P(('seq', 'hd'))
- grad_w_qkv: float32 [768, 2304], P(('seq', 'hd'))
- grad_qv_bias: float32 [1536], P(('seq', 'hd'))
- grad_w_out: float32 [768, 768], P(('seq', 'hd'))
- grad_b_out: float32 [768], P(('seq', 'hd'))
- grad_ln2_gain: float32 [768], P(('seq', 'hd'))
- grad_ln2_bias: float32 [768], P(('seq', 'hd'))
- grad_w_fc1: float32 [768, 3072], P(('seq', 'hd'))
- grad_b_fc1: float32 [3072], P(('seq', 'hd'))
- grad_w_fc2: float32 [3072, 768], P(('seq', 'hd'))
- grad_b_fc2: float32 [768], P(('seq', 'hd'))
The draws below stay inside these ranges and needn't reach their ends.
Inputs may be any that keep to these rules, and one draw needn't show every extreme that they name: `image_ids`: within each pack of 1536 rows the image number starts at 0 and rises by one from image to image; images are runs of 102, 198 or 578 rows, except that the image just before a 578-row image and the pack's last image may be cut short; a 578-row image covers rows 767 and 768 of every pack.
All inputs are finite; a program needn't handle non-finite values. No bound on the sum of `keep_masks` on one device may be relied on, other than what follows from the above.
Results may differ from the reference program's by a relative error of at most 0.0095.
Values may be sent and summed in bfloat16 or wider, within the bound.
A program may use at most 192 MiB of HBM per device.

```python
import jax
import jax.numpy as jnp
from jax import lax

HEADS = 12
HEAD = 64
D = 768
FF = 3072
TOK_DEV = 768
SMALL_IMG = 102
MID_IMG = 198
BIG_IMG = 578
SLOTS = 12
TOKENS = 24576
N_SEQ = 16
N_HD = 2


def draw_image_ids(key, part):
    key = jax.random.fold_in(key, 7)
    group_rows = 2 * TOK_DEV
    pack_count = TOKENS // group_rows
    length_table = jnp.array([SMALL_IMG, MID_IMG, BIG_IMG], jnp.int32)
    slot_count = group_rows // SMALL_IMG + 1
    lowest_start = TOK_DEV - BIG_IMG + 1
    fullest_start = lowest_start + (1 - lowest_start) % SMALL_IMG
    chosen_key, packs_key = jax.random.split(key)
    chosen_pack = jax.random.randint(chosen_key, (), 0, pack_count).astype(jnp.int32)

    def one_pack(pack_key, pack_index):
        first_key, second_key, third_key = jax.random.split(pack_key, 3)
        is_full = pack_index == chosen_pack
        drawn_start = jax.random.randint(first_key, (), lowest_start, TOK_DEV).astype(jnp.int32)
        big_start = jnp.where(is_full, fullest_start, drawn_start).astype(jnp.int32)
        kinds_before = jnp.where(is_full, 0, jax.random.randint(second_key, (slot_count,), 0, 3))
        kinds_after = jnp.where(is_full, 0, jax.random.randint(third_key, (slot_count,), 0, 3))
        ends_before = jnp.cumsum(length_table[kinds_before])
        ends_after = jnp.cumsum(length_table[kinds_after])
        position = jnp.arange(group_rows, dtype=jnp.int32)
        seg_before = jnp.sum((ends_before[None, :] <= position[:, None]).astype(jnp.int32), axis=1)
        big_number = jnp.sum((ends_before <= big_start - 1).astype(jnp.int32)) + 1
        relative = position - big_start - BIG_IMG
        seg_after = jnp.sum((ends_after[None, :] <= relative[:, None]).astype(jnp.int32), axis=1)
        return jnp.where(position < big_start, seg_before, jnp.where(relative < 0, big_number, big_number + 1 + seg_after)).astype(jnp.int32)
    pack_keys = jax.random.split(packs_key, pack_count)
    indices = jnp.arange(pack_count, dtype=jnp.int32)
    return jax.vmap(one_pack)(pack_keys, indices).reshape(-1).astype(jnp.int32)


def touch_ends(values, stream_key, least, top_value):
    longest = values.shape.index(max(values.shape))
    spots = []
    for shift in (0, 1):
        where = [jax.random.randint(jax.random.fold_in(stream_key, axis), (), 0, length) for axis, length in enumerate(values.shape)]
        where[longest] = (where[longest] + shift) % values.shape[longest]
        spots.append(tuple(where))
    return values.at[spots[0]].set(least).at[spots[1]].set(top_value)


def level_of(rng, shape, cuts, least, high):
    def one(dim, parts):
        steps = jax.random.uniform(jax.random.fold_in(jax.random.fold_in(rng, 6), dim), (parts,), jnp.float32, least / len(cuts), high / len(cuts))
        return jnp.repeat(jnp.exp(steps), shape[dim] // parts).reshape((-1,) + (1,) * (len(shape) - dim - 1))

    level = one(*cuts[0])
    for cut in cuts[1:]:
        level = level * one(*cut)
    return level


def centred(key, dims, width, limit, cuts=(), held_as=jnp.bfloat16):
    result = jax.random.normal(key, dims, jnp.float32) * width
    if len(cuts) > 0:
        result = level_of(key, dims, cuts, -0.22, 0.18) * result
    return jnp.clip(result, min=-limit, max=limit).astype(held_as)


def setup_inputs(seed: int = 0) -> dict:
    key_of = jax.random.split(jax.random.key(seed), 17)
    return {
        "tokens": centred(key_of[0], (TOKENS, D), 1.0, 6.0, ((0, 32),)),
        "image_ids": draw_image_ids(jax.random.fold_in(key_of[16], 71), 0),
        "keep_masks": touch_ends((jax.random.randint(key_of[2], (N_SEQ, SLOTS, 2), 0, 10) < 9).astype(jnp.int32), jax.random.fold_in(key_of[2], 1), 0, 1),
        "ln1_gain": jnp.clip(1.0 + 0.1 * jax.random.normal(key_of[3], (D,), jnp.float32), 0.5, 1.5),
        "ln1_bias": centred(key_of[4], (D,), 0.3, 4.0, (), jnp.float32),
        "w_qkv": centred(key_of[5], (D, 3 * D), D ** -0.5, 0.21875),
        "qv_bias": centred(key_of[6], (2 * D,), 0.5, 6.0, (), jnp.float32),
        "w_out": centred(key_of[7], (D, D), (D // 16) ** -0.5, 0.875),
        "b_out": centred(key_of[8], (D,), 0.3, 4.0, (), jnp.float32),
        "ln2_gain": jnp.clip(1.0 + 0.1 * jax.random.normal(key_of[9], (D,), jnp.float32), 0.5, 1.5),
        "ln2_bias": centred(key_of[10], (D,), 0.3, 4.0, (), jnp.float32),
        "w_fc1": centred(key_of[11], (D, FF), D ** -0.5, 0.21875),
        "b_fc1": centred(key_of[12], (FF,), 0.5, 6.0, (), jnp.float32),
        "w_fc2": centred(key_of[13], (FF, D), FF ** -0.5, 0.109375),
        "b_fc2": centred(key_of[14], (D,), 0.3, 4.0, (), jnp.float32),
        "cotangent": centred(key_of[15], (TOKENS, D), 1.0, 6.0, ((0, 32),)),
    }


ln_epsilon = 1e-06
drop_scale = 1.0 / 0.9
masked_score = -1e+30

@jax.custom_vjp
def low(v):
    return lax.optimization_barrier(v.astype(jnp.bfloat16)).astype(jnp.float32)

@jax.custom_vjp
def low_back(v):
    return v

def low_keep(v):
    return (low(v), None)

def low_pass(kept, grad):
    return (grad,)

def back_keep(v):
    return (v, None)

def back_low(kept, grad):
    return (low(grad),)
low.defvjp(low_keep, low_pass)
low_back.defvjp(back_keep, back_low)

def layer_norm(values, gain_row, bias_row):
    center = values - lax.optimization_barrier(jnp.mean(values, -1, keepdims=True))
    variance = lax.optimization_barrier(jnp.mean(center * center, -1, keepdims=True))
    return center * lax.rsqrt(variance + ln_epsilon) * gain_row + bias_row

def product(left_side, right_side):
    return jnp.dot(left_side, right_side, precision=lax.Precision.HIGHEST, preferred_element_type=jnp.float32)

def head_attention(queries, keys_head, values_head, same_image):
    score_scale = HEAD ** (-0.5)
    scores = low_back(product(queries, keys_head.T) * score_scale)
    scores = jnp.where(same_image, scores, masked_score)
    chances = low(jax.nn.softmax(scores, axis=-1))
    return product(chances, values_head)

def layer_forward(inputs, keep_rows, same_image, ln1_gain, ln1_bias, w_qkv, qv_bias, w_out, b_out, ln2_gain, ln2_bias, w_fc1, b_fc1, w_fc2, b_fc2):
    group_rows = inputs.shape[0]
    normed_first = low(layer_norm(inputs, ln1_gain, ln1_bias))
    bias_all = jnp.concatenate([qv_bias[:D], jnp.zeros((D,), qv_bias.dtype), qv_bias[D:]])
    projected = low(low_back(product(normed_first, w_qkv) + bias_all))
    split_heads = projected.reshape(group_rows, 3, HEADS, HEAD).transpose(1, 2, 0, 3)
    checked = jax.checkpoint(head_attention)
    attended = lax.map(lambda triple: checked(triple[0], triple[1], triple[2], same_image), (split_heads[0], split_heads[1], split_heads[2]))
    attended = low(low_back(attended.transpose(1, 0, 2).reshape(group_rows, D)))
    branch = low_back(product(attended, w_out) + b_out)
    middle = inputs + keep_rows[:, 0:1] * branch
    normed_second = low(layer_norm(middle, ln2_gain, ln2_bias))
    hidden_pre = low_back(product(normed_second, w_fc1) + b_fc1)
    activated = low(jax.nn.gelu(hidden_pre, approximate=False))
    mlp_out = low_back(product(activated, w_fc2) + b_fc2)
    return middle + keep_rows[:, 1:2] * mlp_out

def reference(tokens, image_ids, keep_masks, ln1_gain, ln1_bias, w_qkv, qv_bias, w_out, b_out, ln2_gain, ln2_bias, w_fc1, b_fc1, w_fc2, b_fc2, cotangent):
    weights = tuple((source.astype(jnp.float32) for source in (ln1_gain, ln1_bias, w_qkv, qv_bias, w_out, b_out, ln2_gain, ln2_bias, w_fc1, b_fc1, w_fc2, b_fc2)))
    group_rows = N_HD * TOK_DEV
    inputs = tokens.astype(jnp.float32).reshape(N_SEQ, group_rows, D)
    owners = image_ids.reshape(N_SEQ, group_rows)
    grads_in = cotangent.astype(jnp.float32).reshape(N_SEQ, group_rows, D)

    def group_step(grad_total, item):
        group_inputs, group_ids, group_keep, group_cot = item
        keep_rows = group_keep.astype(jnp.float32)[group_ids] * drop_scale
        same_image = group_ids[:, None] == group_ids[None, :]

        def forward_fn(values_in, *params):
            return layer_forward(values_in, keep_rows, same_image, *params)
        outputs, pull_back = jax.vjp(forward_fn, group_inputs, *weights)
        grads = pull_back(group_cot)
        new_total = tuple((earlier + later for earlier, later in zip(grad_total, grads[1:])))
        return (new_total, (outputs.astype(jnp.bfloat16), grads[0]))
    start_total = tuple((jnp.zeros_like(source) for source in weights))
    grad_total, (mixed_all, grad_input) = lax.scan(group_step, start_total, (inputs, owners, keep_masks, grads_in))
    return (mixed_all.reshape(TOKENS, D), grad_input.reshape(TOKENS, D), grad_total[0], grad_total[1], grad_total[2], grad_total[3], grad_total[4], grad_total[5], grad_total[6], grad_total[7], grad_total[8], grad_total[9], grad_total[10], grad_total[11])
```

```python
import functools
import jax, jax.numpy as jnp
from jax import lax
from jax.experimental import pallas as pl
from jax.experimental.pallas import tpu as pltpu
from jax.sharding import PartitionSpec as P

HEADS, HEAD = 12, 64
T = 128
VM = pl.BlockSpec(memory_space=pltpu.VMEM)
SM = pl.BlockSpec(memory_space=pltpu.SMEM)
F32, BF16 = jnp.float32, jnp.bfloat16
NT = (((1,), (1,)), ((), ()))
TN = (((0,), (0,)), ((), ()))


def mm(a, b):
    return jnp.dot(a, b, preferred_element_type=F32)


def mm_nt(a, b):
    return lax.dot_general(a, b, NT, preferred_element_type=F32)


def mm_tn(a, b):
    return lax.dot_general(a, b, TN, preferred_element_type=F32)


def by_head(pair):
    lane = lax.broadcasted_iota(jnp.int32, pair.shape, 1)
    zero = jnp.zeros_like(pair)
    return jnp.concatenate(
        [jnp.where(lane < HEAD, pair, zero), jnp.where(lane < HEAD, zero, pair)], 0
    )


def attn_forward_kernel(width, tiles, low_ref, high_ref, off_ref, qkv, id_col, id_row, out, lse, sc, peak, total, acc):
    pairs = width // 128
    own = out.shape[0] // T
    off = off_ref[0]

    @pl.loop(0, own)
    def _(i):
        tile = off + i
        q0 = pl.multiple_of(tile * T, T)
        low, high = low_ref[tile], high_ref[tile]
        ids = id_col[pl.ds(q0, T), :]
        for p in range(pairs):
            peak[p] = jnp.full((T, 2 * T), -jnp.inf, F32)
            total[p] = jnp.zeros((T, 2 * T), F32)
            acc[p] = jnp.zeros((T, 128), F32)

        @pl.loop(low, high)
        def _(j):
            k0 = pl.multiple_of(j * T, T)
            same = ids == id_row[j]
            for p in range(pairs):
                q = qkv[pl.ds(q0, T), p * 128 : p * 128 + 128] * BF16(HEAD**-0.5)
                k = by_head(qkv[pl.ds(k0, T), width + p * 128 : width + p * 128 + 128])
                s = mm_nt(q, k)
                s = jnp.concatenate([jnp.where(same, s[:, :T], -1e30), jnp.where(same, s[:, T:], -1e30)], 1)
                sc[p, j - low] = s
                peak[p] = jnp.maximum(peak[p], s)

        for p in range(pairs):
            m = peak[p]
            peak[p] = jnp.concatenate(
                [
                    jnp.broadcast_to(jnp.max(m[:, :T], -1, keepdims=True), (T, T)),
                    jnp.broadcast_to(jnp.max(m[:, T:], -1, keepdims=True), (T, T)),
                ],
                1,
            )

        @pl.loop(low, high)
        def _(j):
            k0 = pl.multiple_of(j * T, T)
            for p in range(pairs):
                v = by_head(qkv[pl.ds(k0, T), 2 * width + p * 128 : 2 * width + p * 128 + 128])
                e = jnp.exp(sc[p, j - low] - peak[p])
                total[p] += e
                acc[p] += mm(e.astype(BF16), v)

        lane = lax.broadcasted_iota(jnp.int32, (T, 128), 1)
        gathered = jnp.zeros((T, 128), F32)
        for p in range(pairs):
            t = total[p]
            t0 = jnp.sum(t[:, :T], -1, keepdims=True)
            t1 = jnp.sum(t[:, T:], -1, keepdims=True)
            inv = jnp.where(lane < HEAD, 1.0 / t0, 1.0 / t1)
            out[pl.ds(pl.multiple_of(i * T, T), T), p * 128 : p * 128 + 128] = (acc[p] * inv).astype(BF16)
            l0 = peak[p][:, 0:1] + jnp.log(t0)
            l1 = peak[p][:, T : T + 1] + jnp.log(t1)
            gathered = jnp.where(lane == 2 * p, l0, jnp.where(lane == 2 * p + 1, l1, gathered))
        lse[i] = gathered.T[: lse.shape[1], :]


def attn_forward(low, high, off, qkv, id_col, id_row, own_rows):
    all_rows, columns = qkv.shape
    width = columns // 3
    tiles = all_rows // T
    pairs = width // 128
    return pl.pallas_call(
        functools.partial(attn_forward_kernel, width, tiles),
        out_shape=(
            jax.ShapeDtypeStruct((own_rows, width), BF16),
            jax.ShapeDtypeStruct((own_rows // T, 16, T), F32),
        ),
        in_specs=[SM, SM, SM, VM, VM, VM],
        out_specs=(VM, VM),
        scratch_shapes=[
            pltpu.VMEM((pairs, tiles, T, 2 * T), F32),
            pltpu.VMEM((pairs, T, 2 * T), F32),
            pltpu.VMEM((pairs, T, 2 * T), F32),
            pltpu.VMEM((pairs, T, 128), F32),
        ],
        compiler_params=pltpu.CompilerParams(vmem_limit_bytes=56 * 2**20),
        name="attention_forward",
    )(low, high, off, qkv, id_col, id_row)


def attn_backward_kernel(width, tiles, low_ref, high_ref, off_ref, qkv, do, id_col, id_row, lse, delta, out, dq, dk, dv):
    pairs = width // 128
    own = out.shape[0] // T
    off = off_ref[0]
    dq[...] = jnp.zeros_like(dq)

    @pl.loop(0, tiles)
    def _(j):
        k0 = pl.multiple_of(j * T, T)
        mine = jnp.logical_and(j >= off, j < off + own)
        low = jnp.where(mine, low_ref[j], jnp.maximum(low_ref[j], off))
        high = jnp.where(mine, high_ref[j], jnp.minimum(high_ref[j], off + own))
        ids = id_col[pl.ds(k0, T), :]
        for p in range(pairs):
            dk[p] = jnp.zeros((T, 128), F32)
            dv[p] = jnp.zeros((T, 128), F32)

        @pl.loop(low, high)
        def _(i):
            q0 = pl.multiple_of(i * T, T)
            same = ids == id_row[i]
            for p in range(pairs):
                cols = p * 128
                k = qkv[pl.ds(k0, T), width + cols : width + cols + 128]
                v = qkv[pl.ds(k0, T), 2 * width + cols : 2 * width + cols + 128]
                q = by_head(qkv[pl.ds(q0, T), cols : cols + 128] * BF16(HEAD**-0.5))
                g = by_head(do[pl.ds(q0, T), cols : cols + 128])
                s = mm_nt(k, q)
                dp = mm_nt(v, g)
                es, ds = [], []
                for h in range(2):
                    sh = jnp.where(same, s[:, h * T : h * T + T], -1e30)
                    e = jnp.exp(sh - lse[i, 2 * p + h : 2 * p + h + 1, :])
                    es.append(e.astype(BF16))
                    ds.append((e * (dp[:, h * T : h * T + T] - delta[i, 2 * p + h : 2 * p + h + 1, :])).astype(BF16))
                dsc = jnp.concatenate(ds, 1)
                dv[p] += mm(jnp.concatenate(es, 1), g)
                dk[p] += mm(dsc, q)
                both = by_head(k)
                dq[i, :, cols : cols + 128] += mm_tn(jnp.concatenate(ds, 0), both)

        @pl.when(mine)
        def _():
            r0 = pl.multiple_of((j - off) * T, T)
            for p in range(pairs):
                cols = p * 128
                out[pl.ds(r0, T), width + cols : width + cols + 128] = dk[p].astype(BF16)
                out[pl.ds(r0, T), 2 * width + cols : 2 * width + cols + 128] = dv[p].astype(BF16)

    @pl.loop(0, own)
    def _(i):
        out[pl.ds(pl.multiple_of(i * T, T), T), 0:width] = (dq[off + i] * HEAD**-0.5).astype(BF16)


def attn_backward(low, high, off, qkv, do, id_col, id_row, lse, delta, own_rows):
    all_rows, columns = qkv.shape
    width = columns // 3
    tiles = all_rows // T
    pairs = width // 128
    return pl.pallas_call(
        functools.partial(attn_backward_kernel, width, tiles),
        out_shape=jax.ShapeDtypeStruct((own_rows, columns), BF16),
        in_specs=[SM, SM, SM] + [VM] * 6,
        out_specs=VM,
        scratch_shapes=[
            pltpu.VMEM((tiles, T, width), F32),
            pltpu.VMEM((pairs, T, 128), F32),
            pltpu.VMEM((pairs, T, 128), F32),
        ],
        compiler_params=pltpu.CompilerParams(vmem_limit_bytes=56 * 2**20),
        name="attention_backward",
    )(low, high, off, qkv, do, id_col, id_row, lse, delta)


ln_epsilon = 1e-06
drop_scale = 1.0 / 0.9


MESH = pl.DeviceIdType.MESH


class Place:
    def __init__(self):
        self.seq = lax.axis_index("seq")
        self.x = lax.axis_index("hd")
        self.c = lax.rem(self.seq, 2)
        self.y = lax.rem(self.seq // 2, 2)
        self.z = self.seq // 4

    def partner(self, axis):
        if axis == "c":
            return (self.seq + 1 - 2 * self.c, self.x)
        if axis == "y":
            return (self.seq + 2 - 4 * self.y, self.x)
        return (self.seq, 1 - self.x)

    def level(self, step):
        return (lax.rem(self.z + step, 4) * 4 + lax.rem(self.seq, 4), self.x)

    def index(self, axis):
        return {"x": self.x, "y": self.y, "c": self.c}[axis]


def greet(place):
    barrier = pltpu.get_barrier_semaphore()
    others = [place.partner(a) for a in "cxy"] + [place.level(d) for d in (1, 2, 3)]
    for other in others:
        pl.semaphore_signal(barrier, inc=1, device_id=other, device_id_type=MESH)
    pl.semaphore_wait(barrier, len(others))


def send(source, target, send_sem, recv_sem, other):
    copy = pltpu.make_async_remote_copy(
        src_ref=source, dst_ref=target, send_sem=send_sem, recv_sem=recv_sem, device_id=other, device_id_type=MESH
    )
    copy.start()
    return copy


class Flow:
    def __init__(self, place, axes, g, r0, r1, r2, r3, sems, recvs):
        self.place, self.axes, self.g = place, axes, g
        self.r0, self.r1, self.r2, self.r3 = r0, r1, r2, r3
        self.sems, self.recvs = sems, recvs
        self.copies = []

    def start(self):
        p = self.place
        self.copies.append(send(self.g.at[1 - p.c], self.r0, self.sems.at[0], self.recvs.at[0], p.partner("c")))

    def first(self):
        p = self.place
        self.copies[0].wait_recv()
        me = p.index(self.axes[0])

        def add(half):
            @pl.loop(0, 8)
            def _(i):
                b, z = i // 4, lax.rem(i, 4)
                self.r0[half, b, z] = self.r0[half, b, z] + self.g[p.c, half, b, z]

        add(1 - me)
        self.copies.append(
            send(self.r0.at[1 - me], self.r1, self.sems.at[1], self.recvs.at[1], p.partner(self.axes[0]))
        )
        add(me)

    def second(self):
        p = self.place
        self.copies[1].wait_recv()
        me, before = p.index(self.axes[1]), p.index(self.axes[0])

        def add(half):
            @pl.loop(0, 4)
            def _(z):
                self.r1[half, z] = self.r1[half, z] + self.r0[before, half, z]

        add(1 - me)
        self.copies.append(
            send(self.r1.at[1 - me], self.r2, self.sems.at[2], self.recvs.at[2], p.partner(self.axes[1]))
        )
        add(me)

    def third(self):
        p = self.place
        self.copies[2].wait_recv()
        before = p.index(self.axes[1])

        @pl.loop(0, 4)
        def _(z):
            self.r2[z] = self.r2[z] + self.r1[before, z]

        for d in (1, 2, 3):
            target = lax.rem(p.z + d, 4)
            self.copies.append(
                send(self.r2.at[target], self.r3.at[d - 1], self.sems.at[2 + d], self.recvs.at[2 + d], p.level(d))
            )

    def last(self):
        p = self.place
        total = self.r2[p.z].astype(F32)
        for d in (1, 2, 3):
            self.copies[2 + d].wait_recv()
            total = total + self.r3[d - 1].astype(F32)
        return total

    def finish(self):
        for copy in self.copies:
            copy.wait_send()


def flow_scratch(rows, cols):
    return [
        pltpu.VMEM((2, 2, 4, rows, cols), BF16),
        pltpu.VMEM((2, 4, rows, cols), BF16),
        pltpu.VMEM((4, rows, cols), BF16),
        pltpu.VMEM((3, rows, cols), BF16),
        pltpu.SemaphoreType.DMA((6,)),
        pltpu.SemaphoreType.DMA((6,)),
    ]


class ChunkFlow(Flow):
    def __init__(self, place, axes, home, *refs):
        super().__init__(place, axes, *refs)
        self.home = home

    def third(self):
        p = self.place
        self.copies[2].wait_recv()
        self.r2[...] = self.r2[...] + self.r1[p.index(self.axes[1])]
        slot = lax.rem(p.z - self.home + 3, 4)
        self.hop = pltpu.make_async_remote_copy(
            src_ref=self.r2,
            dst_ref=self.r3.at[slot],
            send_sem=self.sems.at[3],
            recv_sem=self.recvs.at[3 + slot],
            device_id=(self.home * 4 + lax.rem(p.seq, 4), p.x),
            device_id_type=MESH,
        )

        @pl.when(p.z != self.home)
        def _():
            self.hop.start()

    def first(self):
        p = self.place
        self.copies[0].wait_recv()
        me = p.index(self.axes[0])

        def add(half):
            for b in range(2):
                self.r0[half, b] = self.r0[half, b] + self.g[p.c, half, b]

        add(1 - me)
        self.copies.append(
            send(self.r0.at[1 - me], self.r1, self.sems.at[1], self.recvs.at[1], p.partner(self.axes[0]))
        )
        add(me)

    def second(self):
        p = self.place
        self.copies[1].wait_recv()
        me, before = p.index(self.axes[1]), p.index(self.axes[0])
        self.r1[1 - me] = self.r1[1 - me] + self.r0[before, 1 - me]
        self.copies.append(
            send(self.r1.at[1 - me], self.r2, self.sems.at[2], self.recvs.at[2], p.partner(self.axes[1]))
        )
        self.r1[me] = self.r1[me] + self.r0[before, me]

    def last_into(self, out):
        p = self.place

        @pl.when(p.z == self.home)
        def _():
            total = self.r2[...].astype(F32)
            for slot in range(3):
                pltpu.make_async_remote_copy(
                    src_ref=self.r2,
                    dst_ref=self.r3.at[slot],
                    send_sem=self.sems.at[3],
                    recv_sem=self.recvs.at[3 + slot],
                    device_id=p.level(1),
                    device_id_type=MESH,
                ).wait_recv()
                total = total + self.r3[slot].astype(F32)
            out[...] = total

    def finish(self):
        super().finish()

        @pl.when(self.place.z != self.home)
        def _():
            self.hop.wait_send()


def chunk_scratch(rows, cols):
    return [
        pltpu.VMEM((2, 2, rows, cols), BF16),
        pltpu.VMEM((2, rows, cols), BF16),
        pltpu.VMEM((rows, cols), BF16),
        pltpu.VMEM((3, rows, cols), BF16),
        pltpu.SemaphoreType.DMA((6,)),
        pltpu.SemaphoreType.DMA((6,)),
    ]


def row_norm(x):
    mean = jnp.mean(x, -1, keepdims=True)
    center = x - mean
    rstd = lax.rsqrt(jnp.mean(center * center, -1, keepdims=True) + ln_epsilon)
    return center * rstd, rstd


def norm_back(hat, rstd, gain, grad):
    scaled = grad * gain
    return rstd * (scaled - jnp.mean(scaled, -1, keepdims=True) - hat * jnp.mean(scaled * hat, -1, keepdims=True))


def col_sum(x):
    return jnp.sum(x, 0, keepdims=True)


def put_blocks(product, z, axes, g):
    half = product.shape[1] // 2
    for y in range(2):
        for c in range(2):
            for x in range(2):
                r = ((y * 2 + c) * 2 + x) * 24
                block = jnp.concatenate([product[r : r + 24, :half], product[r : r + 24, half:]], 0)
                at = {"x": x, "y": y}
                g[c, at[axes[0]], at[axes[1]], z] = block.astype(BF16)


def put_chunk(product, y, axes, g):
    for c in range(2):
        for x in range(2):
            r = (c * 2 + x) * 96
            at = {"x": x, "y": y}
            g[c, at[axes[0]], at[axes[1]]] = product[r : r + 96].astype(BF16)


R = 256
FLOW_REFS = 6


def mlp_kernel(reduce, chunks, *refs):
    o, x, keep, cot, w_out, b_out, gain, bias, w1, b1, w2, b2 = refs[:12]
    mixed, dx1, do, delta, small, g_out, out1, out2 = refs[12:20]
    v1, v2, x1s, n2s, n2t, dms, gs, dus, macc, nacc, load1, load2 = refs[20:32]
    flow_refs = refs[32:]
    das = gs
    owner = lax.broadcasted_iota(jnp.int32, (16, o.shape[1]), 1) // HEAD
    heads = (owner == lax.broadcasted_iota(jnp.int32, (16, o.shape[1]), 0)).astype(BF16)
    rows, width = o.shape
    tiles = rows // R
    loads = []
    for k in range(chunks):
        cols = pl.ds(k * width, width)
        loads.append(
            (
                pltpu.make_async_copy(w1.at[:, cols], v1.at[k], load1.at[k]),
                pltpu.make_async_copy(w2.at[cols, :], v2.at[k], load2.at[k]),
            )
        )
        loads[k][0].start()
        loads[k][1].start()
    if reduce:
        place = Place()
        greet(place)
        per = 1 + FLOW_REFS
        flows1 = [Flow(place, "xy", *flow_refs[2 * per * k : 2 * per * k + per]) for k in range(chunks)]
        flows2 = [ChunkFlow(place, "yx", k, *flow_refs[2 * per * k + per : 2 * per * (k + 1)]) for k in range(chunks)]

    small[...] = jnp.zeros_like(small)

    @pl.loop(0, tiles)
    def _(t):
        r = pl.ds(pl.multiple_of(t * R, R), R)
        x1 = x[r, :].astype(F32) + keep[r, 0:1] * (mm(o[r, :], w_out[...]) + b_out[...])
        x1s[r, :] = x1
        hat, _ = row_norm(x1)
        n2 = (hat * gain[...] + bias[...]).astype(BF16)
        n2s[r, :] = n2
        dm = (cot[r, :].astype(F32) * keep[r, 1:2]).astype(BF16)
        dms[r, :] = dm
        small[7:8, :] += col_sum(dm.astype(F32))

    n2t[...] = n2s[...].T

    for k in range(chunks):
        loads[k][0].wait()
        loads[k][1].wait()

        @pl.loop(0, tiles)
        def _(t):
            r = pl.ds(pl.multiple_of(t * R, R), R)
            u = mm(n2s[r, :], v1[k]) + b1[:, k * width : k * width + width]
            dg = mm_nt(dms[r, :], v2[k])
            cdf = 0.5 + 0.5 * lax.erf(u * 0.7071067811865476)
            pdf = jnp.exp(u * u * -0.5) * 0.3989422804014327
            g = (u * cdf).astype(BF16)
            du = (dg * (cdf + u * pdf)).astype(BF16)
            gs[r, :] = g
            dus[r, :] = du
            small[3 + k : 4 + k, :] += col_sum(du.astype(F32))
            if k == 0:
                macc[r, :] = mm(g, v2[k])
                nacc[r, :] = mm_nt(du, v1[k])
            else:
                macc[r, :] += mm(g, v2[k])
                nacc[r, :] += mm_nt(du, v1[k])

        if reduce:
            if k >= 2:
                flows1[k - 2].third()
                flows2[k - 2].third()
            if k >= 1:
                flows1[k - 1].first()
                flows2[k - 1].first()

            @pl.loop(0, 2)
            def _(y):
                product = mm_tn(gs[:, pl.ds(pl.multiple_of(y * 384, 384), 384)], dms[...])
                put_chunk(product, y, "yx", flows2[k].g)

            flows2[k].start()

            @pl.loop(0, 4)
            def _(z):
                product = mm(n2t[pl.ds(pl.multiple_of(z * 192, 64), 192), :], dus[...])
                put_blocks(product, z, "xy", flows1[k].g)

            flows1[k].start()
            if k >= 1:
                flows1[k - 1].second()
                flows2[k - 1].second()
        else:

            @pl.loop(0, 3)
            def _(t):
                r = pl.ds(pl.multiple_of(t * 256, 256), 256)
                out2[pl.ds(pl.multiple_of(k * width + t * 256, 256), 256), :] = mm_tn(gs[:, r], dms[...]).astype(BF16)
                out1[r, k * width : k * width + width] = mm(n2t[r, :], dus[...]).astype(BF16)

    last = chunks - 1
    n2t[...] = o[...].T
    if reduce:
        flows1[last].first()
        flows2[last].first()
        flows1[last - 1].third()
        flows2[last - 1].third()

    @pl.loop(0, tiles)
    def _(t):
        r = pl.ds(pl.multiple_of(t * R, R), R)
        hat, rstd = row_norm(x1s[r, :])
        dn2 = nacc[r, :]
        dx = cot[r, :].astype(F32) + norm_back(hat, rstd, gain[...], dn2)
        dx1[r, :] = dx
        da = (dx * keep[r, 0:1]).astype(BF16)
        das[r, :] = da
        grad_o = mm_nt(da, w_out[...]).astype(BF16)
        do[r, :] = grad_o
        small[0:1, :] += col_sum(da.astype(F32))
        small[1:2, :] += col_sum(dn2 * hat)
        small[2:3, :] += col_sum(dn2)
        prod = grad_o.astype(F32) * o[r, :].astype(F32)
        high = prod.astype(BF16)
        low = (prod - high.astype(F32)).astype(BF16)
        sums = mm_nt(heads, high) + mm_nt(heads, low)
        for s in range(R // T):
            delta[t * (R // T) + s] = sums[:, s * T : s * T + T]

    if reduce:
        flows1[last].second()
        flows2[last].second()

        @pl.loop(0, 4)
        def _(z):
            product = mm(n2t[pl.ds(pl.multiple_of(z * 192, 64), 192), :], das[...])
            put_blocks(product, z, "xy", g_out)
    else:

        @pl.loop(0, 3)
        def _(t):
            r = pl.ds(pl.multiple_of(t * 256, 256), 256)
            g_out[r, :] = mm(n2t[r, :], das[...]).astype(BF16)

    @pl.loop(0, tiles)
    def _(t):
        r = pl.ds(pl.multiple_of(t * R, R), R)
        mixed[r, :] = (x1s[r, :] + keep[r, 1:2] * (macc[r, :] + b2[...])).astype(BF16)

    if reduce:
        half = width // 2

        def keep_share(k):
            total = flows1[k].last()
            out1[:, k * width : k * width + half] = total[:24]
            out1[:, k * width + half : (k + 1) * width] = total[24:]
            flows2[k].last_into(out2)

        for k in range(last):
            keep_share(k)
        flows1[last].third()
        flows2[last].third()
        keep_share(last)
        for k in range(chunks):
            flows1[k].finish()
            flows2[k].finish()


def mlp_step(reduce, o, x, keep, cot, w_out, b_out, gain, bias, w1, b1, w2, b2):
    rows, width = o.shape
    chunks = w1.shape[1] // width
    block = lambda dims, kind: jax.ShapeDtypeStruct(dims, kind)
    outs = [
        block((rows, width), BF16),
        block((rows, width), F32),
        block((rows, width), BF16),
        block((rows // T, 16, T), F32),
        block((16, width), F32),
    ]
    if reduce:
        outs += [block((2, 2, 2, 4, 48, width // 2), BF16), block((24, chunks * width), F32), block((96, width), F32)]
    else:
        outs += [block((width, width), BF16), block(w1.shape, BF16), block(w2.shape, BF16)]
    scratch = [
        pltpu.VMEM((chunks, width, width), BF16),
        pltpu.VMEM((chunks, width, width), BF16),
        pltpu.VMEM((rows, width), F32),
        pltpu.VMEM((rows, width), BF16),
        pltpu.VMEM((width, rows), BF16),
        pltpu.VMEM((rows, width), BF16),
        pltpu.VMEM((rows, width), BF16),
        pltpu.VMEM((rows, width), BF16),
        pltpu.VMEM((rows, width), F32),
        pltpu.VMEM((rows, width), F32),
        pltpu.SemaphoreType.DMA((chunks,)),
        pltpu.SemaphoreType.DMA((chunks,)),
    ]
    params = dict(vmem_limit_bytes=60 * 2**20)
    if reduce:
        for _ in range(chunks):
            scratch += [pltpu.VMEM((2, 2, 2, 4, 48, width // 2), BF16)] + flow_scratch(48, width // 2)
            scratch += [pltpu.VMEM((2, 2, 2, 96, width), BF16)] + chunk_scratch(96, width)
        params.update(collective_id=1, has_side_effects=True)
    anywhere = pl.BlockSpec(memory_space=pl.ANY)
    return pl.pallas_call(
        functools.partial(mlp_kernel, reduce, chunks),
        out_shape=outs,
        in_specs=[VM] * 8 + [anywhere, VM, anywhere, VM],
        out_specs=[VM] * 6 + ([VM] * 2 if reduce else [VM] * 2),
        scratch_shapes=scratch,
        compiler_params=pltpu.CompilerParams(**params),
        name="mlp_step",
    )(o, x, keep, cot, w_out, b_out, gain, bias, w1, b1, w2, b2)


class SumFlow:
    def __init__(self, place, parts, arrived, sems, recvs):
        self.place, self.parts, self.arrived = place, parts, arrived
        self.sems, self.recvs = sems, recvs
        self.copies = []

    def start(self, step):
        others = "cxy"
        if step > 0:
            self.copies[step - 1].wait_recv()
            self.parts[step] = self.parts[step - 1] + self.arrived[step - 1]
        if step < 3:
            self.copies.append(
                send(self.parts.at[step], self.arrived.at[step], self.sems.at[step], self.recvs.at[step],
                     self.place.partner(others[step]))
            )
        else:
            for d in (1, 2, 3):
                self.copies.append(
                    send(self.parts.at[3], self.arrived.at[2 + d], self.sems.at[2 + d], self.recvs.at[2 + d],
                         self.place.level(d))
                )

    def last(self):
        total = self.parts[3]
        for d in (1, 2, 3):
            self.copies[2 + d].wait_recv()
            total = total + self.arrived[2 + d]
        return total

    def finish(self):
        for copy in self.copies:
            copy.wait_send()


def tail_kernel(reduce, *refs):
    dqkv, x, dx1, gain, bias, w, g_out, small_in = refs[:8]
    grad_x, grad_w, grad_o, small = refs[8:12]
    n1s, n1t = refs[12:14]
    rest = refs[14:]
    rows, width = x.shape
    tiles = rows // R
    if reduce:
        place = Place()
        greet(place)
        out_flow = Flow(place, "xy", g_out, *rest[:6])
        flows = [Flow(place, ("yx", "xy", "yx")[i], *rest[6 + 7 * i : 13 + 7 * i]) for i in range(3)]
        sums = SumFlow(place, *rest[27:31])
        sum_parts = rest[27]
        out_flow.start()

    @pl.loop(0, tiles)
    def _(t):
        r = pl.ds(pl.multiple_of(t * R, R), R)
        hat, _ = row_norm(x[r, :].astype(F32))
        n1s[r, :] = (hat * gain[...] + bias[...]).astype(BF16)

    n1t[...] = n1s[...].T
    if reduce:
        for i in range(3):

            @pl.loop(0, 4)
            def _(z):
                product = mm(n1t[pl.ds(pl.multiple_of(z * 192, 64), 192), :], dqkv[:, i * width : (i + 1) * width])
                put_blocks(product, z, flows[i].axes, flows[i].g)

            flows[i].start()
            if i == 0:
                out_flow.first()
            else:
                flows[i - 1].first()
    else:

        @pl.loop(0, 3)
        def _(t):
            r = pl.ds(pl.multiple_of(t * 256, 256), 256)
            for i in range(3):
                grad_w[r, i * width : (i + 1) * width] = mm(n1t[r, :], dqkv[:, i * width : (i + 1) * width]).astype(BF16)

    small_ref = sum_parts.at[0] if reduce else small
    small_ref[...] = small_in[...]

    def rows_back(t):
        r = pl.ds(pl.multiple_of(t * R, R), R)
        hat, rstd = row_norm(x[r, :].astype(F32))
        dn1 = mm_nt(dqkv[r, :], w[...])
        grad_x[r, :] = dx1[r, :] + norm_back(hat, rstd, gain[...], dn1)
        small_ref[8:9, :] += col_sum(dn1 * hat)
        small_ref[9:10, :] += col_sum(dn1)
        small_ref[10:11, :] += col_sum(dqkv[r, :width].astype(F32))
        small_ref[11:12, :] += col_sum(dqkv[r, 2 * width :].astype(F32))

    pl.loop(0, tiles)(rows_back)
    if reduce:
        half = width // 2
        flows[2].first()
        sums.start(0)
        out_flow.second()
        sums.start(1)
        flows[0].second()
        sums.start(2)
        flows[1].second()
        out_flow.third()
        sums.start(3)
        flows[2].second()
        flows[0].third()
        flows[1].third()
        flows[2].third()
        total = out_flow.last()
        grad_o[:, :half] = total[:24]
        grad_o[:, half:] = total[24:]
        small[...] = sums.last()
        for i in range(3):
            total = flows[i].last()
            grad_w[:, i * width : i * width + half] = total[:24]
            grad_w[:, i * width + half : (i + 1) * width] = total[24:]
        for flow in (out_flow, *flows, sums):
            flow.finish()


def tail_step(reduce, dqkv, x, dx1, gain, bias, w, g_out, small):
    rows, width = x.shape
    block = lambda dims, kind: jax.ShapeDtypeStruct(dims, kind)
    outs = [block((rows, width), F32)]
    scratch = [pltpu.VMEM((rows, width), BF16), pltpu.VMEM((width, rows), BF16)]
    params = dict(vmem_limit_bytes=60 * 2**20)
    args = [dqkv, x, dx1, gain, bias, w, g_out, small]
    if reduce:
        outs += [block((24, 3 * width), F32), block((24, width), F32), block((16, width), F32)]
        scratch += flow_scratch(48, width // 2)
        for _ in range(3):
            scratch += [pltpu.VMEM((2, 2, 2, 4, 48, width // 2), BF16)] + flow_scratch(48, width // 2)
        scratch += [
            pltpu.VMEM((4, 16, width), F32),
            pltpu.VMEM((6, 16, width), F32),
            pltpu.SemaphoreType.DMA((6,)),
            pltpu.SemaphoreType.DMA((6,)),
        ]
        params.update(collective_id=2, has_side_effects=True)
    else:
        outs += [block(w.shape, BF16), block((8, 128), F32), block((16, width), F32)]
    return pl.pallas_call(
        functools.partial(tail_kernel, reduce),
        out_shape=outs,
        in_specs=[VM] * 8,
        out_specs=[VM] * 4,
        scratch_shapes=scratch,
        compiler_params=pltpu.CompilerParams(**params),
        name="tail_step",
    )(*args)


def layer_norm(values, gain_row, bias_row):
    center = values - jnp.mean(values, -1, keepdims=True)
    variance = jnp.mean(center * center, -1, keepdims=True)
    return center * lax.rsqrt(variance + ln_epsilon) * gain_row + bias_row


def halo_of(rows, halo, side):
    mine = jnp.where(side == 0, rows[rows.shape[0] - halo :], rows[:halo])
    return lax.ppermute(mine, "hd", [(0, 1), (1, 0)])


def in_pack_order(own, halo, side):
    return jnp.where(side == 0, jnp.concatenate([own, halo], 0), jnp.concatenate([halo, own], 0))


def per_device(tokens, image_ids, keep_masks, ln1_gain, ln1_bias, w_qkv, qv_bias, w_out, b_out,
               ln2_gain, ln2_bias, w_fc1, b_fc1, w_fc2, b_fc2, cotangent):
    rows, width = tokens.shape
    halo = 640
    both = ("seq", "hd")
    side = lax.axis_index("hd")
    reduce = lax.axis_size("seq") == 16 and lax.axis_size("hd") == 2
    halo_tiles = halo // T
    tok_halo = halo_of(tokens, halo, side)
    id_halo = halo_of(image_ids, halo, side)
    id_all = in_pack_order(image_ids, id_halo, side)
    id_tiles = id_all.reshape(-1, T)
    low = jnp.sum((id_all[None, :] < id_tiles[:, :1]).astype(jnp.int32), 1) // T
    high = (jnp.sum((id_all[None, :] <= id_tiles[:, -1:]).astype(jnp.int32), 1) + T - 1) // T
    off = jnp.where(side == 0, 0, halo_tiles).astype(jnp.int32).reshape(1)
    one_hot = (image_ids[:, None] == jnp.arange(keep_masks.shape[1], dtype=jnp.int32)[None, :]).astype(F32)
    keep_rows = jnp.dot(one_hot, keep_masks[0].astype(F32)) * drop_scale
    bias_all = jnp.concatenate([qv_bias[:width], jnp.zeros((width,), F32), qv_bias[width:]])

    def project(x):
        n = layer_norm(x.astype(F32), ln1_gain, ln1_bias).astype(BF16)
        return (mm(n, w_qkv) + bias_all).astype(BF16)

    qkv_all = in_pack_order(project(tokens), project(tok_halo), side)
    id_col, id_row = id_all[:, None], id_tiles[:, None, :]
    heads_out, lse = attn_forward(low, high, off, qkv_all, id_col, id_row, rows)
    row = lambda v: v.reshape(1, -1)
    mixed, dx1, do, delta, small, g_out, grad_fc1, grad_fc2 = mlp_step(
        reduce, heads_out, tokens, keep_rows, cotangent, w_out, row(b_out), row(ln2_gain), row(ln2_bias),
        w_fc1, row(b_fc1), w_fc2, row(b_fc2))
    stats = jnp.concatenate([lse, delta], 1)
    do_all = in_pack_order(do, halo_of(do, halo, side), side)
    stats_all = in_pack_order(stats, halo_of(stats, halo_tiles, side), side)
    dqkv = attn_backward(low, high, off, qkv_all, do_all, id_col, id_row, stats_all[:, :16], stats_all[:, 16:], rows)
    grad_x, grad_qkv, grad_out, small = tail_step(
        reduce, dqkv, tokens, dx1, row(ln1_gain), row(ln1_bias), w_qkv, g_out, small)
    if not reduce:
        grad_out = g_out

        def scatter(v):
            return lax.psum_scatter(v, both, scatter_dimension=0, tiled=True).astype(F32)

        grad_fc1, grad_fc2, grad_qkv, grad_out = map(scatter, (grad_fc1, grad_fc2, grad_qkv, grad_out))
        small = lax.psum(small, both)
    small = small.reshape(-1)
    shards = lax.axis_size("seq") * lax.axis_size("hd")
    place = lax.axis_index("seq") * lax.axis_size("hd") + side

    def share(first, count):
        part = small[first * width : (first + count) * width]
        size = count * width // shards
        return lax.dynamic_slice(part, (place * size,), (size,))

    return (mixed, grad_x, share(8, 1), share(9, 1), grad_qkv, share(10, 2), grad_out, share(0, 1),
            share(1, 1), share(2, 1), grad_fc1, share(3, 4), grad_fc2, share(7, 1))


def solution(mesh):
    both = P(("seq", "hd"))
    split = P(("seq", "hd"), None)
    return jax.shard_map(
        per_device,
        mesh=mesh,
        in_specs=(split, both, P("seq", None, None)) + (P(),) * 12 + (split,),
        out_specs=(split, split, both, both, split, both, split, both, both, both, split, both, split, both),
        check_vma=False,
    )
```

```python
import functools
import jax, jax.numpy as jnp
from jax import lax
from jax.experimental import pallas as pl
from jax.experimental.pallas import tpu as pltpu
from jax.sharding import PartitionSpec as P

HEADS, HEAD = 12, 64
T = 128
W2 = 256
VM = pl.BlockSpec(memory_space=pltpu.VMEM)
SM = pl.BlockSpec(memory_space=pltpu.SMEM)
F32, BF16 = jnp.float32, jnp.bfloat16
NT = (((1,), (1,)), ((), ()))
TN = (((0,), (0,)), ((), ()))


def mm(a, b):
    return jnp.dot(a, b, preferred_element_type=F32)


def mm_nt(a, b):
    return lax.dot_general(a, b, NT, preferred_element_type=F32)


def mm_tn(a, b):
    return lax.dot_general(a, b, TN, preferred_element_type=F32)


def by_head(pair):
    lane = lax.broadcasted_iota(jnp.int32, pair.shape, 1)
    zero = jnp.zeros_like(pair)
    return jnp.concatenate(
        [jnp.where(lane < HEAD, pair, zero), jnp.where(lane < HEAD, zero, pair)], 0
    )


def by_head_rows(pair):
    row = lax.broadcasted_iota(jnp.int32, pair.shape, 0)
    zero = jnp.zeros_like(pair)
    return jnp.concatenate([jnp.where(row < HEAD, pair, zero), jnp.where(row < HEAD, zero, pair)], 1)


def tile_span(ids, first_tile, last_tile):
    low, high = 0, 0
    for u in range(ids.shape[0]):
        low += (ids[u, T - 1] < ids[first_tile, 0]).astype(jnp.int32)
        high += (ids[u, 0] <= ids[last_tile, T - 1]).astype(jnp.int32)
    return low, high


def id_columns(id_row, id_col):
    @pl.loop(0, id_row.shape[0])
    def _(j):
        line = jnp.broadcast_to(id_row[pl.ds(j, 1), :].astype(F32), (T, T))
        id_col[pl.ds(pl.multiple_of(j * T, T), T), :] = line.T


def same_image(id_col, rows, id_row, tile):
    left = id_col[rows, :]
    right = id_row[pl.ds(tile, 1), :].astype(F32)
    return jnp.concatenate([left, left], 1) == jnp.concatenate([right, right], 1)


HALO_ROWS = 320


def attn_forward_kernel(width, ids, id_row, own_qkv, halo, gain, bias, w, b, out, lse, all_qkv, qkv, sc, vt, acc, id_col, sems):
    pairs = width // 128
    rows, tiles = out.shape[0], id_row.shape[0]
    own = rows // T
    side = lax.axis_index("hd")
    off = side * own
    apart = rows - halo.shape[0]
    fetch = pltpu.make_async_copy(own_qkv, qkv.at[pl.ds(pl.multiple_of(side * rows, rows), rows), :], sems.at[0])
    fetch.start()
    id_columns(id_row, id_col)
    qkv[pl.ds(pl.multiple_of((1 - side) * (2 * rows - apart), apart), apart), :] = jnp.zeros((apart, 3 * width), BF16)

    @pl.loop(0, halo.shape[0] // HALO_ROWS)
    def _(t):
        r = pl.ds(pl.multiple_of(t * HALO_ROWS, 64), HALO_ROWS)
        hat, _ = row_norm(halo[r, :].astype(F32))
        n1 = (hat * gain[...] + bias[...]).astype(BF16)
        first = pl.multiple_of((1 - side) * rows + side * apart + t * HALO_ROWS, 64)
        qkv[pl.ds(first, HALO_ROWS), :] = (mm(n1, w[...]) + b[...]).astype(BF16)

    fetch.wait()
    store = pltpu.make_async_copy(qkv, all_qkv, sems.at[1])
    store.start()

    @pl.loop(0, tiles)
    def _(j):
        k0 = pl.multiple_of(j * T, T)
        vt[:, pl.ds(k0, T)] = qkv[pl.ds(k0, T), 2 * width :].T

    @pl.loop(0, own)
    def _(i):
        tile = off + i
        q0 = pl.multiple_of(tile * T, T)
        low, high = tile_span(ids, tile, tile)
        low = jnp.where(jnp.logical_and(lax.rem(high - low, 2) == 1, low > 0), low - 1, low)
        count = (high - low + 1) // 2
        turned = (qkv[pl.ds(q0, T), :width] * BF16(HEAD**-0.5)).T
        stacks = [by_head_rows(turned[p * 128 : p * 128 + 128]) for p in range(pairs)]

        def scores(j, peaks):
            k0 = pl.multiple_of((low + 2 * j) * T, T)
            same = same_image(id_col, pl.ds(k0, W2), id_row, tile)
            held = [mm(qkv[pl.ds(k0, W2), width + p * 128 : width + p * 128 + 128], stacks[p]) for p in range(pairs)]
            news = []
            for p, s in enumerate(held):
                s = jnp.where(same, s, -1e30)
                sc[p, j] = s
                news.append(jnp.maximum(peaks[p], jnp.max(s.reshape(W2 // 8, 8, 2 * T), 0)))
            return tuple(news)

        start = tuple(jnp.full((8, 2 * T), -jnp.inf, F32) for _ in range(pairs))
        peaks = lax.fori_loop(0, count, scores, start)
        peaks = [jnp.max(m, 0, keepdims=True) for m in peaks]
        for p in range(pairs):
            acc[p] = jnp.zeros((128, 2 * T), F32)

        def outputs(j, totals):
            k0 = pl.multiple_of((low + 2 * j) * T, T)
            es, news = [], []
            for p in range(pairs):
                e = jnp.exp(sc[p, j] - peaks[p])
                news.append(totals[p] + jnp.sum(e.reshape(W2 // 8, 8, 2 * T), 0))
                es.append(e.astype(BF16))
            held = [mm(vt[p * 128 : p * 128 + 128, pl.ds(k0, W2)], es[p]) for p in range(pairs)]
            for p in range(pairs):
                acc[p] += held[p]
            return tuple(news)

        totals = lax.fori_loop(0, count, outputs, tuple(jnp.zeros((8, 2 * T), F32) for _ in range(pairs)))
        stats = []
        for p in range(pairs):
            total = jnp.sum(totals[p], 0, keepdims=True)
            scaled = acc[p] * (1.0 / total)
            o = jnp.concatenate([scaled[:HEAD, :T], scaled[HEAD:, T:]], 0)
            out[pl.ds(pl.multiple_of(i * T, T), T), p * 128 : p * 128 + 128] = o.T.astype(BF16)
            stat = peaks[p] + jnp.log(total)
            stats += [stat[:, :T], stat[:, T:]]
        lse[i] = jnp.concatenate(stats + [jnp.zeros((4, T), F32)], 0)

    store.wait()


def attn_forward(ids, own_qkv, halo, gain, bias, w, b):
    rows, width = own_qkv.shape[0], own_qkv.shape[1] // 3
    tiles = ids.shape[0]
    pairs = width // 128
    anywhere = pl.BlockSpec(memory_space=pl.ANY)
    return pl.pallas_call(
        functools.partial(attn_forward_kernel, width),
        out_shape=(
            jax.ShapeDtypeStruct((rows, width), BF16),
            jax.ShapeDtypeStruct((rows // T, 16, T), F32),
            jax.ShapeDtypeStruct((2 * rows, 3 * width), BF16),
        ),
        in_specs=[SM, VM, anywhere] + [VM] * 5,
        out_specs=(VM, VM, anywhere),
        scratch_shapes=[
            pltpu.VMEM((2 * rows, 3 * width), BF16),
            pltpu.VMEM((pairs, tiles // 2, W2, 2 * T), F32),
            pltpu.VMEM((width, 2 * rows), BF16),
            pltpu.VMEM((pairs, 128, 2 * T), F32),
            pltpu.VMEM((2 * rows, T), F32),
            pltpu.SemaphoreType.DMA((2,)),
        ],
        compiler_params=pltpu.CompilerParams(vmem_limit_bytes=56 * 2**20),
        name="attention_forward",
    )(ids, ids, own_qkv, halo, gain, bias, w, b)


def attn_backward_kernel(width, ids, id_row, qkv, do, stats, out, dq, dk, dv, qt, kt, gt, id_col):
    pairs = width // 128
    own = out.shape[0] // T
    off = lax.axis_index("hd") * own
    id_columns(id_row, id_col)
    tiles = id_row.shape[0]
    dq[...] = jnp.zeros_like(dq)

    @pl.loop(0, tiles)
    def _(j):
        k0 = pl.multiple_of(j * T, T)
        rows = pl.ds(k0, T)
        qt[:, rows] = (qkv[rows, :width] * BF16(HEAD**-0.5)).T
        kt[:, rows] = qkv[rows, width : 2 * width].T
        gt[:, rows] = do[rows, :].T

    @pl.loop(0, tiles // 2)
    def _(j):
        k0 = pl.multiple_of(j * W2, W2)
        mine = jnp.logical_and(2 * j >= off, 2 * j < off + own)
        low, high = tile_span(ids, 2 * j, 2 * j + 1)
        low = jnp.where(mine, low, jnp.maximum(low, off))
        high = jnp.where(mine, high, jnp.minimum(high, off + own))
        for p in range(pairs):
            dk[p] = jnp.zeros((W2, 128), F32)
            dv[p] = jnp.zeros((W2, 128), F32)

        @pl.loop(low, high)
        def _(i):
            q0 = pl.multiple_of(i * T, T)
            same = same_image(id_col, pl.ds(k0, W2), id_row, i)
            qs, gs, ss, ps, es, ds = [], [], [], [], [], []
            for p in range(pairs):
                cols = p * 128
                k = qkv[pl.ds(k0, W2), width + cols : width + cols + 128]
                v = qkv[pl.ds(k0, W2), 2 * width + cols : 2 * width + cols + 128]
                ss.append(mm(k, by_head_rows(qt[cols : cols + 128, pl.ds(q0, T)])))
                ps.append(mm(v, by_head_rows(gt[cols : cols + 128, pl.ds(q0, T)])))
            for p in range(pairs):
                one = jnp.concatenate([stats[i, 2 * p : 2 * p + 1, :], stats[i, 2 * p + 1 : 2 * p + 2, :]], 1)
                two = jnp.concatenate([stats[i, 2 * p + 16 : 2 * p + 17, :], stats[i, 2 * p + 17 : 2 * p + 18, :]], 1)
                e = jnp.exp(jnp.where(same, ss[p], -1e30) - one)
                es.append(e.astype(BF16))
                ds.append((e * (ps[p] - two)).astype(BF16))
            a, b, c = [], [], []
            for p in range(pairs):
                cols = p * 128
                a.append(mm(es[p], by_head(do[pl.ds(q0, T), cols : cols + 128])))
                b.append(mm(ds[p], by_head(qkv[pl.ds(q0, T), cols : cols + 128] * BF16(HEAD**-0.5))))
                c.append(mm(kt[cols : cols + 128, pl.ds(k0, W2)], ds[p]))
            for p in range(pairs):
                dv[p] += a[p]
                dk[p] += b[p]
                dq[p, i] += jnp.concatenate([c[p][:HEAD, :T], c[p][HEAD:, T:]], 0)

        @pl.when(mine)
        def _():
            r0 = pl.multiple_of(j * W2 - off * T, W2)
            for p in range(pairs):
                cols = p * 128
                out[pl.ds(r0, W2), width + cols : width + cols + 128] = dk[p].astype(BF16)
                out[pl.ds(r0, W2), 2 * width + cols : 2 * width + cols + 128] = dv[p].astype(BF16)

    @pl.loop(0, own)
    def _(i):
        for p in range(pairs):
            cols = p * 128
            out[pl.ds(pl.multiple_of(i * T, T), T), cols : cols + 128] = (dq[p, off + i] * HEAD**-0.5).T.astype(BF16)


def attn_backward(ids, qkv, do, stats):
    all_rows, columns = qkv.shape
    own_rows = all_rows // 2
    width = columns // 3
    tiles = all_rows // T
    pairs = width // 128
    return pl.pallas_call(
        functools.partial(attn_backward_kernel, width),
        out_shape=jax.ShapeDtypeStruct((own_rows, columns), BF16),
        in_specs=[SM] + [VM] * 4,
        out_specs=VM,
        scratch_shapes=[
            pltpu.VMEM((pairs, tiles, 128, T), F32),
            pltpu.VMEM((pairs, W2, 128), F32),
            pltpu.VMEM((pairs, W2, 128), F32),
            pltpu.VMEM((width, all_rows), BF16),
            pltpu.VMEM((width, all_rows), BF16),
            pltpu.VMEM((width, all_rows), BF16),
            pltpu.VMEM((all_rows, T), F32),
        ],
        compiler_params=pltpu.CompilerParams(vmem_limit_bytes=56 * 2**20),
        name="attention_backward",
    )(ids, ids, qkv, do, stats)


ln_epsilon = 1e-06
drop_scale = 1.0 / 0.9


MESH = pl.DeviceIdType.MESH


class Place:
    def __init__(self):
        self.seq = lax.axis_index("seq")
        self.x = lax.axis_index("hd")
        self.c = lax.rem(self.seq, 2)
        self.y = lax.rem(self.seq // 2, 2)
        self.z = self.seq // 4

    def partner(self, axis):
        if axis == "c":
            return (self.seq + 1 - 2 * self.c, self.x)
        if axis == "y":
            return (self.seq + 2 - 4 * self.y, self.x)
        return (self.seq, 1 - self.x)

    def level(self, step):
        return (lax.rem(self.z + step, 4) * 4 + lax.rem(self.seq, 4), self.x)

    def index(self, axis):
        return {"x": self.x, "y": self.y, "c": self.c}[axis]


def greet(place):
    barrier = pltpu.get_barrier_semaphore()
    for other in [place.partner(a) for a in "cxy"] + [place.level(d) for d in (1, 2, 3)]:
        pl.semaphore_signal(barrier, inc=1, device_id=other, device_id_type=MESH)


def meet():
    pl.semaphore_wait(pltpu.get_barrier_semaphore(), 6)


def send(source, target, send_sem, recv_sem, other):
    copy = pltpu.make_async_remote_copy(
        src_ref=source, dst_ref=target, send_sem=send_sem, recv_sem=recv_sem, device_id=other, device_id_type=MESH
    )
    copy.start()
    return copy


class Flow:
    def __init__(self, place, axes, g, r0, r1, r2, r3, sems, recvs):
        self.place, self.axes, self.g = place, axes, g
        self.r0, self.r1, self.r2, self.r3 = r0, r1, r2, r3
        self.sems, self.recvs = sems, recvs
        self.copies = []

    def start(self):
        p = self.place
        self.copies.append(send(self.g.at[1 - p.c], self.r0, self.sems.at[0], self.recvs.at[0], p.partner("c")))

    def first(self):
        p = self.place
        self.copies[0].wait_recv()
        me = p.index(self.axes[0])

        def add(half):
            @pl.loop(0, 8)
            def _(i):
                b, z = i // 4, lax.rem(i, 4)
                self.r0[half, b, z] = self.r0[half, b, z] + self.g[p.c, half, b, z]

        add(1 - me)
        self.copies.append(
            send(self.r0.at[1 - me], self.r1, self.sems.at[1], self.recvs.at[1], p.partner(self.axes[0]))
        )
        add(me)

    def second(self):
        p = self.place
        self.copies[1].wait_recv()
        me, before = p.index(self.axes[1]), p.index(self.axes[0])

        def add(half):
            @pl.loop(0, 4)
            def _(z):
                self.r1[half, z] = self.r1[half, z] + self.r0[before, half, z]

        add(1 - me)
        self.copies.append(
            send(self.r1.at[1 - me], self.r2, self.sems.at[2], self.recvs.at[2], p.partner(self.axes[1]))
        )
        add(me)

    def third(self):
        p = self.place
        self.copies[2].wait_recv()
        before = p.index(self.axes[1])

        @pl.loop(0, 4)
        def _(z):
            self.r2[z] = self.r2[z] + self.r1[before, z]

        for d in (1, 2, 3):
            target = lax.rem(p.z + d, 4)
            self.copies.append(
                send(self.r2.at[target], self.r3.at[d - 1], self.sems.at[2 + d], self.recvs.at[2 + d], p.level(d))
            )

    def last(self):
        p = self.place
        total = self.r2[p.z].astype(F32)
        for d in (1, 2, 3):
            self.copies[2 + d].wait_recv()
            total = total + self.r3[d - 1].astype(F32)
        return total

    def finish(self):
        for copy in self.copies:
            copy.wait_send()


def flow_scratch(rows, cols, kind=BF16):
    return [
        pltpu.VMEM((2, 2, 4, rows, cols), kind),
        pltpu.VMEM((2, 4, rows, cols), kind),
        pltpu.VMEM((4, rows, cols), kind),
        pltpu.VMEM((3, rows, cols), kind),
        pltpu.SemaphoreType.DMA((6,)),
        pltpu.SemaphoreType.DMA((6,)),
    ]


class ChunkFlow(Flow):
    def __init__(self, place, axes, home, *refs):
        super().__init__(place, axes, *refs)
        self.home = home

    def third(self):
        p = self.place
        self.copies[2].wait_recv()
        self.r2[...] = self.r2[...] + self.r1[p.index(self.axes[1])]
        slot = lax.rem(p.z - self.home + 3, 4)
        self.hop = pltpu.make_async_remote_copy(
            src_ref=self.r2,
            dst_ref=self.r3.at[slot],
            send_sem=self.sems.at[3],
            recv_sem=self.recvs.at[3 + slot],
            device_id=(self.home * 4 + lax.rem(p.seq, 4), p.x),
            device_id_type=MESH,
        )

        @pl.when(p.z != self.home)
        def _():
            self.hop.start()

    def first(self):
        p = self.place
        self.copies[0].wait_recv()
        me = p.index(self.axes[0])

        def add(half):
            for b in range(2):
                self.r0[half, b] = self.r0[half, b] + self.g[p.c, half, b]

        add(1 - me)
        self.copies.append(
            send(self.r0.at[1 - me], self.r1, self.sems.at[1], self.recvs.at[1], p.partner(self.axes[0]))
        )
        add(me)

    def second(self):
        p = self.place
        self.copies[1].wait_recv()
        me, before = p.index(self.axes[1]), p.index(self.axes[0])
        self.r1[1 - me] = self.r1[1 - me] + self.r0[before, 1 - me]
        self.copies.append(
            send(self.r1.at[1 - me], self.r2, self.sems.at[2], self.recvs.at[2], p.partner(self.axes[1]))
        )
        self.r1[me] = self.r1[me] + self.r0[before, me]

    def last_into(self, out):
        p = self.place

        @pl.when(p.z == self.home)
        def _():
            total = self.r2[...].astype(F32)
            for slot in range(3):
                pltpu.make_async_remote_copy(
                    src_ref=self.r2,
                    dst_ref=self.r3.at[slot],
                    send_sem=self.sems.at[3],
                    recv_sem=self.recvs.at[3 + slot],
                    device_id=p.level(1),
                    device_id_type=MESH,
                ).wait_recv()
                total = total + self.r3[slot].astype(F32)
            out[...] = total

    def finish(self):
        super().finish()

        @pl.when(self.place.z != self.home)
        def _():
            self.hop.wait_send()


def chunk_scratch(rows, cols):
    return [
        pltpu.VMEM((2, 2, rows, cols), BF16),
        pltpu.VMEM((2, rows, cols), BF16),
        pltpu.VMEM((rows, cols), BF16),
        pltpu.VMEM((3, rows, cols), BF16),
        pltpu.SemaphoreType.DMA((6,)),
        pltpu.SemaphoreType.DMA((6,)),
    ]


def row_norm(x):
    mean = jnp.mean(x, -1, keepdims=True)
    center = x - mean
    rstd = lax.rsqrt(jnp.mean(center * center, -1, keepdims=True) + ln_epsilon)
    return center * rstd, rstd


def norm_back(hat, rstd, gain, grad):
    scaled = grad * gain
    return rstd * (scaled - jnp.mean(scaled, -1, keepdims=True) - hat * jnp.mean(scaled * hat, -1, keepdims=True))


def col_sum(x):
    return jnp.sum(x, 0, keepdims=True)


def put_blocks(product, z, axes, g):
    half = product.shape[1] // 2
    for y in range(2):
        for c in range(2):
            for x in range(2):
                r = ((y * 2 + c) * 2 + x) * 24
                block = jnp.concatenate([product[r : r + 24, :half], product[r : r + 24, half:]], 0)
                at = {"x": x, "y": y}
                g[c, at[axes[0]], at[axes[1]], z] = block.astype(BF16)


def put_chunk(product, y, axes, g):
    for c in range(2):
        for x in range(2):
            r = (c * 2 + x) * 96
            at = {"x": x, "y": y}
            g[c, at[axes[0]], at[axes[1]]] = product[r : r + 96].astype(BF16)


R = 256
HALO = 640
FLOW_REFS = 6
ORDER = (0, 3, 1, 2)
PATHS1 = ("xy", "xy", "xy", "xy")
PATHS2 = ("yx", "yx", "yx", "yx")


def mlp_kernel(reduce, chunks, *refs):
    o, lse, x, keep, cot, w_out, b_out, gain, bias, w1, b1, w2, b2 = refs[:13]
    mixed, dx1, do, stats, small, g_out, out1, out2 = refs[13:21]
    v1, v2, x1s, n2s, n2t, dms, gs, dus, macc, nacc, load1, load2, halo_sems = refs[21:34]
    flow_refs = refs[34:]
    side = lax.axis_index("hd")
    base = pl.multiple_of(side * o.shape[0], o.shape[0])
    das = gs
    owner = lax.broadcasted_iota(jnp.int32, (16, o.shape[1]), 1) // HEAD
    heads = (owner == lax.broadcasted_iota(jnp.int32, (16, o.shape[1]), 0)).astype(BF16)
    rows, width = o.shape
    tiles = rows // R
    loads = []
    for k in range(chunks):
        cols = pl.ds(k * width, width)
        loads.append(
            (
                pltpu.make_async_copy(w1.at[:, cols], v1.at[k], load1.at[k]),
                pltpu.make_async_copy(w2.at[cols, :], v2.at[k], load2.at[k]),
            )
        )
        loads[k][0].start()
        loads[k][1].start()
    if reduce:
        place = Place()
        greet(place)
        per = 1 + FLOW_REFS
        flows1 = [Flow(place, PATHS1[k], *flow_refs[2 * per * k : 2 * per * k + per]) for k in range(chunks)]
        flows2 = [ChunkFlow(place, PATHS2[k], k, *flow_refs[2 * per * k + per : 2 * per * (k + 1)]) for k in range(chunks)]

    small[...] = jnp.zeros_like(small)

    @pl.loop(0, tiles)
    def _(t):
        r = pl.ds(pl.multiple_of(t * R, R), R)
        x1 = x[r, :].astype(F32) + keep[r, 0:1] * (mm(o[r, :], w_out[...]) + b_out[...])
        x1s[r, :] = x1
        hat, _ = row_norm(x1)
        n2 = (hat * gain[...] + bias[...]).astype(BF16)
        n2s[r, :] = n2
        dm = (cot[r, :].astype(F32) * keep[r, 1:2]).astype(BF16)
        dms[r, :] = dm
        small[7:8, :] += col_sum(dm.astype(F32))

    n2t[...] = n2s[...].T

    def row_tile(k, t, first):
        r = slice(t * R, t * R + R)
        u = mm(n2s[r, :], v1[k]) + b1[k * width : k * width + width]
        dg = mm_nt(dms[r, :], v2[k])
        cdf = 0.5 + 0.5 * lax.erf(u * 0.7071067811865476)
        pdf = jnp.exp(u * u * -0.5) * 0.3989422804014327
        g = (u * cdf).astype(BF16)
        du = (dg * (cdf + u * pdf)).astype(BF16)
        gs[r, :] = g
        dus[r, :] = du
        small[3 + k : 4 + k, :] += col_sum(du.astype(F32))
        if first:
            macc[r, :] = mm(g, v2[k])
            nacc[r, :] = mm_nt(du, v1[k])
        else:
            macc[r, :] += mm(g, v2[k])
            nacc[r, :] += mm_nt(du, v1[k])

    steps = {}
    last = chunks - 1
    if reduce:
        for at, k in enumerate(ORDER):
            for flow, late in ((flows2[k], 0), (flows1[k], 1)):
                steps.setdefault((at + 1, 1 + late if at < last else 1), []).append(flow.first)
                steps.setdefault((at + 1, 5) if at < last else (at + 2, late), []).append(flow.second)
                steps.setdefault((at + 2, 2 + late), []).append(flow.third)

    def point(*at):
        for step in steps.pop(at, []):
            step()

    for at, k in enumerate(ORDER if reduce else range(chunks)):
        loads[k][0].wait()
        loads[k][1].wait()
        for t in range(tiles):
            row_tile(k, t, at == 0)
            point(at, t + 1)
        if reduce and at == 0:
            meet()
        if reduce:

            @pl.loop(0, 2)
            def _(y):
                product = mm_tn(gs[:, pl.ds(pl.multiple_of(y * 384, 384), 384)], dms[...])
                put_chunk(product, y, flows2[k].axes, flows2[k].g)

            flows2[k].start()
            point(at, 4)

            @pl.loop(0, 2)
            def _(h):
                product = mm(n2t[pl.ds(pl.multiple_of(h * 384, 128), 384), :], dus[...])
                for z in range(2):
                    put_blocks(product[z * 192 : z * 192 + 192], 2 * h + z, flows1[k].axes, flows1[k].g)

            flows1[k].start()
            point(at, 5)
        else:

            @pl.loop(0, 3)
            def _(t):
                r = pl.ds(pl.multiple_of(t * 256, 256), 256)
                out2[pl.ds(pl.multiple_of(k * width + t * 256, 256), 256), :] = mm_tn(gs[:, r], dms[...]).astype(BF16)
                out1[r, k * width : k * width + width] = mm(n2t[r, :], dus[...]).astype(BF16)

    apart = rows - HALO
    pad = pl.multiple_of((1 - side) * (2 * rows - apart), apart)
    do[pl.ds(pad, apart), :] = jnp.zeros((apart, width), BF16)
    for s in range(apart // T):
        stats[(1 - side) * (2 * rows - apart) // T + s] = jnp.zeros((32, T), F32)
    exchange = []

    def exchange_rows(ref, first, count, n):
        part = ref.at[pl.ds(first, count)]
        exchange.append(send(part, part, halo_sems.at[2 * n], halo_sems.at[2 * n + 1], place.partner("x")))

    n2t[...] = o[...].T
    for t in range(tiles):
        at = lax.rem(t + 1 - side, tiles)
        r = pl.ds(pl.multiple_of(at * R, R), R)
        hat, rstd = row_norm(x1s[r, :])
        dn2 = nacc[r, :]
        dx = cot[r, :].astype(F32) + norm_back(hat, rstd, gain[...], dn2)
        dx1[r, :] = dx
        da = (dx * keep[r, 0:1]).astype(BF16)
        das[r, :] = da
        grad_o = mm_nt(da, w_out[...]).astype(BF16)
        do[pl.ds(pl.multiple_of(base + at * R, R), R), :] = grad_o
        small[0:1, :] += col_sum(da.astype(F32))
        small[1:2, :] += col_sum(dn2 * hat)
        small[2:3, :] += col_sum(dn2)
        prod = grad_o.astype(F32) * o[r, :].astype(F32)
        high = prod.astype(BF16)
        low = (prod - high.astype(F32)).astype(BF16)
        sums = mm_nt(heads, high) + mm_nt(heads, low)
        for s in range(R // T):
            own = at * (R // T) + s
            stats[side * (rows // T) + own, :16] = lse[own]
            stats[side * (rows // T) + own, 16:] = sums[:, s * T : s * T + T]
        point(chunks, t + 1)
        if reduce and t == 0:
            exchange_rows(do, pl.multiple_of(base + at * R, R), R, 0)

    if reduce:
        first_tile = apart // T + side * (rows - apart) // T
        exchange_rows(stats, first_tile, HALO // T, 3)

        @pl.loop(0, 2)
        def _(h):
            product = mm(n2t[pl.ds(pl.multiple_of(h * 384, 128), 384), :], das[...])
            for z in range(2):
                put_blocks(product[z * 192 : z * 192 + 192], 2 * h + z, "xy", g_out)

    else:

        @pl.loop(0, 3)
        def _(t):
            r = pl.ds(pl.multiple_of(t * 256, 256), 256)
            g_out[r, :] = mm(n2t[r, :], das[...]).astype(BF16)

    @pl.loop(0, tiles)
    def _(t):
        r = pl.ds(pl.multiple_of(t * R, R), R)
        mixed[r, :] = (x1s[r, :] + keep[r, 1:2] * (macc[r, :] + b2[...])).astype(BF16)

    if reduce:
        half = width // 2

        def keep_share(k):
            total = flows1[k].last()
            out1[:, k * width : k * width + half] = total[:24]
            out1[:, k * width + half : (k + 1) * width] = total[24:]
            flows2[k].last_into(out2)

        point(chunks + 1, 0)
        second_tile = 2 - side
        exchange_rows(do, pl.multiple_of(base + second_tile * R, R), R, 1)
        exchange_rows(do, pl.multiple_of(base + (1 - side) * apart + side * 2 * R, T), HALO - 2 * R, 2)
        point(chunks + 1, 1)
        for at in sorted(steps):
            point(*at)
        for k in range(chunks):
            keep_share(k)
        for k in range(chunks):
            flows1[k].finish()
            flows2[k].finish()
        for copy in exchange:
            copy.wait()


def mlp_step(reduce, o, lse, x, keep, cot, w_out, b_out, gain, bias, w1, b1, w2, b2):
    rows, width = o.shape
    chunks = w1.shape[1] // width
    block = lambda dims, kind: jax.ShapeDtypeStruct(dims, kind)
    outs = [
        block((rows, width), BF16),
        block((rows, width), F32),
        block((2 * rows, width), BF16),
        block((2 * rows // T, 32, T), F32),
        block((16, width), F32),
    ]
    if reduce:
        outs += [block((2, 2, 2, 4, 48, width // 2), BF16), block((24, chunks * width), F32), block((96, width), F32)]
    else:
        outs += [block((width, width), BF16), block(w1.shape, BF16), block(w2.shape, BF16)]
    scratch = [
        pltpu.VMEM((chunks, width, width), BF16),
        pltpu.VMEM((chunks, width, width), BF16),
        pltpu.VMEM((rows, width), F32),
        pltpu.VMEM((rows, width), BF16),
        pltpu.VMEM((width, rows), BF16),
        pltpu.VMEM((rows, width), BF16),
        pltpu.VMEM((rows, width), BF16),
        pltpu.VMEM((rows, width), BF16),
        pltpu.VMEM((rows, width), F32),
        pltpu.VMEM((rows, width), F32),
        pltpu.SemaphoreType.DMA((chunks,)),
        pltpu.SemaphoreType.DMA((chunks,)),
        pltpu.SemaphoreType.DMA((8,)),
    ]
    params = dict(vmem_limit_bytes=60 * 2**20)
    if reduce:
        for _ in range(chunks):
            scratch += [pltpu.VMEM((2, 2, 2, 4, 48, width // 2), BF16)] + flow_scratch(48, width // 2)
            scratch += [pltpu.VMEM((2, 2, 2, 96, width), BF16)] + chunk_scratch(96, width)
        params.update(collective_id=1, has_side_effects=True)
    anywhere = pl.BlockSpec(memory_space=pl.ANY)
    return pl.pallas_call(
        functools.partial(mlp_kernel, reduce, chunks),
        out_shape=outs,
        in_specs=[VM] * 9 + [anywhere, VM, anywhere, VM],
        out_specs=[VM] * 8,
        scratch_shapes=scratch,
        compiler_params=pltpu.CompilerParams(**params),
        name="mlp_step",
    )(o, lse, x, keep, cot, w_out, b_out, gain, bias, w1, b1, w2, b2)


SMALLS = ((8, 1), (9, 1), (10, 2), (0, 1), (1, 1), (2, 1), (3, 4), (7, 1))


def by_owner(sums):
    width = sums.shape[1]
    lane = lax.broadcasted_iota(jnp.int32, (32, width), 1)
    block = lax.broadcasted_iota(jnp.int32, (32, width), 0)
    source = lax.broadcasted_iota(jnp.int32, (width, 128), 0)
    target = lax.broadcasted_iota(jnp.int32, (width, 128), 1)
    parts = []
    for first, rows in SMALLS:
        size = rows * width // 32
        row = block // (32 // rows)
        spread = jnp.zeros((32, width), F32)
        for r in range(rows):
            spread = jnp.where(row == r, sums[first + r : first + r + 1, :], spread)
        spread = jnp.where(lane // size == lax.rem(block, 32 // rows), spread, 0.0)
        pick = (lax.rem(source, size) == target).astype(BF16)
        total = jnp.zeros((32, 128), F32)
        for _ in range(3):
            piece = spread.astype(BF16)
            total = total + mm(piece, pick)
            spread = spread - piece.astype(F32)
        parts.append(total.reshape(32, 1, 128))
    return jnp.concatenate(parts, 1)


def tail_kernel(reduce, *refs):
    dqkv, x, dx1, gain, bias, w, g_out, small_in = refs[:8]
    grad_x, grad_w, grad_o, small = refs[8:12]
    n1s, n1t = refs[12:14]
    rest = refs[14:]
    rows, width = x.shape
    tiles = rows // R
    if reduce:
        place = Place()
        greet(place)
        out_flow = Flow(place, "xy", g_out, *rest[:6])
        flows = [Flow(place, ("yx", "xy", "yx")[i], *rest[6 + 7 * i : 13 + 7 * i]) for i in range(3)]
        sums = Flow(place, "xy", *rest[27:34])

    @pl.loop(0, tiles)
    def _(t):
        r = pl.ds(pl.multiple_of(t * R, R), R)
        hat, _ = row_norm(x[r, :].astype(F32))
        n1s[r, :] = (hat * gain[...] + bias[...]).astype(BF16)

    n1t[...] = n1s[...].T
    if reduce:
        meet()
        out_flow.start()
        for i in range(3):

            @pl.loop(0, 2)
            def _(h):
                product = mm(n1t[pl.ds(pl.multiple_of(h * 384, 128), 384), :], dqkv[:, i * width : (i + 1) * width])
                for z in range(2):
                    put_blocks(product[z * 192 : z * 192 + 192], 2 * h + z, flows[i].axes, flows[i].g)

            flows[i].start()
            if i == 0:
                out_flow.first()
            else:
                flows[i - 1].first()
    else:

        @pl.loop(0, 3)
        def _(t):
            r = pl.ds(pl.multiple_of(t * 256, 256), 256)
            for i in range(3):
                grad_w[r, i * width : (i + 1) * width] = mm(n1t[r, :], dqkv[:, i * width : (i + 1) * width]).astype(BF16)

    small_ref = rest[34] if reduce else small
    small_ref[...] = small_in[...]

    def rows_back(t):
        r = pl.ds(pl.multiple_of(t * R, R), R)
        hat, rstd = row_norm(x[r, :].astype(F32))
        dn1 = mm_nt(dqkv[r, :], w[...])
        grad_x[r, :] = dx1[r, :] + norm_back(hat, rstd, gain[...], dn1)
        small_ref[8:9, :] += col_sum(dn1 * hat)
        small_ref[9:10, :] += col_sum(dn1)
        small_ref[10:11, :] += col_sum(dqkv[r, :width].astype(F32))
        small_ref[11:12, :] += col_sum(dqkv[r, 2 * width :].astype(F32))

    pl.loop(0, tiles)(rows_back)
    if reduce:
        half = width // 2
        shares = by_owner(small_ref[...])
        for b in range(32):
            sums.g[b // 2 % 2, b % 2, b // 4 % 2, b // 8] = shares[b]
        sums.start()
        flows[2].first()
        out_flow.second()
        sums.first()
        flows[0].second()
        flows[1].second()
        sums.second()
        flows[2].second()
        flows[0].third()
        out_flow.third()
        sums.third()
        flows[2].third()
        flows[1].third()
        total = out_flow.last()
        grad_o[:, :half] = total[:24]
        grad_o[:, half:] = total[24:]
        small[...] = sums.last()
        for i in range(3):
            total = flows[i].last()
            grad_w[:, i * width : i * width + half] = total[:24]
            grad_w[:, i * width + half : (i + 1) * width] = total[24:]
        for flow in (out_flow, *flows, sums):
            flow.finish()


def tail_step(reduce, dqkv, x, dx1, gain, bias, w, g_out, small):
    rows, width = x.shape
    block = lambda dims, kind: jax.ShapeDtypeStruct(dims, kind)
    outs = [block((rows, width), F32)]
    scratch = [pltpu.VMEM((rows, width), BF16), pltpu.VMEM((width, rows), BF16)]
    params = dict(vmem_limit_bytes=60 * 2**20)
    args = [dqkv, x, dx1, gain, bias, w, g_out, small]
    if reduce:
        outs += [block((24, 3 * width), F32), block((24, width), F32), block((8, 128), F32)]
        scratch += flow_scratch(48, width // 2)
        for _ in range(3):
            scratch += [pltpu.VMEM((2, 2, 2, 4, 48, width // 2), BF16)] + flow_scratch(48, width // 2)
        scratch += [pltpu.VMEM((2, 2, 2, 4, 8, 128), F32)] + flow_scratch(8, 128, F32)
        scratch += [pltpu.VMEM((16, width), F32)]
        params.update(collective_id=2, has_side_effects=True)
    else:
        outs += [block(w.shape, BF16), block((8, 128), F32), block((16, width), F32)]
    return pl.pallas_call(
        functools.partial(tail_kernel, reduce),
        out_shape=outs,
        in_specs=[VM] * 8,
        out_specs=[VM] * 4,
        scratch_shapes=scratch,
        compiler_params=pltpu.CompilerParams(**params),
        name="tail_step",
    )(*args)


def project_kernel(x, gain, bias, w, b, out):
    @pl.loop(0, x.shape[0] // T)
    def _(t):
        r = pl.ds(pl.multiple_of(t * T, T), T)
        hat, _ = row_norm(x[r, :].astype(F32))
        n1 = (hat * gain[...] + bias[...]).astype(BF16)
        out[r, :] = (mm(n1, w[...]) + b[...]).astype(BF16)


def project(x, gain, bias, w, b):
    return pl.pallas_call(
        project_kernel,
        out_shape=jax.ShapeDtypeStruct((x.shape[0], w.shape[1]), BF16),
        in_specs=[VM] * 5,
        out_specs=VM,
        compiler_params=pltpu.CompilerParams(vmem_limit_bytes=32 * 2**20),
        cost_estimate=pl.CostEstimate(flops=2 * x.shape[0] * w.shape[0] * w.shape[1], bytes_accessed=9 * 2**20, transcendentals=0),
        name="project",
    )(x, gain, bias, w, b)


def finish_kernel(small, *refs):
    copied = (len(refs) - len(SMALLS)) // 2
    for source, target in zip(refs[:copied], refs[copied : 2 * copied]):
        target[...] = source[...]
    for row, out in enumerate(refs[2 * copied :]):
        out[...] = small[row, : out.shape[0]]


def finish(shards, small, *arrays):
    width = arrays[1].shape[1]
    outs = [jax.ShapeDtypeStruct(a.shape, a.dtype) for a in arrays]
    outs += [jax.ShapeDtypeStruct((rows * width // shards,), F32) for _, rows in SMALLS]
    return pl.pallas_call(
        finish_kernel,
        out_shape=outs,
        in_specs=[VM] * (1 + len(arrays)),
        out_specs=[VM] * len(outs),
        name="finish",
    )(small, *arrays)


def halo_of(rows, halo, side):
    mine = jnp.where(side == 0, rows[rows.shape[0] - halo :], rows[:halo])
    return lax.ppermute(mine, "hd", [(0, 1), (1, 0)])


def in_pack_order(own, halo, side, before=0, after=0):
    dims = (own.shape[0] - halo.shape[0], *own.shape[1:])
    late, early = jnp.full(dims, after, own.dtype), jnp.full(dims, before, own.dtype)
    return jnp.where(side == 0, jnp.concatenate([own, halo, late], 0), jnp.concatenate([early, halo, own], 0))


def per_device(tokens, image_ids, keep_masks, ln1_gain, ln1_bias, w_qkv, qv_bias, w_out, b_out,
               ln2_gain, ln2_bias, w_fc1, b_fc1, w_fc2, b_fc2, cotangent):
    rows, width = tokens.shape
    halo = HALO
    both = ("seq", "hd")
    side = lax.axis_index("hd")
    reduce = lax.axis_size("seq") == 16 and lax.axis_size("hd") == 2
    halo_tiles = halo // T
    tok_halo = halo_of(tokens, halo, side)
    id_halo = halo_of(image_ids, halo, side)
    id_all = in_pack_order(image_ids, id_halo, side, -1, 1 << 20)
    ids = id_all.reshape(-1, T)
    one_hot = (image_ids[:, None] == jnp.arange(keep_masks.shape[1], dtype=jnp.int32)[None, :]).astype(F32)
    keep_rows = jnp.dot(one_hot, keep_masks[0].astype(F32)) * drop_scale
    bias_all = jnp.concatenate([qv_bias[:width], jnp.zeros((width,), F32), qv_bias[width:]])

    norm1 = (ln1_gain, ln1_bias, w_qkv, bias_all)
    qkv_own = project(tokens, *norm1)
    heads_out, lse, qkv_all = attn_forward(ids, qkv_own, tok_halo, *norm1)
    mixed, dx1, do_all, stats_all, small, g_out, grad_fc1, grad_fc2 = mlp_step(
        reduce, heads_out, lse, tokens, keep_rows, cotangent, w_out, b_out, ln2_gain, ln2_bias,
        w_fc1, b_fc1, w_fc2, b_fc2)
    if not reduce:
        first = side * rows
        do_own = lax.dynamic_slice_in_dim(do_all, first, rows, 0)
        stats_own = lax.dynamic_slice_in_dim(stats_all, first // T, rows // T, 0)
        do_all = in_pack_order(do_own, halo_of(do_own, halo, side), side)
        stats_all = in_pack_order(stats_own, halo_of(stats_own, halo_tiles, side), side)
    dqkv = attn_backward(ids, qkv_all, do_all, stats_all)
    grad_x, grad_qkv, grad_out, small = tail_step(
        reduce, dqkv, tokens, dx1, ln1_gain, ln1_bias, w_qkv, g_out, small)
    if not reduce:
        grad_out = g_out

        def scatter(v):
            return lax.psum_scatter(v, both, scatter_dimension=0, tiled=True).astype(F32)

        grad_fc1, grad_fc2, grad_qkv, grad_out = map(scatter, (grad_fc1, grad_fc2, grad_qkv, grad_out))
        small = lax.psum(small, both)
    shards = lax.axis_size("seq") * lax.axis_size("hd")
    if reduce:
        grad_qkv, grad_out, grad_fc1, grad_fc2, *vectors = finish(shards, small, grad_qkv, grad_out, grad_fc1, grad_fc2)
    else:
        place = lax.axis_index("seq") * lax.axis_size("hd") + side
        vectors = []
        for first, count in SMALLS:
            size = count * width // shards
            vectors.append(lax.dynamic_slice(small[first : first + count].reshape(-1), (place * size,), (size,)))
    g1, b1, qv, bo, g2, b2, bf1, bf2 = vectors
    return mixed, grad_x, g1, b1, grad_qkv, qv, grad_out, bo, g2, b2, grad_fc1, bf1, grad_fc2, bf2


def solution(mesh):
    both = P(("seq", "hd"))
    split = P(("seq", "hd"), None)
    return jax.shard_map(
        per_device,
        mesh=mesh,
        in_specs=(split, both, P("seq", None, None)) + (P(),) * 12 + (split,),
        out_specs=(split, split, both, both, split, both, split, both, both, both, split, both, split, both),
        check_vma=False,
    )
```

```python
import functools
import jax, jax.numpy as jnp
from jax import lax
from jax.experimental import pallas as pl
from jax.experimental.pallas import tpu as pltpu
from jax.sharding import PartitionSpec as P

HEADS, HEAD = 12, 64
T = 128
W2 = 256
VM = pl.BlockSpec(memory_space=pltpu.VMEM)
SM = pl.BlockSpec(memory_space=pltpu.SMEM)
F32, BF16 = jnp.float32, jnp.bfloat16
NT = (((1,), (1,)), ((), ()))
TN = (((0,), (0,)), ((), ()))


def mm(a, b):
    return jnp.dot(a, b, preferred_element_type=F32)


def mm_nt(a, b):
    return lax.dot_general(a, b, NT, preferred_element_type=F32)


def mm_tn(a, b):
    return lax.dot_general(a, b, TN, preferred_element_type=F32)


def by_head(pair):
    lane = lax.broadcasted_iota(jnp.int32, pair.shape, 1)
    zero = jnp.zeros_like(pair)
    return jnp.concatenate(
        [jnp.where(lane < HEAD, pair, zero), jnp.where(lane < HEAD, zero, pair)], 0
    )


def by_head_rows(pair):
    row = lax.broadcasted_iota(jnp.int32, pair.shape, 0)
    zero = jnp.zeros_like(pair)
    return jnp.concatenate([jnp.where(row < HEAD, pair, zero), jnp.where(row < HEAD, zero, pair)], 1)


def tile_span(ids, first_tile, last_tile):
    low, high = 0, 0
    for u in range(ids.shape[0]):
        low += (ids[u, T - 1] < ids[first_tile, 0]).astype(jnp.int32)
        high += (ids[u, 0] <= ids[last_tile, T - 1]).astype(jnp.int32)
    return low, high


def id_columns(id_row, id_col):
    @pl.loop(0, id_row.shape[0])
    def _(j):
        line = jnp.broadcast_to(id_row[pl.ds(j, 1), :].astype(F32), (T, T))
        id_col[pl.ds(pl.multiple_of(j * T, T), T), :] = line.T


def same_image(id_col, rows, id_row, tile):
    left = id_col[rows, :]
    right = id_row[pl.ds(tile, 1), :].astype(F32)
    return jnp.concatenate([left, left], 1) == jnp.concatenate([right, right], 1)


HALO_ROWS = 304


def attn_forward_kernel(width, ids, id_row, own_qkv, halo, gain, bias, w, b, out, lse, all_qkv, qkv, sc, vt, acc, id_col, sems):
    pairs = width // 128
    rows, tiles = out.shape[0], id_row.shape[0]
    own = rows // T
    side = lax.axis_index("hd")
    off = side * own
    apart = rows - halo.shape[0]
    fetch = pltpu.make_async_copy(own_qkv, qkv.at[pl.ds(pl.multiple_of(side * rows, rows), rows), :], sems.at[0])
    fetch.start()
    id_columns(id_row, id_col)
    qkv[pl.ds(pl.multiple_of((1 - side) * (2 * rows - apart), 16), apart), :] = jnp.zeros((apart, 3 * width), BF16)

    @pl.loop(0, halo.shape[0] // HALO_ROWS)
    def _(t):
        r = pl.ds(pl.multiple_of(t * HALO_ROWS, 16), HALO_ROWS)
        hat, _ = row_norm(halo[r, :].astype(F32))
        n1 = (hat * gain[...] + bias[...]).astype(BF16)
        first = pl.multiple_of((1 - side) * rows + side * apart + t * HALO_ROWS, 16)
        qkv[pl.ds(first, HALO_ROWS), :] = (mm(n1, w[...]) + b[...]).astype(BF16)

    fetch.wait()
    store = pltpu.make_async_copy(qkv, all_qkv, sems.at[1])
    store.start()

    @pl.loop(0, tiles)
    def _(j):
        k0 = pl.multiple_of(j * T, T)
        vt[:, pl.ds(k0, T)] = qkv[pl.ds(k0, T), 2 * width :].T

    @pl.loop(0, own)
    def _(i):
        tile = off + i
        q0 = pl.multiple_of(tile * T, T)
        low, high = tile_span(ids, tile, tile)
        low = jnp.where(jnp.logical_and(lax.rem(high - low, 2) == 1, low > 0), low - 1, low)
        count = (high - low + 1) // 2
        turned = (qkv[pl.ds(q0, T), :width] * BF16(HEAD**-0.5)).T
        stacks = [by_head_rows(turned[p * 128 : p * 128 + 128]) for p in range(pairs)]

        def scores(j, peaks):
            k0 = pl.multiple_of((low + 2 * j) * T, T)
            same = same_image(id_col, pl.ds(k0, W2), id_row, tile)
            held = [mm(qkv[pl.ds(k0, W2), width + p * 128 : width + p * 128 + 128], stacks[p]) for p in range(pairs)]
            news = []
            for p, s in enumerate(held):
                s = jnp.where(same, s, -1e30)
                sc[p, j] = s
                news.append(jnp.maximum(peaks[p], jnp.max(s.reshape(W2 // 8, 8, 2 * T), 0)))
            return tuple(news)

        start = tuple(jnp.full((8, 2 * T), -jnp.inf, F32) for _ in range(pairs))
        peaks = lax.fori_loop(0, count, scores, start)
        peaks = [jnp.max(m, 0, keepdims=True) for m in peaks]
        for p in range(pairs):
            acc[p] = jnp.zeros((128, 2 * T), F32)

        def outputs(j, totals):
            k0 = pl.multiple_of((low + 2 * j) * T, T)
            es, news = [], []
            for p in range(pairs):
                e = jnp.exp(sc[p, j] - peaks[p])
                news.append(totals[p] + jnp.sum(e.reshape(W2 // 8, 8, 2 * T), 0))
                es.append(e.astype(BF16))
            held = [mm(vt[p * 128 : p * 128 + 128, pl.ds(k0, W2)], es[p]) for p in range(pairs)]
            for p in range(pairs):
                acc[p] += held[p]
            return tuple(news)

        totals = lax.fori_loop(0, count, outputs, tuple(jnp.zeros((8, 2 * T), F32) for _ in range(pairs)))
        stats = []
        for p in range(pairs):
            total = jnp.sum(totals[p], 0, keepdims=True)
            scaled = acc[p] * (1.0 / total)
            o = jnp.concatenate([scaled[:HEAD, :T], scaled[HEAD:, T:]], 0)
            out[pl.ds(pl.multiple_of(i * T, T), T), p * 128 : p * 128 + 128] = o.T.astype(BF16)
            stat = peaks[p] + jnp.log(total)
            stats += [stat[:, :T], stat[:, T:]]
        lse[i] = jnp.concatenate(stats + [jnp.zeros((4, T), F32)], 0)

    store.wait()


def attn_forward(ids, own_qkv, halo, gain, bias, w, b):
    rows, width = own_qkv.shape[0], own_qkv.shape[1] // 3
    tiles = ids.shape[0]
    pairs = width // 128
    anywhere = pl.BlockSpec(memory_space=pl.ANY)
    return pl.pallas_call(
        functools.partial(attn_forward_kernel, width),
        out_shape=(
            jax.ShapeDtypeStruct((rows, width), BF16),
            jax.ShapeDtypeStruct((rows // T, 16, T), F32),
            jax.ShapeDtypeStruct((2 * rows, 3 * width), BF16),
        ),
        in_specs=[SM, VM, anywhere] + [VM] * 5,
        out_specs=(VM, VM, anywhere),
        scratch_shapes=[
            pltpu.VMEM((2 * rows, 3 * width), BF16),
            pltpu.VMEM((pairs, tiles // 2, W2, 2 * T), F32),
            pltpu.VMEM((width, 2 * rows), BF16),
            pltpu.VMEM((pairs, 128, 2 * T), F32),
            pltpu.VMEM((2 * rows, T), F32),
            pltpu.SemaphoreType.DMA((2,)),
        ],
        compiler_params=pltpu.CompilerParams(vmem_limit_bytes=56 * 2**20),
        name="attention_forward",
    )(ids, ids, own_qkv, halo, gain, bias, w, b)


def attn_backward_kernel(width, ids, id_row, qkv, do, stats, out, dq, dk, dv, qt, kt, gt, id_col):
    pairs = width // 128
    own = out.shape[0] // T
    off = lax.axis_index("hd") * own
    id_columns(id_row, id_col)
    tiles = id_row.shape[0]
    dq[...] = jnp.zeros_like(dq)

    @pl.loop(0, tiles)
    def _(j):
        k0 = pl.multiple_of(j * T, T)
        rows = pl.ds(k0, T)
        qt[:, rows] = (qkv[rows, :width] * BF16(HEAD**-0.5)).T
        kt[:, rows] = qkv[rows, width : 2 * width].T
        gt[:, rows] = do[rows, :].T

    @pl.loop(0, tiles // 2)
    def _(j):
        k0 = pl.multiple_of(j * W2, W2)
        mine = jnp.logical_and(2 * j >= off, 2 * j < off + own)
        low, high = tile_span(ids, 2 * j, 2 * j + 1)
        low = jnp.where(mine, low, jnp.maximum(low, off))
        high = jnp.where(mine, high, jnp.minimum(high, off + own))
        for p in range(pairs):
            dk[p] = jnp.zeros((W2, 128), F32)
            dv[p] = jnp.zeros((W2, 128), F32)

        @pl.loop(low, high)
        def _(i):
            q0 = pl.multiple_of(i * T, T)
            same = same_image(id_col, pl.ds(k0, W2), id_row, i)
            qs, gs, ss, ps, es, ds = [], [], [], [], [], []
            for p in range(pairs):
                cols = p * 128
                k = qkv[pl.ds(k0, W2), width + cols : width + cols + 128]
                v = qkv[pl.ds(k0, W2), 2 * width + cols : 2 * width + cols + 128]
                ss.append(mm(k, by_head_rows(qt[cols : cols + 128, pl.ds(q0, T)])))
                ps.append(mm(v, by_head_rows(gt[cols : cols + 128, pl.ds(q0, T)])))
            for p in range(pairs):
                one = jnp.concatenate([stats[i, 2 * p : 2 * p + 1, :], stats[i, 2 * p + 1 : 2 * p + 2, :]], 1)
                two = jnp.concatenate([stats[i, 2 * p + 16 : 2 * p + 17, :], stats[i, 2 * p + 17 : 2 * p + 18, :]], 1)
                e = jnp.exp(jnp.where(same, ss[p], -1e30) - one)
                es.append(e.astype(BF16))
                ds.append((e * (ps[p] - two)).astype(BF16))
            a, b, c = [], [], []
            for p in range(pairs):
                cols = p * 128
                a.append(mm(es[p], by_head(do[pl.ds(q0, T), cols : cols + 128])))
                b.append(mm(ds[p], by_head(qkv[pl.ds(q0, T), cols : cols + 128] * BF16(HEAD**-0.5))))
                c.append(mm(kt[cols : cols + 128, pl.ds(k0, W2)], ds[p]))
            for p in range(pairs):
                dv[p] += a[p]
                dk[p] += b[p]
                dq[p, i] += jnp.concatenate([c[p][:HEAD, :T], c[p][HEAD:, T:]], 0)

        @pl.when(mine)
        def _():
            r0 = pl.multiple_of(j * W2 - off * T, W2)
            for p in range(pairs):
                cols = p * 128
                out[pl.ds(r0, W2), width + cols : width + cols + 128] = dk[p].astype(BF16)
                out[pl.ds(r0, W2), 2 * width + cols : 2 * width + cols + 128] = dv[p].astype(BF16)

    @pl.loop(0, own)
    def _(i):
        for p in range(pairs):
            cols = p * 128
            out[pl.ds(pl.multiple_of(i * T, T), T), cols : cols + 128] = (dq[p, off + i] * HEAD**-0.5).T.astype(BF16)


def attn_backward(ids, qkv, do, stats):
    all_rows, columns = qkv.shape
    own_rows = all_rows // 2
    width = columns // 3
    tiles = all_rows // T
    pairs = width // 128
    return pl.pallas_call(
        functools.partial(attn_backward_kernel, width),
        out_shape=jax.ShapeDtypeStruct((own_rows, columns), BF16),
        in_specs=[SM] + [VM] * 4,
        out_specs=VM,
        scratch_shapes=[
            pltpu.VMEM((pairs, tiles, 128, T), F32),
            pltpu.VMEM((pairs, W2, 128), F32),
            pltpu.VMEM((pairs, W2, 128), F32),
            pltpu.VMEM((width, all_rows), BF16),
            pltpu.VMEM((width, all_rows), BF16),
            pltpu.VMEM((width, all_rows), BF16),
            pltpu.VMEM((all_rows, T), F32),
        ],
        compiler_params=pltpu.CompilerParams(vmem_limit_bytes=56 * 2**20),
        name="attention_backward",
    )(ids, ids, qkv, do, stats)


ln_epsilon = 1e-06
drop_scale = 1.0 / 0.9


MESH = pl.DeviceIdType.MESH


class Place:
    def __init__(self):
        self.seq = lax.axis_index("seq")
        self.x = lax.axis_index("hd")
        self.c = lax.rem(self.seq, 2)
        self.y = lax.rem(self.seq // 2, 2)
        self.z = self.seq // 4

    def partner(self, axis):
        if axis == "c":
            return (self.seq + 1 - 2 * self.c, self.x)
        if axis == "y":
            return (self.seq + 2 - 4 * self.y, self.x)
        return (self.seq, 1 - self.x)

    def level(self, step):
        return (lax.rem(self.z + step, 4) * 4 + lax.rem(self.seq, 4), self.x)

    def index(self, axis):
        return {"x": self.x, "y": self.y, "c": self.c}[axis]


def greet(place):
    barrier = pltpu.get_barrier_semaphore()
    for other in [place.partner(a) for a in "cxy"] + [place.level(d) for d in (1, 2, 3)]:
        pl.semaphore_signal(barrier, inc=1, device_id=other, device_id_type=MESH)


def meet():
    pl.semaphore_wait(pltpu.get_barrier_semaphore(), 6)


def send(source, target, send_sem, recv_sem, other):
    copy = pltpu.make_async_remote_copy(
        src_ref=source, dst_ref=target, send_sem=send_sem, recv_sem=recv_sem, device_id=other, device_id_type=MESH
    )
    copy.start()
    return copy


class Flow:
    def __init__(self, place, axes, g, r0, r1, r2, r3, sems, recvs):
        self.place, self.axes, self.g = place, axes, g
        self.r0, self.r1, self.r2, self.r3 = r0, r1, r2, r3
        self.sems, self.recvs = sems, recvs
        self.copies = []

    def start(self):
        p = self.place
        self.copies.append(send(self.g.at[1 - p.c], self.r0, self.sems.at[0], self.recvs.at[0], p.partner("c")))

    def first(self):
        p = self.place
        self.copies[0].wait_recv()
        me = p.index(self.axes[0])

        def add(half):
            @pl.loop(0, 8)
            def _(i):
                b, z = i // 4, lax.rem(i, 4)
                self.r0[half, b, z] = self.r0[half, b, z] + self.g[p.c, half, b, z]

        add(1 - me)
        self.copies.append(
            send(self.r0.at[1 - me], self.r1, self.sems.at[1], self.recvs.at[1], p.partner(self.axes[0]))
        )
        add(me)

    def second(self):
        p = self.place
        self.copies[1].wait_recv()
        me, before = p.index(self.axes[1]), p.index(self.axes[0])

        def add(half):
            @pl.loop(0, 4)
            def _(z):
                self.r1[half, z] = self.r1[half, z] + self.r0[before, half, z]

        add(1 - me)
        self.copies.append(
            send(self.r1.at[1 - me], self.r2, self.sems.at[2], self.recvs.at[2], p.partner(self.axes[1]))
        )
        add(me)

    def third(self):
        p = self.place
        self.copies[2].wait_recv()
        before = p.index(self.axes[1])

        @pl.loop(0, 4)
        def _(z):
            self.r2[z] = self.r2[z] + self.r1[before, z]

        for d in (1, 2, 3):
            target = lax.rem(p.z + d, 4)
            self.copies.append(
                send(self.r2.at[target], self.r3.at[d - 1], self.sems.at[2 + d], self.recvs.at[2 + d], p.level(d))
            )

    def last(self):
        p = self.place
        total = self.r2[p.z].astype(F32)
        for d in (1, 2, 3):
            self.copies[2 + d].wait_recv()
            total = total + self.r3[d - 1].astype(F32)
        return total

    def finish(self):
        for copy in self.copies:
            copy.wait_send()


def flow_scratch(rows, cols, kind=BF16):
    return [
        pltpu.VMEM((2, 2, 4, rows, cols), kind),
        pltpu.VMEM((2, 4, rows, cols), kind),
        pltpu.VMEM((4, rows, cols), kind),
        pltpu.VMEM((3, rows, cols), kind),
        pltpu.SemaphoreType.DMA((6,)),
        pltpu.SemaphoreType.DMA((6,)),
    ]


class ChunkFlow(Flow):
    def __init__(self, place, axes, home, *refs):
        super().__init__(place, axes, *refs)
        self.home = home

    def third(self):
        p = self.place
        self.copies[2].wait_recv()
        self.r2[...] = self.r2[...] + self.r1[p.index(self.axes[1])]
        slot = lax.rem(p.z - self.home + 3, 4)
        self.hop = pltpu.make_async_remote_copy(
            src_ref=self.r2,
            dst_ref=self.r3.at[slot],
            send_sem=self.sems.at[3],
            recv_sem=self.recvs.at[3 + slot],
            device_id=(self.home * 4 + lax.rem(p.seq, 4), p.x),
            device_id_type=MESH,
        )

        @pl.when(p.z != self.home)
        def _():
            self.hop.start()

    def first(self):
        p = self.place
        self.copies[0].wait_recv()
        me = p.index(self.axes[0])

        def add(half):
            for b in range(2):
                self.r0[half, b] = self.r0[half, b] + self.g[p.c, half, b]

        add(1 - me)
        self.copies.append(
            send(self.r0.at[1 - me], self.r1, self.sems.at[1], self.recvs.at[1], p.partner(self.axes[0]))
        )
        add(me)

    def second(self):
        p = self.place
        self.copies[1].wait_recv()
        me, before = p.index(self.axes[1]), p.index(self.axes[0])
        self.r1[1 - me] = self.r1[1 - me] + self.r0[before, 1 - me]
        self.copies.append(
            send(self.r1.at[1 - me], self.r2, self.sems.at[2], self.recvs.at[2], p.partner(self.axes[1]))
        )
        self.r1[me] = self.r1[me] + self.r0[before, me]

    def last_into(self, out):
        p = self.place

        @pl.when(p.z == self.home)
        def _():
            total = self.r2[...].astype(F32)
            for slot in range(3):
                pltpu.make_async_remote_copy(
                    src_ref=self.r2,
                    dst_ref=self.r3.at[slot],
                    send_sem=self.sems.at[3],
                    recv_sem=self.recvs.at[3 + slot],
                    device_id=p.level(1),
                    device_id_type=MESH,
                ).wait_recv()
                total = total + self.r3[slot].astype(F32)
            out[...] = total

    def finish(self):
        super().finish()

        @pl.when(self.place.z != self.home)
        def _():
            self.hop.wait_send()


class LevelFlow(Flow):
    axes = "zxy"

    def __init__(self, place, g, r0, r1, r2, r3, sems, recvs):
        super().__init__(place, "zxy", g, r0, r1, r2, r3, sems, recvs)

    def first(self):
        p = self.place
        self.copies[0].wait_recv()

        @pl.loop(0, 4)
        def _(z):
            for x in range(2):
                for y in range(2):
                    self.r0[z, x, y] = self.r0[z, x, y] + self.g[p.c, z, x, y]

        for d in (1, 2, 3):
            self.copies.append(
                send(self.r0.at[lax.rem(p.z + d, 4)], self.r1.at[d - 1], self.sems.at[d], self.recvs.at[d], p.level(d))
            )

    def second(self):
        p = self.place
        for d in (1, 2, 3):
            self.copies[d].wait_recv()
        for x in range(2):
            for y in range(2):
                total = self.r0[p.z, x, y].astype(F32)
                for d in range(3):
                    total = total + self.r1[d, x, y].astype(F32)
                self.r1[0, x, y] = total.astype(BF16)
        self.copies.append(
            send(self.r1.at[0, 1 - p.x], self.r2, self.sems.at[4], self.recvs.at[4], p.partner("x"))
        )

    def third(self):
        p = self.place
        self.copies[4].wait_recv()
        for y in range(2):
            self.r2[y] = self.r2[y] + self.r1[0, p.x, y]
        self.copies.append(send(self.r2.at[1 - p.y], self.r3, self.sems.at[5], self.recvs.at[5], p.partner("y")))

    def last(self):
        self.copies[5].wait_recv()
        return self.r2[self.place.y].astype(F32) + self.r3[...].astype(F32)


def level_scratch(rows, cols):
    return [
        pltpu.VMEM((4, 2, 2, rows, cols), BF16),
        pltpu.VMEM((3, 2, 2, rows, cols), BF16),
        pltpu.VMEM((2, rows, cols), BF16),
        pltpu.VMEM((rows, cols), BF16),
        pltpu.SemaphoreType.DMA((6,)),
        pltpu.SemaphoreType.DMA((6,)),
    ]


def chunk_scratch(rows, cols):
    return [
        pltpu.VMEM((2, 2, rows, cols), BF16),
        pltpu.VMEM((2, rows, cols), BF16),
        pltpu.VMEM((rows, cols), BF16),
        pltpu.VMEM((3, rows, cols), BF16),
        pltpu.SemaphoreType.DMA((6,)),
        pltpu.SemaphoreType.DMA((6,)),
    ]


def row_norm(x):
    mean = jnp.mean(x, -1, keepdims=True)
    center = x - mean
    rstd = lax.rsqrt(jnp.mean(center * center, -1, keepdims=True) + ln_epsilon)
    return center * rstd, rstd


def norm_back(hat, rstd, gain, grad):
    scaled = grad * gain
    return rstd * (scaled - jnp.mean(scaled, -1, keepdims=True) - hat * jnp.mean(scaled * hat, -1, keepdims=True))


def col_sum(x):
    return jnp.sum(x, 0, keepdims=True)


def put_blocks(product, z, axes, g):
    half = product.shape[1] // 2
    for y in range(2):
        for c in range(2):
            for x in range(2):
                r = ((y * 2 + c) * 2 + x) * 24
                block = jnp.concatenate([product[r : r + 24, :half], product[r : r + 24, half:]], 0)
                at = {"x": x, "y": y}
                if axes == "zxy":
                    g[c, z, x, y] = block.astype(BF16)
                else:
                    g[c, at[axes[0]], at[axes[1]], z] = block.astype(BF16)


def put_chunk(product, y, axes, g):
    for c in range(2):
        for x in range(2):
            r = (c * 2 + x) * 96
            at = {"x": x, "y": y}
            g[c, at[axes[0]], at[axes[1]]] = product[r : r + 96].astype(BF16)


R = 256
HALO = 608
FLOW_REFS = 6
ORDER = (0, 3, 1, 2)
PATHS1 = ("xy", "xy", "zxy", "xy")
PATHS2 = ("yx", "yx", "yx", "yx")


def mlp_kernel(reduce, chunks, *refs):
    o, lse, x, keep, cot, w_out, b_out, gain, bias, w1, b1, w2, b2 = refs[:13]
    mixed, dx1, do, stats, small, g_out, out1, out2 = refs[13:21]
    v1, v2, x1s, n2s, n2t, dms, gs, dus, das, macc, nacc, load1, load2, halo_sems = refs[21:35]
    flow_refs = refs[35:]
    side = lax.axis_index("hd")
    base = pl.multiple_of(side * o.shape[0], o.shape[0])
    owner = lax.broadcasted_iota(jnp.int32, (16, o.shape[1]), 1) // HEAD
    heads = (owner == lax.broadcasted_iota(jnp.int32, (16, o.shape[1]), 0)).astype(BF16)
    rows, width = o.shape
    tiles = rows // R
    loads = []
    for k in range(chunks):
        cols = pl.ds(k * width, width)
        loads.append(
            (
                pltpu.make_async_copy(w1.at[:, cols], v1.at[k], load1.at[k]),
                pltpu.make_async_copy(w2.at[cols, :], v2.at[k], load2.at[k]),
            )
        )
        loads[k][0].start()
        loads[k][1].start()
    if reduce:
        place = Place()
        greet(place)
        per = 1 + FLOW_REFS
        flows1 = []
        for k in range(chunks):
            mine = flow_refs[2 * per * k : 2 * per * k + per]
            flows1.append(LevelFlow(place, *mine) if PATHS1[k] == "zxy" else Flow(place, PATHS1[k], *mine))
        flows2 = [ChunkFlow(place, PATHS2[k], k, *flow_refs[2 * per * k + per : 2 * per * (k + 1)]) for k in range(chunks)]

    small[...] = jnp.zeros_like(small)

    @pl.loop(0, tiles)
    def _(t):
        r = pl.ds(pl.multiple_of(t * R, R), R)
        x1 = x[r, :].astype(F32) + keep[r, 0:1] * (mm(o[r, :], w_out[...]) + b_out[...])
        x1s[r, :] = x1
        hat, _ = row_norm(x1)
        n2 = (hat * gain[...] + bias[...]).astype(BF16)
        n2s[r, :] = n2
        dm = (cot[r, :].astype(F32) * keep[r, 1:2]).astype(BF16)
        dms[r, :] = dm
        small[7:8, :] += col_sum(dm.astype(F32))

    n2t[...] = n2s[...].T

    def row_tile(k, t, first, slot):
        r = slice(t * R, t * R + R)
        u = mm(n2s[r, :], v1[k]) + b1[k * width : k * width + width]
        dg = mm_nt(dms[r, :], v2[k])
        cdf = 0.5 + 0.5 * lax.erf(u * 0.7071067811865476)
        pdf = jnp.exp(u * u * -0.5) * 0.3989422804014327
        g = (u * cdf).astype(BF16)
        du = (dg * (cdf + u * pdf)).astype(BF16)
        gs[slot, r, :] = g
        dus[slot, r, :] = du
        small[3 + k : 4 + k, :] += col_sum(du.astype(F32))
        if first:
            macc[r, :] = mm(g, v2[k])
            nacc[r, :] = mm_nt(du, v1[k])
        else:
            macc[r, :] += mm(g, v2[k])
            nacc[r, :] += mm_nt(du, v1[k])

    steps = {}
    if reduce:
        for at, k in enumerate(ORDER[:3]):
            for flow, late in ((flows2[k], 0), (flows1[k], 1)):
                steps.setdefault((at + 1, 1 + late), []).append(flow.first)
                if at < 2:
                    steps.setdefault((at + 2, 1 + late), []).append(flow.second)
                    steps.setdefault((2, 5) if at == 0 else (4, 1 + late), []).append(flow.third)

    def point(*at):
        for step in steps.pop(at, []):
            step()

    def gradient2(k, slot):
        @pl.loop(0, 2)
        def _(y):
            product = mm_tn(gs[slot, :, pl.ds(pl.multiple_of(y * 384, 384), 384)], dms[...])
            put_chunk(product, y, flows2[k].axes, flows2[k].g)

        flows2[k].start()

    def gradient1(k, slot):
        @pl.loop(0, 2)
        def _(h):
            product = mm(n2t[pl.ds(pl.multiple_of(h * 384, 128), 384), :], dus[slot])
            for z in range(2):
                put_blocks(product[z * 192 : z * 192 + 192], 2 * h + z, flows1[k].axes, flows1[k].g)

        flows1[k].start()

    for at, k in enumerate(ORDER if reduce else range(chunks)):
        slot = at % 2
        loads[k][0].wait()
        loads[k][1].wait()
        for t in range(tiles):
            row_tile(k, t, at == 0, slot)
            point(at, t + 1)
        if reduce and at == 0:
            meet()
        if reduce and at < 3:
            gradient2(k, slot)
            point(at, 4)
            gradient1(k, slot)
            point(at, 5)
        if not reduce:

            @pl.loop(0, 3)
            def _(t):
                r = pl.ds(pl.multiple_of(t * 256, 256), 256)
                out2[pl.ds(pl.multiple_of(k * width + t * 256, 256), 256), :] = mm_tn(gs[slot, :, r], dms[...]).astype(BF16)
                out1[r, k * width : k * width + width] = mm(n2t[r, :], dus[slot]).astype(BF16)

    apart = rows - HALO
    pad = pl.multiple_of((1 - side) * (2 * rows - apart), 16)
    do[pl.ds(pad, apart), :] = jnp.zeros((apart, width), BF16)
    stat_tiles = pl.cdiv(HALO, T)
    spare = rows // T - stat_tiles
    for s in range(spare):
        stats[(1 - side) * (2 * rows // T - spare) + s] = jnp.zeros((32, T), F32)
    exchange = []

    def exchange_rows(ref, first, count, n):
        part = ref.at[pl.ds(first, count)]
        exchange.append(send(part, part, halo_sems.at[2 * n], halo_sems.at[2 * n + 1], place.partner("x")))

    for t in range(tiles):
        at = lax.rem(t + 1 - side, tiles)
        r = pl.ds(pl.multiple_of(at * R, R), R)
        hat, rstd = row_norm(x1s[r, :])
        dn2 = nacc[r, :]
        dx = cot[r, :].astype(F32) + norm_back(hat, rstd, gain[...], dn2)
        dx1[r, :] = dx
        da = (dx * keep[r, 0:1]).astype(BF16)
        das[r, :] = da
        grad_o = mm_nt(da, w_out[...]).astype(BF16)
        do[pl.ds(pl.multiple_of(base + at * R, R), R), :] = grad_o
        small[0:1, :] += col_sum(da.astype(F32))
        small[1:2, :] += col_sum(dn2 * hat)
        small[2:3, :] += col_sum(dn2)
        prod = grad_o.astype(F32) * o[r, :].astype(F32)
        high = prod.astype(BF16)
        low = (prod - high.astype(F32)).astype(BF16)
        sums = mm_nt(heads, high) + mm_nt(heads, low)
        for s in range(R // T):
            own = at * (R // T) + s
            stats[side * (rows // T) + own, :16] = lse[own]
            stats[side * (rows // T) + own, 16:] = sums[:, s * T : s * T + T]
        point(chunks, t + 1)
        if reduce and t == 0:
            exchange_rows(do, pl.multiple_of(base + at * R, R), R, 0)

    if reduce:
        third, fourth = ORDER[2], ORDER[3]
        exchange_rows(stats, spare + side * stat_tiles, stat_tiles, 3)
        gradient2(fourth, 1)
        gradient1(fourth, 1)

    n2t[...] = o[...].T
    if reduce:

        @pl.loop(0, 2)
        def _(h):
            product = mm(n2t[pl.ds(pl.multiple_of(h * 384, 128), 384), :], das[...])
            for z in range(2):
                put_blocks(product[z * 192 : z * 192 + 192], 2 * h + z, "zxy", g_out)

        flows2[fourth].first()
        flows1[fourth].first()
        flows2[third].second()
        flows1[third].second()
    else:

        @pl.loop(0, 3)
        def _(t):
            r = pl.ds(pl.multiple_of(t * 256, 256), 256)
            g_out[r, :] = mm(n2t[r, :], das[...]).astype(BF16)

    @pl.loop(0, tiles)
    def _(t):
        r = pl.ds(pl.multiple_of(t * R, R), R)
        mixed[r, :] = (x1s[r, :] + keep[r, 1:2] * (macc[r, :] + b2[...])).astype(BF16)

    if reduce:
        half = width // 2

        def keep_share(k):
            total = flows1[k].last()
            out1[:, k * width : k * width + half] = total[:24]
            out1[:, k * width + half : (k + 1) * width] = total[24:]
            flows2[k].last_into(out2)

        for at in sorted(steps):
            point(*at)
        second_tile = 2 - side
        exchange_rows(do, pl.multiple_of(base + second_tile * R, R), R, 1)
        flows2[third].third()
        flows1[third].third()
        flows2[fourth].second()
        exchange_rows(do, pl.multiple_of(base + (1 - side) * apart + side * 2 * R, 16), HALO - 2 * R, 2)
        flows1[fourth].second()
        flows2[fourth].third()
        flows1[fourth].third()
        for k in range(chunks):
            keep_share(k)
        for k in range(chunks):
            flows1[k].finish()
            flows2[k].finish()
        for copy in exchange:
            copy.wait()


def mlp_step(reduce, o, lse, x, keep, cot, w_out, b_out, gain, bias, w1, b1, w2, b2):
    rows, width = o.shape
    chunks = w1.shape[1] // width
    block = lambda dims, kind: jax.ShapeDtypeStruct(dims, kind)
    outs = [
        block((rows, width), BF16),
        block((rows, width), F32),
        block((2 * rows, width), BF16),
        block((2 * rows // T, 32, T), F32),
        block((16, width), F32),
    ]
    if reduce:
        outs += [block((2, 4, 2, 2, 48, width // 2), BF16), block((24, chunks * width), F32), block((96, width), F32)]
    else:
        outs += [block((width, width), BF16), block(w1.shape, BF16), block(w2.shape, BF16)]
    scratch = [
        pltpu.VMEM((chunks, width, width), BF16),
        pltpu.VMEM((chunks, width, width), BF16),
        pltpu.VMEM((rows, width), F32),
        pltpu.VMEM((rows, width), BF16),
        pltpu.VMEM((width, rows), BF16),
        pltpu.VMEM((rows, width), BF16),
        pltpu.VMEM((2, rows, width), BF16),
        pltpu.VMEM((2, rows, width), BF16),
        pltpu.VMEM((rows, width), BF16),
        pltpu.VMEM((rows, width), F32),
        pltpu.VMEM((rows, width), F32),
        pltpu.SemaphoreType.DMA((chunks,)),
        pltpu.SemaphoreType.DMA((chunks,)),
        pltpu.SemaphoreType.DMA((8,)),
    ]
    params = dict(vmem_limit_bytes=60 * 2**20)
    if reduce:
        for k in range(chunks):
            if PATHS1[k] == "zxy":
                scratch += [pltpu.VMEM((2, 4, 2, 2, 48, width // 2), BF16)] + level_scratch(48, width // 2)
            else:
                scratch += [pltpu.VMEM((2, 2, 2, 4, 48, width // 2), BF16)] + flow_scratch(48, width // 2)
            scratch += [pltpu.VMEM((2, 2, 2, 96, width), BF16)] + chunk_scratch(96, width)
        params.update(collective_id=1, has_side_effects=True)
    anywhere = pl.BlockSpec(memory_space=pl.ANY)
    return pl.pallas_call(
        functools.partial(mlp_kernel, reduce, chunks),
        out_shape=outs,
        in_specs=[VM] * 9 + [anywhere, VM, anywhere, VM],
        out_specs=[VM] * 8,
        scratch_shapes=scratch,
        compiler_params=pltpu.CompilerParams(**params),
        name="mlp_step",
    )(o, lse, x, keep, cot, w_out, b_out, gain, bias, w1, b1, w2, b2)


SMALLS = ((8, 1), (9, 1), (10, 2), (0, 1), (1, 1), (2, 1), (3, 4), (7, 1))


def by_owner(sums):
    width = sums.shape[1]
    lane = lax.broadcasted_iota(jnp.int32, (32, width), 1)
    block = lax.broadcasted_iota(jnp.int32, (32, width), 0)
    source = lax.broadcasted_iota(jnp.int32, (width, 128), 0)
    target = lax.broadcasted_iota(jnp.int32, (width, 128), 1)
    parts = []
    for first, rows in SMALLS:
        size = rows * width // 32
        row = block // (32 // rows)
        spread = jnp.zeros((32, width), F32)
        for r in range(rows):
            spread = jnp.where(row == r, sums[first + r : first + r + 1, :], spread)
        spread = jnp.where(lane // size == lax.rem(block, 32 // rows), spread, 0.0)
        pick = (lax.rem(source, size) == target).astype(BF16)
        total = jnp.zeros((32, 128), F32)
        for _ in range(3):
            piece = spread.astype(BF16)
            total = total + mm(piece, pick)
            spread = spread - piece.astype(F32)
        parts.append(total.reshape(32, 1, 128))
    return jnp.concatenate(parts, 1)


def tail_kernel(reduce, *refs):
    dqkv, x, dx1, gain, bias, w, g_out, small_in = refs[:8]
    grad_x, grad_w, grad_o, small = refs[8:12]
    n1s, n1t = refs[12:14]
    rest = refs[14:]
    rows, width = x.shape
    tiles = rows // R
    if reduce:
        place = Place()
        greet(place)
        out_flow = LevelFlow(place, g_out, *rest[:6])
        flows = [Flow(place, ("yx", "xy", "yx")[i], *rest[6 + 7 * i : 13 + 7 * i]) for i in range(3)]
        sums = Flow(place, "xy", *rest[27:34])

    @pl.loop(0, tiles)
    def _(t):
        r = pl.ds(pl.multiple_of(t * R, R), R)
        hat, _ = row_norm(x[r, :].astype(F32))
        n1s[r, :] = (hat * gain[...] + bias[...]).astype(BF16)

    n1t[...] = n1s[...].T
    if reduce:
        meet()
        out_flow.start()
        for i in range(3):

            @pl.loop(0, 2)
            def _(h):
                product = mm(n1t[pl.ds(pl.multiple_of(h * 384, 128), 384), :], dqkv[:, i * width : (i + 1) * width])
                for z in range(2):
                    put_blocks(product[z * 192 : z * 192 + 192], 2 * h + z, flows[i].axes, flows[i].g)

            flows[i].start()
            if i == 0:
                out_flow.first()
            else:
                flows[i - 1].first()
    else:

        @pl.loop(0, 3)
        def _(t):
            r = pl.ds(pl.multiple_of(t * 256, 256), 256)
            for i in range(3):
                grad_w[r, i * width : (i + 1) * width] = mm(n1t[r, :], dqkv[:, i * width : (i + 1) * width]).astype(BF16)

    small_ref = rest[34] if reduce else small
    small_ref[...] = small_in[...]

    def rows_back(t):
        r = pl.ds(pl.multiple_of(t * R, R), R)
        hat, rstd = row_norm(x[r, :].astype(F32))
        dn1 = mm_nt(dqkv[r, :], w[...])
        grad_x[r, :] = dx1[r, :] + norm_back(hat, rstd, gain[...], dn1)
        small_ref[8:9, :] += col_sum(dn1 * hat)
        small_ref[9:10, :] += col_sum(dn1)
        small_ref[10:11, :] += col_sum(dqkv[r, :width].astype(F32))
        small_ref[11:12, :] += col_sum(dqkv[r, 2 * width :].astype(F32))

    pl.loop(0, tiles)(rows_back)
    if reduce:
        half = width // 2
        shares = by_owner(small_ref[...])
        for b in range(32):
            sums.g[b // 2 % 2, b % 2, b // 4 % 2, b // 8] = shares[b]
        sums.start()
        flows[0].second()
        flows[2].first()
        sums.first()
        flows[1].second()
        out_flow.second()
        sums.second()
        flows[0].third()
        out_flow.third()
        flows[1].third()
        sums.third()
        flows[2].second()
        flows[2].third()
        total = out_flow.last()
        grad_o[:, :half] = total[:24]
        grad_o[:, half:] = total[24:]
        small[...] = sums.last()
        for i in range(3):
            total = flows[i].last()
            grad_w[:, i * width : i * width + half] = total[:24]
            grad_w[:, i * width + half : (i + 1) * width] = total[24:]
        for flow in (out_flow, *flows, sums):
            flow.finish()


def tail_step(reduce, dqkv, x, dx1, gain, bias, w, g_out, small):
    rows, width = x.shape
    block = lambda dims, kind: jax.ShapeDtypeStruct(dims, kind)
    outs = [block((rows, width), F32)]
    scratch = [pltpu.VMEM((rows, width), BF16), pltpu.VMEM((width, rows), BF16)]
    params = dict(vmem_limit_bytes=60 * 2**20)
    args = [dqkv, x, dx1, gain, bias, w, g_out, small]
    if reduce:
        outs += [block((24, 3 * width), F32), block((24, width), F32), block((8, 128), F32)]
        scratch += level_scratch(48, width // 2)
        for _ in range(3):
            scratch += [pltpu.VMEM((2, 2, 2, 4, 48, width // 2), BF16)] + flow_scratch(48, width // 2)
        scratch += [pltpu.VMEM((2, 2, 2, 4, 8, 128), F32)] + flow_scratch(8, 128, F32)
        scratch += [pltpu.VMEM((16, width), F32)]
        params.update(collective_id=2, has_side_effects=True)
    else:
        outs += [block(w.shape, BF16), block((8, 128), F32), block((16, width), F32)]
    return pl.pallas_call(
        functools.partial(tail_kernel, reduce),
        out_shape=outs,
        in_specs=[VM] * 8,
        out_specs=[VM] * 4,
        scratch_shapes=scratch,
        compiler_params=pltpu.CompilerParams(**params),
        name="tail_step",
    )(*args)


def project_kernel(x, gain, bias, w, b, out):
    @pl.loop(0, x.shape[0] // T)
    def _(t):
        r = pl.ds(pl.multiple_of(t * T, T), T)
        hat, _ = row_norm(x[r, :].astype(F32))
        n1 = (hat * gain[...] + bias[...]).astype(BF16)
        out[r, :] = (mm(n1, w[...]) + b[...]).astype(BF16)


def project(x, gain, bias, w, b):
    return pl.pallas_call(
        project_kernel,
        out_shape=jax.ShapeDtypeStruct((x.shape[0], w.shape[1]), BF16),
        in_specs=[VM] * 5,
        out_specs=VM,
        compiler_params=pltpu.CompilerParams(vmem_limit_bytes=32 * 2**20),
        cost_estimate=pl.CostEstimate(flops=2 * x.shape[0] * w.shape[0] * w.shape[1], bytes_accessed=9 * 2**20, transcendentals=0),
        name="project",
    )(x, gain, bias, w, b)


def finish_kernel(small, *refs):
    copied = (len(refs) - len(SMALLS)) // 2
    for source, target in zip(refs[:copied], refs[copied : 2 * copied]):
        target[...] = source[...]
    for row, out in enumerate(refs[2 * copied :]):
        out[...] = small[row, : out.shape[0]]


def finish(shards, small, *arrays):
    width = arrays[1].shape[1]
    outs = [jax.ShapeDtypeStruct(a.shape, a.dtype) for a in arrays]
    outs += [jax.ShapeDtypeStruct((rows * width // shards,), F32) for _, rows in SMALLS]
    return pl.pallas_call(
        finish_kernel,
        out_shape=outs,
        in_specs=[VM] * (1 + len(arrays)),
        out_specs=[VM] * len(outs),
        name="finish",
    )(small, *arrays)


def halo_of(rows, halo, side):
    mine = jnp.where(side == 0, rows[rows.shape[0] - halo :], rows[:halo])
    return lax.ppermute(mine, "hd", [(0, 1), (1, 0)])


def in_pack_order(own, halo, side, before=0, after=0):
    dims = (own.shape[0] - halo.shape[0], *own.shape[1:])
    late, early = jnp.full(dims, after, own.dtype), jnp.full(dims, before, own.dtype)
    return jnp.where(side == 0, jnp.concatenate([own, halo, late], 0), jnp.concatenate([early, halo, own], 0))


def per_device(tokens, image_ids, keep_masks, ln1_gain, ln1_bias, w_qkv, qv_bias, w_out, b_out,
               ln2_gain, ln2_bias, w_fc1, b_fc1, w_fc2, b_fc2, cotangent):
    rows, width = tokens.shape
    halo = HALO
    both = ("seq", "hd")
    side = lax.axis_index("hd")
    reduce = lax.axis_size("seq") == 16 and lax.axis_size("hd") == 2
    halo_tiles = pl.cdiv(halo, T)
    tok_halo = halo_of(tokens, halo, side)
    id_halo = halo_of(image_ids, halo, side)
    id_all = in_pack_order(image_ids, id_halo, side, -1, 1 << 20)
    ids = id_all.reshape(-1, T)
    one_hot = (image_ids[:, None] == jnp.arange(keep_masks.shape[1], dtype=jnp.int32)[None, :]).astype(F32)
    keep_rows = jnp.dot(one_hot, keep_masks[0].astype(F32)) * drop_scale
    bias_all = jnp.concatenate([qv_bias[:width], jnp.zeros((width,), F32), qv_bias[width:]])

    norm1 = (ln1_gain, ln1_bias, w_qkv, bias_all)
    qkv_own = project(tokens, *norm1)
    heads_out, lse, qkv_all = attn_forward(ids, qkv_own, tok_halo, *norm1)
    mixed, dx1, do_all, stats_all, small, g_out, grad_fc1, grad_fc2 = mlp_step(
        reduce, heads_out, lse, tokens, keep_rows, cotangent, w_out, b_out, ln2_gain, ln2_bias,
        w_fc1, b_fc1, w_fc2, b_fc2)
    if not reduce:
        first = side * rows
        do_own = lax.dynamic_slice_in_dim(do_all, first, rows, 0)
        stats_own = lax.dynamic_slice_in_dim(stats_all, first // T, rows // T, 0)
        do_all = in_pack_order(do_own, halo_of(do_own, halo, side), side)
        stats_all = in_pack_order(stats_own, halo_of(stats_own, halo_tiles, side), side)
    dqkv = attn_backward(ids, qkv_all, do_all, stats_all)
    grad_x, grad_qkv, grad_out, small = tail_step(
        reduce, dqkv, tokens, dx1, ln1_gain, ln1_bias, w_qkv, g_out, small)
    if not reduce:
        grad_out = g_out

        def scatter(v):
            return lax.psum_scatter(v, both, scatter_dimension=0, tiled=True).astype(F32)

        grad_fc1, grad_fc2, grad_qkv, grad_out = map(scatter, (grad_fc1, grad_fc2, grad_qkv, grad_out))
        small = lax.psum(small, both)
    shards = lax.axis_size("seq") * lax.axis_size("hd")
    if reduce:
        grad_qkv, grad_out, grad_fc1, grad_fc2, *vectors = finish(shards, small, grad_qkv, grad_out, grad_fc1, grad_fc2)
    else:
        place = lax.axis_index("seq") * lax.axis_size("hd") + side
        vectors = []
        for first, count in SMALLS:
            size = count * width // shards
            vectors.append(lax.dynamic_slice(small[first : first + count].reshape(-1), (place * size,), (size,)))
    g1, b1, qv, bo, g2, b2, bf1, bf2 = vectors
    return mixed, grad_x, g1, b1, grad_qkv, qv, grad_out, bo, g2, b2, grad_fc1, bf1, grad_fc2, bf2


def solution(mesh):
    both = P(("seq", "hd"))
    split = P(("seq", "hd"), None)
    return jax.shard_map(
        per_device,
        mesh=mesh,
        in_specs=(split, both, P("seq", None, None)) + (P(),) * 12 + (split,),
        out_specs=(split, split, both, both, split, both, split, both, both, both, split, both, split, both),
        check_vma=False,
    )
```

```python
import functools
import jax, jax.numpy as jnp
from jax import lax
from jax.experimental import pallas as pl
from jax.experimental.pallas import tpu as pltpu
from jax.sharding import PartitionSpec as P

HEADS, HEAD = 12, 64
T = 128
W2 = 256
VM = pl.BlockSpec(memory_space=pltpu.VMEM)
SM = pl.BlockSpec(memory_space=pltpu.SMEM)
F32, BF16 = jnp.float32, jnp.bfloat16
NT = (((1,), (1,)), ((), ()))
TN = (((0,), (0,)), ((), ()))


def mm(a, b):
    return jnp.dot(a, b, preferred_element_type=F32)


def mm_nt(a, b):
    return lax.dot_general(a, b, NT, preferred_element_type=F32)


def mm_tn(a, b):
    return lax.dot_general(a, b, TN, preferred_element_type=F32)


def by_head(pair):
    lane = lax.broadcasted_iota(jnp.int32, pair.shape, 1)
    zero = jnp.zeros_like(pair)
    return jnp.concatenate(
        [jnp.where(lane < HEAD, pair, zero), jnp.where(lane < HEAD, zero, pair)], 0
    )


def by_head_rows(pair):
    row = lax.broadcasted_iota(jnp.int32, pair.shape, 0)
    zero = jnp.zeros_like(pair)
    return jnp.concatenate([jnp.where(row < HEAD, pair, zero), jnp.where(row < HEAD, zero, pair)], 1)


def tile_span(ids, first_tile, last_tile):
    low, high = 0, 0
    for u in range(ids.shape[0]):
        low += (ids[u, T - 1] < ids[first_tile, 0]).astype(jnp.int32)
        high += (ids[u, 0] <= ids[last_tile, T - 1]).astype(jnp.int32)
    return low, high


def id_columns(id_row, id_col):
    @pl.loop(0, id_row.shape[0])
    def _(j):
        line = jnp.broadcast_to(id_row[pl.ds(j, 1), :].astype(F32), (T, T))
        id_col[pl.ds(pl.multiple_of(j * T, T), T), :] = line.T


def same_image(id_col, rows, id_row, tile):
    left = id_col[rows, :]
    right = id_row[pl.ds(tile, 1), :].astype(F32)
    return jnp.concatenate([left, left], 1) == jnp.concatenate([right, right], 1)


HALO_ROWS = 304


def attn_forward_kernel(width, ids, id_row, own_qkv, halo, gain, bias, w, b, out, lse, all_qkv, qkv, sc, vt, acc, id_col, sems):
    pairs = width // 128
    rows, tiles = out.shape[0], id_row.shape[0]
    own = rows // T
    side = lax.axis_index("hd")
    off = side * own
    apart = rows - halo.shape[0]
    fetch = pltpu.make_async_copy(own_qkv, qkv.at[pl.ds(pl.multiple_of(side * rows, rows), rows), :], sems.at[0])
    fetch.start()
    id_columns(id_row, id_col)
    qkv[pl.ds(pl.multiple_of((1 - side) * (2 * rows - apart), 16), apart), :] = jnp.zeros((apart, 3 * width), BF16)

    @pl.loop(0, halo.shape[0] // HALO_ROWS)
    def _(t):
        r = pl.ds(pl.multiple_of(t * HALO_ROWS, 16), HALO_ROWS)
        hat, _ = row_norm(halo[r, :].astype(F32))
        n1 = (hat * gain[...] + bias[...]).astype(BF16)
        first = pl.multiple_of((1 - side) * rows + side * apart + t * HALO_ROWS, 16)
        qkv[pl.ds(first, HALO_ROWS), :] = (mm(n1, w[...]) + b[...]).astype(BF16)

    fetch.wait()
    store = pltpu.make_async_copy(qkv, all_qkv, sems.at[1])
    store.start()

    @pl.loop(0, tiles)
    def _(j):
        k0 = pl.multiple_of(j * T, T)
        vt[:, pl.ds(k0, T)] = qkv[pl.ds(k0, T), 2 * width :].T

    @pl.loop(0, own)
    def _(i):
        tile = off + i
        q0 = pl.multiple_of(tile * T, T)
        low, high = tile_span(ids, tile, tile)
        low = jnp.where(jnp.logical_and(lax.rem(high - low, 2) == 1, low > 0), low - 1, low)
        count = (high - low + 1) // 2
        turned = (qkv[pl.ds(q0, T), :width] * BF16(HEAD**-0.5)).T
        stacks = [by_head_rows(turned[p * 128 : p * 128 + 128]) for p in range(pairs)]

        def scores(j, peaks):
            k0 = pl.multiple_of((low + 2 * j) * T, T)
            same = same_image(id_col, pl.ds(k0, W2), id_row, tile)
            held = [mm(qkv[pl.ds(k0, W2), width + p * 128 : width + p * 128 + 128], stacks[p]) for p in range(pairs)]
            news = []
            for p, s in enumerate(held):
                s = jnp.where(same, s, -1e30)
                sc[p, j] = s
                news.append(jnp.maximum(peaks[p], jnp.max(s.reshape(W2 // 8, 8, 2 * T), 0)))
            return tuple(news)

        start = tuple(jnp.full((8, 2 * T), -jnp.inf, F32) for _ in range(pairs))
        peaks = lax.fori_loop(0, count, scores, start)
        peaks = [jnp.max(m, 0, keepdims=True) for m in peaks]
        for p in range(pairs):
            acc[p] = jnp.zeros((128, 2 * T), F32)

        def outputs(j, totals):
            k0 = pl.multiple_of((low + 2 * j) * T, T)
            es, news = [], []
            for p in range(pairs):
                e = jnp.exp(sc[p, j] - peaks[p])
                news.append(totals[p] + jnp.sum(e.reshape(W2 // 8, 8, 2 * T), 0))
                es.append(e.astype(BF16))
            held = [mm(vt[p * 128 : p * 128 + 128, pl.ds(k0, W2)], es[p]) for p in range(pairs)]
            for p in range(pairs):
                acc[p] += held[p]
            return tuple(news)

        totals = lax.fori_loop(0, count, outputs, tuple(jnp.zeros((8, 2 * T), F32) for _ in range(pairs)))
        stats = []
        for p in range(pairs):
            total = jnp.sum(totals[p], 0, keepdims=True)
            scaled = acc[p] * (1.0 / total)
            o = jnp.concatenate([scaled[:HEAD, :T], scaled[HEAD:, T:]], 0)
            out[pl.ds(pl.multiple_of(i * T, T), T), p * 128 : p * 128 + 128] = o.T.astype(BF16)
            stat = peaks[p] + jnp.log(total)
            stats += [stat[:, :T], stat[:, T:]]
        lse[i] = jnp.concatenate(stats + [jnp.zeros((4, T), F32)], 0)

    store.wait()


def attn_forward(ids, own_qkv, halo, gain, bias, w, b):
    rows, width = own_qkv.shape[0], own_qkv.shape[1] // 3
    tiles = ids.shape[0]
    pairs = width // 128
    anywhere = pl.BlockSpec(memory_space=pl.ANY)
    return pl.pallas_call(
        functools.partial(attn_forward_kernel, width),
        out_shape=(
            jax.ShapeDtypeStruct((rows, width), BF16),
            jax.ShapeDtypeStruct((rows // T, 16, T), F32),
            jax.ShapeDtypeStruct((2 * rows, 3 * width), BF16),
        ),
        in_specs=[SM, VM, anywhere] + [VM] * 5,
        out_specs=(VM, VM, anywhere),
        scratch_shapes=[
            pltpu.VMEM((2 * rows, 3 * width), BF16),
            pltpu.VMEM((pairs, tiles // 2, W2, 2 * T), F32),
            pltpu.VMEM((width, 2 * rows), BF16),
            pltpu.VMEM((pairs, 128, 2 * T), F32),
            pltpu.VMEM((2 * rows, T), F32),
            pltpu.SemaphoreType.DMA((2,)),
        ],
        compiler_params=pltpu.CompilerParams(vmem_limit_bytes=56 * 2**20),
        name="attention_forward",
    )(ids, ids, own_qkv, halo, gain, bias, w, b)


def attn_backward_kernel(width, carried, ids, id_row, qkv_far, do_far, stats, *refs):
    sources, (out, *targets) = refs[:carried], refs[carried : 2 * carried + 1]
    dq, dk, dv, qt, kt, gt, id_col, qkv, do, sems, carry_sems, *held = refs[2 * carried + 1 :]
    pairs = width // 128
    own = out.shape[0] // T
    off = lax.axis_index("hd") * own
    tiles = id_row.shape[0]
    def carry_in(n):
        return pltpu.make_async_copy(sources[n], held[n], carry_sems.at[0, n])

    def carry_out(n):
        return pltpu.make_async_copy(held[n], targets[n], carry_sems.at[1, n])

    def loads(j):
        rows = pl.ds(pl.multiple_of(j * T, T), T)
        return (
            pltpu.make_async_copy(qkv_far.at[rows, :], qkv.at[rows, :], sems.at[0, j]),
            pltpu.make_async_copy(do_far.at[rows, :], do.at[rows, :], sems.at[1, j]),
        )

    @pl.loop(0, tiles)
    def _(j):
        for load in loads(j):
            load.start()

    for n in range(carried):
        carry_in(n).start()
    id_columns(id_row, id_col)
    dq[...] = jnp.zeros_like(dq)

    @pl.loop(0, tiles)
    def _(j):
        for load in loads(j):
            load.wait()
        k0 = pl.multiple_of(j * T, T)
        rows = pl.ds(k0, T)
        qt[:, rows] = (qkv[rows, :width] * BF16(HEAD**-0.5)).T
        kt[:, rows] = qkv[rows, width : 2 * width].T
        gt[:, rows] = do[rows, :].T

    for n in range(carried):
        carry_in(n).wait()
        carry_out(n).start()

    @pl.loop(0, tiles // 2)
    def _(j):
        k0 = pl.multiple_of(j * W2, W2)
        mine = jnp.logical_and(2 * j >= off, 2 * j < off + own)
        low, high = tile_span(ids, 2 * j, 2 * j + 1)
        low = jnp.where(mine, low, jnp.maximum(low, off))
        high = jnp.where(mine, high, jnp.minimum(high, off + own))
        for p in range(pairs):
            dk[p] = jnp.zeros((W2, 128), F32)
            dv[p] = jnp.zeros((W2, 128), F32)

        @pl.loop(low, high)
        def _(i):
            q0 = pl.multiple_of(i * T, T)
            same = same_image(id_col, pl.ds(k0, W2), id_row, i)
            qs, gs, ss, ps, es, ds = [], [], [], [], [], []
            for p in range(pairs):
                cols = p * 128
                k = qkv[pl.ds(k0, W2), width + cols : width + cols + 128]
                v = qkv[pl.ds(k0, W2), 2 * width + cols : 2 * width + cols + 128]
                ss.append(mm(k, by_head_rows(qt[cols : cols + 128, pl.ds(q0, T)])))
                ps.append(mm(v, by_head_rows(gt[cols : cols + 128, pl.ds(q0, T)])))
            for p in range(pairs):
                one = jnp.concatenate([stats[i, 2 * p : 2 * p + 1, :], stats[i, 2 * p + 1 : 2 * p + 2, :]], 1)
                two = jnp.concatenate([stats[i, 2 * p + 16 : 2 * p + 17, :], stats[i, 2 * p + 17 : 2 * p + 18, :]], 1)
                e = jnp.exp(jnp.where(same, ss[p], -1e30) - one)
                es.append(e.astype(BF16))
                ds.append((e * (ps[p] - two)).astype(BF16))
            a, b, c = [], [], []
            for p in range(pairs):
                cols = p * 128
                a.append(mm(es[p], by_head(do[pl.ds(q0, T), cols : cols + 128])))
                b.append(mm(ds[p], by_head(qkv[pl.ds(q0, T), cols : cols + 128] * BF16(HEAD**-0.5))))
                c.append(mm(kt[cols : cols + 128, pl.ds(k0, W2)], ds[p]))
            for p in range(pairs):
                dv[p] += a[p]
                dk[p] += b[p]
                dq[p, i] += jnp.concatenate([c[p][:HEAD, :T], c[p][HEAD:, T:]], 0)

        @pl.when(mine)
        def _():
            r0 = pl.multiple_of(j * W2 - off * T, W2)
            for p in range(pairs):
                cols = p * 128
                out[pl.ds(r0, W2), width + cols : width + cols + 128] = dk[p].astype(BF16)
                out[pl.ds(r0, W2), 2 * width + cols : 2 * width + cols + 128] = dv[p].astype(BF16)

    @pl.loop(0, own)
    def _(i):
        for p in range(pairs):
            cols = p * 128
            out[pl.ds(pl.multiple_of(i * T, T), T), cols : cols + 128] = (dq[p, off + i] * HEAD**-0.5).T.astype(BF16)

    for n in range(carried):
        carry_out(n).wait()


def attn_backward(ids, qkv, do, stats, *arrays):
    all_rows, columns = qkv.shape
    own_rows = all_rows // 2
    width = columns // 3
    tiles = all_rows // T
    pairs = width // 128
    anywhere = pl.BlockSpec(memory_space=pl.ANY)
    return pl.pallas_call(
        functools.partial(attn_backward_kernel, width, len(arrays)),
        out_shape=[jax.ShapeDtypeStruct((own_rows, columns), BF16)] + [jax.ShapeDtypeStruct(v.shape, v.dtype) for v in arrays],
        in_specs=[SM, VM, anywhere, anywhere, VM] + [anywhere] * len(arrays),
        out_specs=[VM] + [anywhere] * len(arrays),
        scratch_shapes=[
            pltpu.VMEM((pairs, tiles, 128, T), F32),
            pltpu.VMEM((pairs, W2, 128), F32),
            pltpu.VMEM((pairs, W2, 128), F32),
            pltpu.VMEM((width, all_rows), BF16),
            pltpu.VMEM((width, all_rows), BF16),
            pltpu.VMEM((width, all_rows), BF16),
            pltpu.VMEM((all_rows, T), F32),
            pltpu.VMEM((all_rows, columns), BF16),
            pltpu.VMEM((all_rows, width), BF16),
            pltpu.SemaphoreType.DMA((2, tiles)),
            pltpu.SemaphoreType.DMA((2, max(len(arrays), 1))),
        ]
        + [pltpu.VMEM(v.shape, v.dtype) for v in arrays],
        compiler_params=pltpu.CompilerParams(vmem_limit_bytes=56 * 2**20),
        name="attention_backward",
    )(ids, ids, qkv, do, stats, *arrays)


ln_epsilon = 1e-06
drop_scale = 1.0 / 0.9


MESH = pl.DeviceIdType.MESH


class Place:
    def __init__(self):
        self.seq = lax.axis_index("seq")
        self.x = lax.axis_index("hd")
        self.c = lax.rem(self.seq, 2)
        self.y = lax.rem(self.seq // 2, 2)
        self.z = self.seq // 4

    def partner(self, axis):
        if axis == "c":
            return (self.seq + 1 - 2 * self.c, self.x)
        if axis == "y":
            return (self.seq + 2 - 4 * self.y, self.x)
        return (self.seq, 1 - self.x)

    def level(self, step):
        return (lax.rem(self.z + step, 4) * 4 + lax.rem(self.seq, 4), self.x)

    def index(self, axis):
        return {"x": self.x, "y": self.y, "c": self.c}[axis]


def greet(place):
    barrier = pltpu.get_barrier_semaphore()
    for other in [place.partner(a) for a in "cxy"] + [place.level(d) for d in (1, 2, 3)]:
        pl.semaphore_signal(barrier, inc=1, device_id=other, device_id_type=MESH)


def meet():
    pl.semaphore_wait(pltpu.get_barrier_semaphore(), 6)


def send(source, target, send_sem, recv_sem, other):
    copy = pltpu.make_async_remote_copy(
        src_ref=source, dst_ref=target, send_sem=send_sem, recv_sem=recv_sem, device_id=other, device_id_type=MESH
    )
    copy.start()
    return copy


class Flow:
    def __init__(self, place, axes, g, r0, r1, r2, r3, sems, recvs):
        self.place, self.axes, self.g = place, axes, g
        self.r0, self.r1, self.r2, self.r3 = r0, r1, r2, r3
        self.sems, self.recvs = sems, recvs
        self.copies = []

    def start(self):
        p = self.place
        self.copies.append(send(self.g.at[1 - p.c], self.r0, self.sems.at[0], self.recvs.at[0], p.partner("c")))

    def first(self):
        p = self.place
        self.copies[0].wait_recv()
        me = p.index(self.axes[0])

        def add(half):
            @pl.loop(0, 8)
            def _(i):
                b, z = i // 4, lax.rem(i, 4)
                self.r0[half, b, z] = self.r0[half, b, z] + self.g[p.c, half, b, z]

        add(1 - me)
        self.copies.append(
            send(self.r0.at[1 - me], self.r1, self.sems.at[1], self.recvs.at[1], p.partner(self.axes[0]))
        )
        add(me)

    def second(self):
        p = self.place
        self.copies[1].wait_recv()
        me, before = p.index(self.axes[1]), p.index(self.axes[0])

        def add(half):
            @pl.loop(0, 4)
            def _(z):
                self.r1[half, z] = self.r1[half, z] + self.r0[before, half, z]

        add(1 - me)
        self.copies.append(
            send(self.r1.at[1 - me], self.r2, self.sems.at[2], self.recvs.at[2], p.partner(self.axes[1]))
        )
        add(me)

    def third(self):
        p = self.place
        self.copies[2].wait_recv()
        before = p.index(self.axes[1])

        @pl.loop(0, 4)
        def _(z):
            self.r2[z] = self.r2[z] + self.r1[before, z]

        for d in (1, 2, 3):
            target = lax.rem(p.z + d, 4)
            self.copies.append(
                send(self.r2.at[target], self.r3.at[d - 1], self.sems.at[2 + d], self.recvs.at[2 + d], p.level(d))
            )

    def last(self):
        p = self.place
        total = self.r2[p.z].astype(F32)
        for d in (1, 2, 3):
            self.copies[2 + d].wait_recv()
            total = total + self.r3[d - 1].astype(F32)
        return total

    def finish(self):
        for copy in self.copies:
            copy.wait_send()


def flow_scratch(rows, cols, kind=BF16):
    return [
        pltpu.VMEM((2, 2, 4, rows, cols), kind),
        pltpu.VMEM((2, 4, rows, cols), kind),
        pltpu.VMEM((4, rows, cols), kind),
        pltpu.VMEM((3, rows, cols), kind),
        pltpu.SemaphoreType.DMA((6,)),
        pltpu.SemaphoreType.DMA((6,)),
    ]


class ChunkFlow(Flow):
    def __init__(self, place, axes, home, *refs):
        super().__init__(place, axes, *refs)
        self.home = home

    def third(self):
        p = self.place
        self.copies[2].wait_recv()
        self.r2[...] = self.r2[...] + self.r1[p.index(self.axes[1])]
        slot = lax.rem(p.z - self.home + 3, 4)
        self.hop = pltpu.make_async_remote_copy(
            src_ref=self.r2,
            dst_ref=self.r3.at[slot],
            send_sem=self.sems.at[3],
            recv_sem=self.recvs.at[3 + slot],
            device_id=(self.home * 4 + lax.rem(p.seq, 4), p.x),
            device_id_type=MESH,
        )

        @pl.when(p.z != self.home)
        def _():
            self.hop.start()

    def first(self):
        p = self.place
        self.copies[0].wait_recv()
        me = p.index(self.axes[0])

        def add(half):
            for b in range(2):
                self.r0[half, b] = self.r0[half, b] + self.g[p.c, half, b]

        add(1 - me)
        self.copies.append(
            send(self.r0.at[1 - me], self.r1, self.sems.at[1], self.recvs.at[1], p.partner(self.axes[0]))
        )
        add(me)

    def second(self):
        p = self.place
        self.copies[1].wait_recv()
        me, before = p.index(self.axes[1]), p.index(self.axes[0])
        self.r1[1 - me] = self.r1[1 - me] + self.r0[before, 1 - me]
        self.copies.append(
            send(self.r1.at[1 - me], self.r2, self.sems.at[2], self.recvs.at[2], p.partner(self.axes[1]))
        )
        self.r1[me] = self.r1[me] + self.r0[before, me]

    def last_into(self, out):
        p = self.place

        @pl.when(p.z == self.home)
        def _():
            total = self.r2[...].astype(F32)
            for slot in range(3):
                pltpu.make_async_remote_copy(
                    src_ref=self.r2,
                    dst_ref=self.r3.at[slot],
                    send_sem=self.sems.at[3],
                    recv_sem=self.recvs.at[3 + slot],
                    device_id=p.level(1),
                    device_id_type=MESH,
                ).wait_recv()
                total = total + self.r3[slot].astype(F32)
            out[...] = total

    def finish(self):
        super().finish()

        @pl.when(self.place.z != self.home)
        def _():
            self.hop.wait_send()


class LevelFlow(Flow):
    axes = "zxy"

    def __init__(self, place, g, r0, r1, r2, r3, sems, recvs):
        super().__init__(place, "zxy", g, r0, r1, r2, r3, sems, recvs)

    def first(self):
        p = self.place
        self.copies[0].wait_recv()

        @pl.loop(0, 4)
        def _(z):
            for x in range(2):
                for y in range(2):
                    self.r0[z, x, y] = self.r0[z, x, y] + self.g[p.c, z, x, y]

        for d in (1, 2, 3):
            self.copies.append(
                send(self.r0.at[lax.rem(p.z + d, 4)], self.r1.at[d - 1], self.sems.at[d], self.recvs.at[d], p.level(d))
            )

    def second(self):
        p = self.place
        for d in (1, 2, 3):
            self.copies[d].wait_recv()
        for x in range(2):
            for y in range(2):
                total = self.r0[p.z, x, y].astype(F32)
                for d in range(3):
                    total = total + self.r1[d, x, y].astype(F32)
                self.r1[0, x, y] = total.astype(BF16)
        self.copies.append(
            send(self.r1.at[0, 1 - p.x], self.r2, self.sems.at[4], self.recvs.at[4], p.partner("x"))
        )

    def third(self):
        p = self.place
        self.copies[4].wait_recv()
        for y in range(2):
            self.r2[y] = self.r2[y] + self.r1[0, p.x, y]
        self.copies.append(send(self.r2.at[1 - p.y], self.r3, self.sems.at[5], self.recvs.at[5], p.partner("y")))

    def last(self):
        self.copies[5].wait_recv()
        return self.r2[self.place.y].astype(F32) + self.r3[...].astype(F32)


def level_scratch(rows, cols):
    return [
        pltpu.VMEM((4, 2, 2, rows, cols), BF16),
        pltpu.VMEM((3, 2, 2, rows, cols), BF16),
        pltpu.VMEM((2, rows, cols), BF16),
        pltpu.VMEM((rows, cols), BF16),
        pltpu.SemaphoreType.DMA((6,)),
        pltpu.SemaphoreType.DMA((6,)),
    ]


def chunk_scratch(rows, cols):
    return [
        pltpu.VMEM((2, 2, rows, cols), BF16),
        pltpu.VMEM((2, rows, cols), BF16),
        pltpu.VMEM((rows, cols), BF16),
        pltpu.VMEM((3, rows, cols), BF16),
        pltpu.SemaphoreType.DMA((6,)),
        pltpu.SemaphoreType.DMA((6,)),
    ]


def row_norm(x):
    mean = jnp.mean(x, -1, keepdims=True)
    center = x - mean
    rstd = lax.rsqrt(jnp.mean(center * center, -1, keepdims=True) + ln_epsilon)
    return center * rstd, rstd


def norm_back(hat, rstd, gain, grad):
    scaled = grad * gain
    return rstd * (scaled - jnp.mean(scaled, -1, keepdims=True) - hat * jnp.mean(scaled * hat, -1, keepdims=True))


def col_sum(x):
    return jnp.sum(x, 0, keepdims=True)


def put_blocks(product, z, axes, g):
    half = product.shape[1] // 2
    for y in range(2):
        for c in range(2):
            for x in range(2):
                r = ((y * 2 + c) * 2 + x) * 24
                block = jnp.concatenate([product[r : r + 24, :half], product[r : r + 24, half:]], 0)
                at = {"x": x, "y": y}
                if axes == "zxy":
                    g[c, z, x, y] = block.astype(BF16)
                else:
                    g[c, at[axes[0]], at[axes[1]], z] = block.astype(BF16)


def put_chunk(product, y, axes, g):
    for c in range(2):
        for x in range(2):
            r = (c * 2 + x) * 96
            at = {"x": x, "y": y}
            g[c, at[axes[0]], at[axes[1]]] = product[r : r + 96].astype(BF16)


R = 256
HALO = 608
FLOW_REFS = 6
ORDER = (0, 3, 1, 2)
PATHS1 = ("xy", "xy", "zxy", "xy")
PATHS2 = ("yx", "yx", "yx", "yx")


def mlp_kernel(reduce, chunks, *refs):
    o, lse, x, keep, cot, w_out, b_out, gain, bias, w1, b1, w2, b2 = refs[:13]
    mixed_far, dx1_far, do, stats, small, g_far, out1, out2 = refs[13:21]
    v1, v2, x1s, n2s, n2t, dms, gs, dus, das, macc, nacc, load1, load2, halo_sems = refs[21:35]
    mixed, dx1, g_out, near_sems = refs[35:39]
    flow_refs = refs[39:]
    stores = [
        pltpu.make_async_copy(near, far, near_sems.at[n])
        for n, (near, far) in enumerate(((mixed, mixed_far), (dx1, dx1_far), (g_out, g_far)))
    ]
    side = lax.axis_index("hd")
    base = pl.multiple_of(side * o.shape[0], o.shape[0])
    owner = lax.broadcasted_iota(jnp.int32, (16, o.shape[1]), 1) // HEAD
    heads = (owner == lax.broadcasted_iota(jnp.int32, (16, o.shape[1]), 0)).astype(BF16)
    rows, width = o.shape
    tiles = rows // R
    loads = []
    for k in range(chunks):
        cols = pl.ds(k * width, width)
        loads.append(
            (
                pltpu.make_async_copy(w1.at[:, cols], v1.at[k], load1.at[k]),
                pltpu.make_async_copy(w2.at[cols, :], v2.at[k], load2.at[k]),
            )
        )
        loads[k][0].start()
        loads[k][1].start()
    if reduce:
        place = Place()
        greet(place)
        per = 1 + FLOW_REFS
        flows1 = []
        for k in range(chunks):
            mine = flow_refs[2 * per * k : 2 * per * k + per]
            flows1.append(LevelFlow(place, *mine) if PATHS1[k] == "zxy" else Flow(place, PATHS1[k], *mine))
        flows2 = [ChunkFlow(place, PATHS2[k], k, *flow_refs[2 * per * k + per : 2 * per * (k + 1)]) for k in range(chunks)]

    small[...] = jnp.zeros_like(small)

    @pl.loop(0, tiles)
    def _(t):
        r = pl.ds(pl.multiple_of(t * R, R), R)
        x1 = x[r, :].astype(F32) + keep[r, 0:1] * (mm(o[r, :], w_out[...]) + b_out[...])
        x1s[r, :] = x1
        hat, _ = row_norm(x1)
        n2 = (hat * gain[...] + bias[...]).astype(BF16)
        n2s[r, :] = n2
        dm = (cot[r, :].astype(F32) * keep[r, 1:2]).astype(BF16)
        dms[r, :] = dm
        small[7:8, :] += col_sum(dm.astype(F32))

    n2t[...] = n2s[...].T

    def row_tile(k, t, first, slot):
        r = slice(t * R, t * R + R)
        u = mm(n2s[r, :], v1[k]) + b1[k * width : k * width + width]
        dg = mm_nt(dms[r, :], v2[k])
        cdf = 0.5 + 0.5 * lax.erf(u * 0.7071067811865476)
        pdf = jnp.exp(u * u * -0.5) * 0.3989422804014327
        g = (u * cdf).astype(BF16)
        du = (dg * (cdf + u * pdf)).astype(BF16)
        gs[slot, r, :] = g
        dus[slot, r, :] = du
        small[3 + k : 4 + k, :] += col_sum(du.astype(F32))
        if first:
            macc[r, :] = mm(g, v2[k])
            nacc[r, :] = mm_nt(du, v1[k])
        else:
            macc[r, :] += mm(g, v2[k])
            nacc[r, :] += mm_nt(du, v1[k])

    steps = {}
    if reduce:
        for at, k in enumerate(ORDER[:3]):
            for flow, late in ((flows2[k], 0), (flows1[k], 1)):
                steps.setdefault((at + 1, 1 + late), []).append(flow.first)
                if at < 2:
                    steps.setdefault((at + 2, 1 + late), []).append(flow.second)
                    steps.setdefault((2, 5) if at == 0 else (4, 1 + late), []).append(flow.third)

    def point(*at):
        for step in steps.pop(at, []):
            step()

    def gradient2(k, slot):
        @pl.loop(0, 2)
        def _(y):
            product = mm_tn(gs[slot, :, pl.ds(pl.multiple_of(y * 384, 384), 384)], dms[...])
            put_chunk(product, y, flows2[k].axes, flows2[k].g)

        flows2[k].start()

    def gradient1(k, slot):
        @pl.loop(0, 2)
        def _(h):
            product = mm(n2t[pl.ds(pl.multiple_of(h * 384, 128), 384), :], dus[slot])
            for z in range(2):
                put_blocks(product[z * 192 : z * 192 + 192], 2 * h + z, flows1[k].axes, flows1[k].g)

        flows1[k].start()

    for at, k in enumerate(ORDER if reduce else range(chunks)):
        slot = at % 2
        loads[k][0].wait()
        loads[k][1].wait()
        for t in range(tiles):
            row_tile(k, t, at == 0, slot)
            point(at, t + 1)
        if reduce and at == 0:
            meet()
        if reduce and at < 3:
            gradient2(k, slot)
            point(at, 4)
            gradient1(k, slot)
            point(at, 5)
        if not reduce:

            @pl.loop(0, 3)
            def _(t):
                r = pl.ds(pl.multiple_of(t * 256, 256), 256)
                out2[pl.ds(pl.multiple_of(k * width + t * 256, 256), 256), :] = mm_tn(gs[slot, :, r], dms[...]).astype(BF16)
                out1[r, k * width : k * width + width] = mm(n2t[r, :], dus[slot]).astype(BF16)

    apart = rows - HALO
    pad = pl.multiple_of((1 - side) * (2 * rows - apart), 16)
    do[pl.ds(pad, apart), :] = jnp.zeros((apart, width), BF16)
    stat_tiles = pl.cdiv(HALO, T)
    spare = rows // T - stat_tiles
    for s in range(spare):
        stats[(1 - side) * (2 * rows // T - spare) + s] = jnp.zeros((32, T), F32)
    exchange = []

    def exchange_rows(ref, first, count, n):
        part = ref.at[pl.ds(first, count)]
        exchange.append(send(part, part, halo_sems.at[2 * n], halo_sems.at[2 * n + 1], place.partner("x")))

    for t in range(tiles):
        at = lax.rem(t + 1 - side, tiles)
        r = pl.ds(pl.multiple_of(at * R, R), R)
        hat, rstd = row_norm(x1s[r, :])
        dn2 = nacc[r, :]
        dx = cot[r, :].astype(F32) + norm_back(hat, rstd, gain[...], dn2)
        dx1[r, :] = dx
        da = (dx * keep[r, 0:1]).astype(BF16)
        das[r, :] = da
        grad_o = mm_nt(da, w_out[...]).astype(BF16)
        do[pl.ds(pl.multiple_of(base + at * R, R), R), :] = grad_o
        small[0:1, :] += col_sum(da.astype(F32))
        small[1:2, :] += col_sum(dn2 * hat)
        small[2:3, :] += col_sum(dn2)
        prod = grad_o.astype(F32) * o[r, :].astype(F32)
        high = prod.astype(BF16)
        low = (prod - high.astype(F32)).astype(BF16)
        sums = mm_nt(heads, high) + mm_nt(heads, low)
        for s in range(R // T):
            own = at * (R // T) + s
            stats[side * (rows // T) + own, :16] = lse[own]
            stats[side * (rows // T) + own, 16:] = sums[:, s * T : s * T + T]
        point(chunks, t + 1)
        if reduce and t == 0:
            exchange_rows(do, pl.multiple_of(base + at * R, R), R, 0)

    if reduce:
        third, fourth = ORDER[2], ORDER[3]
        exchange_rows(stats, spare + side * stat_tiles, stat_tiles, 3)
        gradient2(fourth, 1)
        gradient1(fourth, 1)

    stores[1].start()
    n2t[...] = o[...].T
    if reduce:

        @pl.loop(0, 2)
        def _(h):
            product = mm(n2t[pl.ds(pl.multiple_of(h * 384, 128), 384), :], das[...])
            for z in range(2):
                put_blocks(product[z * 192 : z * 192 + 192], 2 * h + z, "zxy", g_out)

        flows2[fourth].first()
        flows1[fourth].first()
        flows2[third].second()
        flows1[third].second()
    else:

        @pl.loop(0, 3)
        def _(t):
            r = pl.ds(pl.multiple_of(t * 256, 256), 256)
            g_out[r, :] = mm(n2t[r, :], das[...]).astype(BF16)

    @pl.loop(0, tiles)
    def _(t):
        r = pl.ds(pl.multiple_of(t * R, R), R)
        mixed[r, :] = (x1s[r, :] + keep[r, 1:2] * (macc[r, :] + b2[...])).astype(BF16)

    stores[0].start()
    stores[2].start()

    if reduce:
        half = width // 2

        def keep_share(k):
            total = flows1[k].last()
            out1[:, k * width : k * width + half] = total[:24]
            out1[:, k * width + half : (k + 1) * width] = total[24:]
            flows2[k].last_into(out2)

        for at in sorted(steps):
            point(*at)
        second_tile = 2 - side
        exchange_rows(do, pl.multiple_of(base + second_tile * R, R), R, 1)
        flows2[third].third()
        flows1[third].third()
        flows2[fourth].second()
        exchange_rows(do, pl.multiple_of(base + (1 - side) * apart + side * 2 * R, 16), HALO - 2 * R, 2)
        flows1[fourth].second()
        flows2[fourth].third()
        flows1[fourth].third()
        for k in range(chunks):
            keep_share(k)
        for k in range(chunks):
            flows1[k].finish()
            flows2[k].finish()
        for copy in exchange:
            copy.wait()
    for store in stores:
        store.wait()


def mlp_step(reduce, o, lse, x, keep, cot, w_out, b_out, gain, bias, w1, b1, w2, b2):
    rows, width = o.shape
    chunks = w1.shape[1] // width
    block = lambda dims, kind: jax.ShapeDtypeStruct(dims, kind)
    outs = [
        block((rows, width), BF16),
        block((rows, width), F32),
        block((2 * rows, width), BF16),
        block((2 * rows // T, 32, T), F32),
        block((16, width), F32),
    ]
    if reduce:
        outs += [block((2, 4, 2, 2, 48, width // 2), BF16), block((24, chunks * width), F32), block((96, width), F32)]
    else:
        outs += [block((width, width), BF16), block(w1.shape, BF16), block(w2.shape, BF16)]
    scratch = [
        pltpu.VMEM((chunks, width, width), BF16),
        pltpu.VMEM((chunks, width, width), BF16),
        pltpu.VMEM((rows, width), F32),
        pltpu.VMEM((rows, width), BF16),
        pltpu.VMEM((width, rows), BF16),
        pltpu.VMEM((rows, width), BF16),
        pltpu.VMEM((2, rows, width), BF16),
        pltpu.VMEM((2, rows, width), BF16),
        pltpu.VMEM((rows, width), BF16),
        pltpu.VMEM((rows, width), F32),
        pltpu.VMEM((rows, width), F32),
        pltpu.SemaphoreType.DMA((chunks,)),
        pltpu.SemaphoreType.DMA((chunks,)),
        pltpu.SemaphoreType.DMA((8,)),
        pltpu.VMEM((rows, width), BF16),
        pltpu.VMEM((rows, width), F32),
        pltpu.VMEM(outs[5].shape, BF16),
        pltpu.SemaphoreType.DMA((3,)),
    ]
    params = dict(vmem_limit_bytes=60 * 2**20)
    if reduce:
        for k in range(chunks):
            if PATHS1[k] == "zxy":
                scratch += [pltpu.VMEM((2, 4, 2, 2, 48, width // 2), BF16)] + level_scratch(48, width // 2)
            else:
                scratch += [pltpu.VMEM((2, 2, 2, 4, 48, width // 2), BF16)] + flow_scratch(48, width // 2)
            scratch += [pltpu.VMEM((2, 2, 2, 96, width), BF16)] + chunk_scratch(96, width)
        params.update(collective_id=1, has_side_effects=True)
    anywhere = pl.BlockSpec(memory_space=pl.ANY)
    return pl.pallas_call(
        functools.partial(mlp_kernel, reduce, chunks),
        out_shape=outs,
        in_specs=[VM] * 9 + [anywhere, VM, anywhere, VM],
        out_specs=[anywhere, anywhere, VM, VM, VM, anywhere, VM, VM],
        scratch_shapes=scratch,
        compiler_params=pltpu.CompilerParams(**params),
        name="mlp_step",
    )(o, lse, x, keep, cot, w_out, b_out, gain, bias, w1, b1, w2, b2)


SMALLS = ((8, 1), (9, 1), (10, 2), (0, 1), (1, 1), (2, 1), (3, 4), (7, 1))


def by_owner(sums):
    width = sums.shape[1]
    lane = lax.broadcasted_iota(jnp.int32, (32, width), 1)
    block = lax.broadcasted_iota(jnp.int32, (32, width), 0)
    source = lax.broadcasted_iota(jnp.int32, (width, 128), 0)
    target = lax.broadcasted_iota(jnp.int32, (width, 128), 1)
    parts = []
    for first, rows in SMALLS:
        size = rows * width // 32
        row = block // (32 // rows)
        spread = jnp.zeros((32, width), F32)
        for r in range(rows):
            spread = jnp.where(row == r, sums[first + r : first + r + 1, :], spread)
        spread = jnp.where(lane // size == lax.rem(block, 32 // rows), spread, 0.0)
        pick = (lax.rem(source, size) == target).astype(BF16)
        total = jnp.zeros((32, 128), F32)
        for _ in range(3):
            piece = spread.astype(BF16)
            total = total + mm(piece, pick)
            spread = spread - piece.astype(F32)
        parts.append(total.reshape(32, 1, 128))
    return jnp.concatenate(parts, 1)


def tail_kernel(reduce, *refs):
    dqkv, x, dx1_far, gain, bias, w_far, g_out, small_in = refs[:8]
    grad_far, grad_w, grad_o, small = refs[8:12]
    n1s, n1t, dx1, w, near_sems = refs[12:17]
    rest = refs[17:]
    load_w = pltpu.make_async_copy(w_far, w, near_sems.at[0])
    load_x = pltpu.make_async_copy(dx1_far, dx1, near_sems.at[1])
    load_w.start()
    load_x.start()
    rows, width = x.shape
    tiles = rows // R
    if reduce:
        place = Place()
        greet(place)
        out_flow = LevelFlow(place, g_out, *rest[:6])
        flows = [Flow(place, ("yx", "xy", "yx")[i], *rest[6 + 7 * i : 13 + 7 * i]) for i in range(3)]
        sums = Flow(place, "xy", *rest[27:34])

    @pl.loop(0, tiles)
    def _(t):
        r = pl.ds(pl.multiple_of(t * R, R), R)
        hat, _ = row_norm(x[r, :].astype(F32))
        n1s[r, :] = (hat * gain[...] + bias[...]).astype(BF16)

    n1t[...] = n1s[...].T
    if reduce:
        meet()
        out_flow.start()
        for i in range(3):

            @pl.loop(0, 2)
            def _(h):
                product = mm(n1t[pl.ds(pl.multiple_of(h * 384, 128), 384), :], dqkv[:, i * width : (i + 1) * width])
                for z in range(2):
                    put_blocks(product[z * 192 : z * 192 + 192], 2 * h + z, flows[i].axes, flows[i].g)

            flows[i].start()
            if i == 0:
                out_flow.first()
            else:
                flows[i - 1].first()
    else:

        @pl.loop(0, 3)
        def _(t):
            r = pl.ds(pl.multiple_of(t * 256, 256), 256)
            for i in range(3):
                grad_w[r, i * width : (i + 1) * width] = mm(n1t[r, :], dqkv[:, i * width : (i + 1) * width]).astype(BF16)

    small_ref = rest[34] if reduce else small
    small_ref[...] = small_in[...]

    def rows_back(t):
        r = pl.ds(pl.multiple_of(t * R, R), R)
        hat, rstd = row_norm(x[r, :].astype(F32))
        dn1 = mm_nt(dqkv[r, :], w[...])
        dx1[r, :] = dx1[r, :] + norm_back(hat, rstd, gain[...], dn1)
        small_ref[8:9, :] += col_sum(dn1 * hat)
        small_ref[9:10, :] += col_sum(dn1)
        small_ref[10:11, :] += col_sum(dqkv[r, :width].astype(F32))
        small_ref[11:12, :] += col_sum(dqkv[r, 2 * width :].astype(F32))

    load_w.wait()
    load_x.wait()
    pl.loop(0, tiles)(rows_back)
    store_x = pltpu.make_async_copy(dx1, grad_far, near_sems.at[2])
    store_x.start()
    if reduce:
        half = width // 2
        shares = by_owner(small_ref[...])
        for b in range(32):
            sums.g[b // 2 % 2, b % 2, b // 4 % 2, b // 8] = shares[b]
        sums.start()
        flows[0].second()
        flows[2].first()
        sums.first()
        flows[1].second()
        out_flow.second()
        sums.second()
        flows[0].third()
        out_flow.third()
        flows[1].third()
        sums.third()
        flows[2].second()
        flows[2].third()
        total = out_flow.last()
        grad_o[:, :half] = total[:24]
        grad_o[:, half:] = total[24:]
        small[...] = sums.last()
        for i in range(3):
            total = flows[i].last()
            grad_w[:, i * width : i * width + half] = total[:24]
            grad_w[:, i * width + half : (i + 1) * width] = total[24:]
        for flow in (out_flow, *flows, sums):
            flow.finish()
    store_x.wait()


def tail_step(reduce, dqkv, x, dx1, gain, bias, w, g_out, small):
    rows, width = x.shape
    block = lambda dims, kind: jax.ShapeDtypeStruct(dims, kind)
    outs = [block((rows, width), F32)]
    scratch = [
        pltpu.VMEM((rows, width), BF16),
        pltpu.VMEM((width, rows), BF16),
        pltpu.VMEM((rows, width), F32),
        pltpu.VMEM(w.shape, BF16),
        pltpu.SemaphoreType.DMA((3,)),
    ]
    anywhere = pl.BlockSpec(memory_space=pl.ANY)
    params = dict(vmem_limit_bytes=60 * 2**20)
    args = [dqkv, x, dx1, gain, bias, w, g_out, small]
    if reduce:
        outs += [block((24, 3 * width), F32), block((24, width), F32), block((8, 128), F32)]
        scratch += level_scratch(48, width // 2)
        for _ in range(3):
            scratch += [pltpu.VMEM((2, 2, 2, 4, 48, width // 2), BF16)] + flow_scratch(48, width // 2)
        scratch += [pltpu.VMEM((2, 2, 2, 4, 8, 128), F32)] + flow_scratch(8, 128, F32)
        scratch += [pltpu.VMEM((16, width), F32)]
        params.update(collective_id=2, has_side_effects=True)
    else:
        outs += [block(w.shape, BF16), block((8, 128), F32), block((16, width), F32)]
    return pl.pallas_call(
        functools.partial(tail_kernel, reduce),
        out_shape=outs,
        in_specs=[VM, VM, anywhere, VM, VM, anywhere, VM, VM],
        out_specs=[anywhere, VM, VM, VM],
        scratch_shapes=scratch,
        compiler_params=pltpu.CompilerParams(**params),
        name="tail_step",
    )(*args)


def project_kernel(x, gain, bias, w, b, out):
    @pl.loop(0, x.shape[0] // T)
    def _(t):
        r = pl.ds(pl.multiple_of(t * T, T), T)
        hat, _ = row_norm(x[r, :].astype(F32))
        n1 = (hat * gain[...] + bias[...]).astype(BF16)
        out[r, :] = (mm(n1, w[...]) + b[...]).astype(BF16)


def project(x, gain, bias, w, b):
    return pl.pallas_call(
        project_kernel,
        out_shape=jax.ShapeDtypeStruct((x.shape[0], w.shape[1]), BF16),
        in_specs=[VM] * 5,
        out_specs=VM,
        compiler_params=pltpu.CompilerParams(vmem_limit_bytes=32 * 2**20),
        cost_estimate=pl.CostEstimate(flops=2 * x.shape[0] * w.shape[0] * w.shape[1], bytes_accessed=9 * 2**20, transcendentals=0),
        name="project",
    )(x, gain, bias, w, b)


def finish_kernel(small, far, *refs):
    near, sems = refs[-2:]
    copied = (len(refs) - 3 - len(SMALLS)) // 2
    loads, stores = [], []
    for n in range(4):
        rows = pl.ds(n * (near.shape[0] // 4), near.shape[0] // 4)
        loads.append(pltpu.make_async_copy(far.at[rows, :], near.at[rows, :], sems.at[0, n]))
        stores.append(pltpu.make_async_copy(near.at[rows, :], refs[copied].at[rows, :], sems.at[1, n]))
        loads[n].start()
    for source, target in zip(refs[:copied], refs[copied + 1 : 2 * copied + 1]):
        target[...] = source[...]
    for row, out in enumerate(refs[2 * copied + 1 : -2]):
        out[...] = small[row, : out.shape[0]]
    for load, store in zip(loads, stores):
        load.wait()
        store.start()
    for store in stores:
        store.wait()


def finish(shards, small, large, *arrays):
    width = large.shape[1]
    anywhere = pl.BlockSpec(memory_space=pl.ANY)
    outs = [jax.ShapeDtypeStruct(a.shape, a.dtype) for a in (large, *arrays)]
    outs += [jax.ShapeDtypeStruct((rows * width // shards,), F32) for _, rows in SMALLS]
    return pl.pallas_call(
        finish_kernel,
        out_shape=outs,
        in_specs=[VM, anywhere] + [VM] * len(arrays),
        out_specs=[anywhere] + [VM] * (len(outs) - 1),
        scratch_shapes=[pltpu.VMEM(large.shape, large.dtype), pltpu.SemaphoreType.DMA((2, 4))],
        name="finish",
    )(small, large, *arrays)


def halo_of(rows, halo, side):
    mine = jnp.where(side == 0, rows[rows.shape[0] - halo :], rows[:halo])
    return lax.ppermute(mine, "hd", [(0, 1), (1, 0)])


def in_pack_order(own, halo, side, before=0, after=0):
    dims = (own.shape[0] - halo.shape[0], *own.shape[1:])
    late, early = jnp.full(dims, after, own.dtype), jnp.full(dims, before, own.dtype)
    return jnp.where(side == 0, jnp.concatenate([own, halo, late], 0), jnp.concatenate([early, halo, own], 0))


def per_device(tokens, image_ids, keep_masks, ln1_gain, ln1_bias, w_qkv, qv_bias, w_out, b_out,
               ln2_gain, ln2_bias, w_fc1, b_fc1, w_fc2, b_fc2, cotangent):
    rows, width = tokens.shape
    halo = HALO
    both = ("seq", "hd")
    side = lax.axis_index("hd")
    reduce = lax.axis_size("seq") == 16 and lax.axis_size("hd") == 2
    halo_tiles = pl.cdiv(halo, T)
    tok_halo = halo_of(tokens, halo, side)
    id_halo = halo_of(image_ids, halo, side)
    id_all = in_pack_order(image_ids, id_halo, side, -1, 1 << 20)
    ids = id_all.reshape(-1, T)
    one_hot = (image_ids[:, None] == jnp.arange(keep_masks.shape[1], dtype=jnp.int32)[None, :]).astype(F32)
    keep_rows = jnp.dot(one_hot, keep_masks[0].astype(F32)) * drop_scale
    bias_all = jnp.concatenate([qv_bias[:width], jnp.zeros((width,), F32), qv_bias[width:]])

    norm1 = (ln1_gain, ln1_bias, w_qkv, bias_all)
    qkv_own = project(tokens, *norm1)
    heads_out, lse, qkv_all = attn_forward(ids, qkv_own, tok_halo, *norm1)
    mixed, dx1, do_all, stats_all, small, g_out, grad_fc1, grad_fc2 = mlp_step(
        reduce, heads_out, lse, tokens, keep_rows, cotangent, w_out, b_out, ln2_gain, ln2_bias,
        w_fc1, b_fc1, w_fc2, b_fc2)
    if not reduce:
        first = side * rows
        do_own = lax.dynamic_slice_in_dim(do_all, first, rows, 0)
        stats_own = lax.dynamic_slice_in_dim(stats_all, first // T, rows // T, 0)
        do_all = in_pack_order(do_own, halo_of(do_own, halo, side), side)
        stats_all = in_pack_order(stats_own, halo_of(stats_own, halo_tiles, side), side)
    dqkv, *carried = attn_backward(ids, qkv_all, do_all, stats_all, *((mixed, grad_fc1, grad_fc2) if reduce else ()))
    if reduce:
        mixed, grad_fc1, grad_fc2 = carried
    grad_x, grad_qkv, grad_out, small = tail_step(
        reduce, dqkv, tokens, dx1, ln1_gain, ln1_bias, w_qkv, g_out, small)
    if not reduce:
        grad_out = g_out

        def scatter(v):
            return lax.psum_scatter(v, both, scatter_dimension=0, tiled=True).astype(F32)

        grad_fc1, grad_fc2, grad_qkv, grad_out = map(scatter, (grad_fc1, grad_fc2, grad_qkv, grad_out))
        small = lax.psum(small, both)
    shards = lax.axis_size("seq") * lax.axis_size("hd")
    if reduce:
        grad_x, grad_qkv, grad_out, *vectors = finish(shards, small, grad_x, grad_qkv, grad_out)
    else:
        place = lax.axis_index("seq") * lax.axis_size("hd") + side
        vectors = []
        for first, count in SMALLS:
            size = count * width // shards
            vectors.append(lax.dynamic_slice(small[first : first + count].reshape(-1), (place * size,), (size,)))
    g1, b1, qv, bo, g2, b2, bf1, bf2 = vectors
    return mixed, grad_x, g1, b1, grad_qkv, qv, grad_out, bo, g2, b2, grad_fc1, bf1, grad_fc2, bf2


def solution(mesh):
    both = P(("seq", "hd"))
    split = P(("seq", "hd"), None)
    return jax.shard_map(
        per_device,
        mesh=mesh,
        in_specs=(split, both, P("seq", None, None)) + (P(),) * 12 + (split,),
        out_specs=(split, split, both, both, split, both, split, both, both, both, split, both, split, both),
        check_vma=False,
    )
```

```python
import functools
import jax, jax.numpy as jnp
from jax import lax
from jax.experimental import pallas as pl
from jax.experimental.pallas import tpu as pltpu
from jax.sharding import PartitionSpec as P

HEADS, HEAD = 12, 64
T = 128
W2 = 256
VM = pl.BlockSpec(memory_space=pltpu.VMEM)
SM = pl.BlockSpec(memory_space=pltpu.SMEM)
F32, BF16 = jnp.float32, jnp.bfloat16
NT = (((1,), (1,)), ((), ()))
TN = (((0,), (0,)), ((), ()))


def mm(a, b):
    return jnp.dot(a, b, preferred_element_type=F32)


def mm_nt(a, b):
    return lax.dot_general(a, b, NT, preferred_element_type=F32)


def mm_tn(a, b):
    return lax.dot_general(a, b, TN, preferred_element_type=F32)


def by_head(pair):
    lane = lax.broadcasted_iota(jnp.int32, pair.shape, 1)
    zero = jnp.zeros_like(pair)
    return jnp.concatenate(
        [jnp.where(lane < HEAD, pair, zero), jnp.where(lane < HEAD, zero, pair)], 0
    )


def by_head_rows(pair):
    row = lax.broadcasted_iota(jnp.int32, pair.shape, 0)
    zero = jnp.zeros_like(pair)
    return jnp.concatenate([jnp.where(row < HEAD, pair, zero), jnp.where(row < HEAD, zero, pair)], 1)


def tile_span(ids, first_tile, last_tile):
    low, high = 0, 0
    for u in range(ids.shape[0]):
        low += (ids[u, T - 1] < ids[first_tile, 0]).astype(jnp.int32)
        high += (ids[u, 0] <= ids[last_tile, T - 1]).astype(jnp.int32)
    return low, high


def id_columns(id_row, id_col):
    @pl.loop(0, id_row.shape[0])
    def _(j):
        line = jnp.broadcast_to(id_row[pl.ds(j, 1), :].astype(F32), (T, T))
        id_col[pl.ds(pl.multiple_of(j * T, T), T), :] = line.T


def same_image(id_col, rows, id_row, tile):
    left = id_col[rows, :]
    right = id_row[pl.ds(tile, 1), :].astype(F32)
    return jnp.concatenate([left, left], 1) == jnp.concatenate([right, right], 1)


HALO_ROWS = 304


def attn_forward_kernel(width, ids, id_row, own_qkv, halo, gain, bias, w, b, out, lse, all_qkv, qkv, sc, vt, acc, id_col, sems):
    pairs = width // 128
    rows, tiles = out.shape[0], id_row.shape[0]
    own = rows // T
    side = lax.axis_index("hd")
    off = side * own
    apart = rows - halo.shape[0]
    fetch = pltpu.make_async_copy(own_qkv, qkv.at[pl.ds(pl.multiple_of(side * rows, rows), rows), :], sems.at[0])
    fetch.start()
    id_columns(id_row, id_col)
    qkv[pl.ds(pl.multiple_of((1 - side) * (2 * rows - apart), 16), apart), :] = jnp.zeros((apart, 3 * width), BF16)

    @pl.loop(0, halo.shape[0] // HALO_ROWS)
    def _(t):
        r = pl.ds(pl.multiple_of(t * HALO_ROWS, 16), HALO_ROWS)
        hat, _ = row_norm(halo[r, :].astype(F32))
        n1 = (hat * gain[...] + bias[...]).astype(BF16)
        first = pl.multiple_of((1 - side) * rows + side * apart + t * HALO_ROWS, 16)
        qkv[pl.ds(first, HALO_ROWS), :] = (mm(n1, w[...]) + b[...]).astype(BF16)

    fetch.wait()
    store = pltpu.make_async_copy(qkv, all_qkv, sems.at[1])
    store.start()

    @pl.loop(0, tiles)
    def _(j):
        k0 = pl.multiple_of(j * T, T)
        vt[:, pl.ds(k0, T)] = qkv[pl.ds(k0, T), 2 * width :].T

    @pl.loop(0, own)
    def _(i):
        tile = off + i
        q0 = pl.multiple_of(tile * T, T)
        low, high = tile_span(ids, tile, tile)
        low = jnp.where(jnp.logical_and(lax.rem(high - low, 2) == 1, low > 0), low - 1, low)
        count = (high - low + 1) // 2
        turned = (qkv[pl.ds(q0, T), :width] * BF16(HEAD**-0.5)).T
        stacks = [by_head_rows(turned[p * 128 : p * 128 + 128]) for p in range(pairs)]

        def scores(j, peaks):
            k0 = pl.multiple_of((low + 2 * j) * T, T)
            same = same_image(id_col, pl.ds(k0, W2), id_row, tile)
            held = [mm(qkv[pl.ds(k0, W2), width + p * 128 : width + p * 128 + 128], stacks[p]) for p in range(pairs)]
            news = []
            for p, s in enumerate(held):
                s = jnp.where(same, s, -1e30)
                sc[p, j] = s
                news.append(jnp.maximum(peaks[p], jnp.max(s.reshape(W2 // 8, 8, 2 * T), 0)))
            return tuple(news)

        start = tuple(jnp.full((8, 2 * T), -jnp.inf, F32) for _ in range(pairs))
        peaks = lax.fori_loop(0, count, scores, start)
        peaks = [jnp.max(m, 0, keepdims=True) for m in peaks]
        for p in range(pairs):
            acc[p] = jnp.zeros((128, 2 * T), F32)

        def outputs(j, totals):
            k0 = pl.multiple_of((low + 2 * j) * T, T)
            es, news = [], []
            for p in range(pairs):
                e = jnp.exp(sc[p, j] - peaks[p])
                news.append(totals[p] + jnp.sum(e.reshape(W2 // 8, 8, 2 * T), 0))
                es.append(e.astype(BF16))
            held = [mm(vt[p * 128 : p * 128 + 128, pl.ds(k0, W2)], es[p]) for p in range(pairs)]
            for p in range(pairs):
                acc[p] += held[p]
            return tuple(news)

        totals = lax.fori_loop(0, count, outputs, tuple(jnp.zeros((8, 2 * T), F32) for _ in range(pairs)))
        stats = []
        for p in range(pairs):
            total = jnp.sum(totals[p], 0, keepdims=True)
            scaled = acc[p] * (1.0 / total)
            o = jnp.concatenate([scaled[:HEAD, :T], scaled[HEAD:, T:]], 0)
            out[pl.ds(pl.multiple_of(i * T, T), T), p * 128 : p * 128 + 128] = o.T.astype(BF16)
            stat = peaks[p] + jnp.log(total)
            stats += [stat[:, :T], stat[:, T:]]
        lse[i] = jnp.concatenate(stats + [jnp.zeros((4, T), F32)], 0)

    store.wait()


def attn_forward(ids, own_qkv, halo, gain, bias, w, b):
    rows, width = own_qkv.shape[0], own_qkv.shape[1] // 3
    tiles = ids.shape[0]
    pairs = width // 128
    anywhere = pl.BlockSpec(memory_space=pl.ANY)
    return pl.pallas_call(
        functools.partial(attn_forward_kernel, width),
        out_shape=(
            jax.ShapeDtypeStruct((rows, width), BF16),
            jax.ShapeDtypeStruct((rows // T, 16, T), F32),
            jax.ShapeDtypeStruct((2 * rows, 3 * width), BF16),
        ),
        in_specs=[SM, VM, anywhere] + [VM] * 5,
        out_specs=(VM, VM, anywhere),
        scratch_shapes=[
            pltpu.VMEM((2 * rows, 3 * width), BF16),
            pltpu.VMEM((pairs, tiles // 2, W2, 2 * T), F32),
            pltpu.VMEM((width, 2 * rows), BF16),
            pltpu.VMEM((pairs, 128, 2 * T), F32),
            pltpu.VMEM((2 * rows, T), F32),
            pltpu.SemaphoreType.DMA((2,)),
        ],
        compiler_params=pltpu.CompilerParams(vmem_limit_bytes=56 * 2**20),
        name="attention_forward",
    )(ids, ids, own_qkv, halo, gain, bias, w, b)


def attn_backward_kernel(width, carried, ids, id_row, qkv_far, do_far, stats, *refs):
    sources, (out, *targets) = refs[:carried], refs[carried : 2 * carried + 1]
    dq, dk, dv, qt, kt, gt, id_col, qkv, do, sems, carry_sems, *held = refs[2 * carried + 1 :]
    pairs = width // 128
    own = out.shape[0] // T
    off = lax.axis_index("hd") * own
    tiles = id_row.shape[0]
    def carry_in(n):
        return pltpu.make_async_copy(sources[n], held[n], carry_sems.at[0, n])

    def carry_out(n):
        return pltpu.make_async_copy(held[n], targets[n], carry_sems.at[1, n])

    def loads(j):
        rows = pl.ds(pl.multiple_of(j * T, T), T)
        return (
            pltpu.make_async_copy(qkv_far.at[rows, :], qkv.at[rows, :], sems.at[0, j]),
            pltpu.make_async_copy(do_far.at[rows, :], do.at[rows, :], sems.at[1, j]),
        )

    @pl.loop(0, tiles)
    def _(j):
        for load in loads(j):
            load.start()

    for n in range(carried):
        carry_in(n).start()
    id_columns(id_row, id_col)
    dq[...] = jnp.zeros_like(dq)

    @pl.loop(0, tiles)
    def _(j):
        for load in loads(j):
            load.wait()
        k0 = pl.multiple_of(j * T, T)
        rows = pl.ds(k0, T)
        qt[:, rows] = (qkv[rows, :width] * BF16(HEAD**-0.5)).T
        kt[:, rows] = qkv[rows, width : 2 * width].T
        gt[:, rows] = do[rows, :].T

    for n in range(carried):
        carry_in(n).wait()
        carry_out(n).start()

    @pl.loop(0, tiles // 2)
    def _(j):
        k0 = pl.multiple_of(j * W2, W2)
        mine = jnp.logical_and(2 * j >= off, 2 * j < off + own)
        low, high = tile_span(ids, 2 * j, 2 * j + 1)
        low = jnp.where(mine, low, jnp.maximum(low, off))
        high = jnp.where(mine, high, jnp.minimum(high, off + own))
        for p in range(pairs):
            dk[p] = jnp.zeros((W2, 128), F32)
            dv[p] = jnp.zeros((W2, 128), F32)

        @pl.loop(low, high)
        def _(i):
            q0 = pl.multiple_of(i * T, T)
            same = same_image(id_col, pl.ds(k0, W2), id_row, i)
            qs, gs, ss, ps, es, ds = [], [], [], [], [], []
            for p in range(pairs):
                cols = p * 128
                k = qkv[pl.ds(k0, W2), width + cols : width + cols + 128]
                v = qkv[pl.ds(k0, W2), 2 * width + cols : 2 * width + cols + 128]
                ss.append(mm(k, by_head_rows(qt[cols : cols + 128, pl.ds(q0, T)])))
                ps.append(mm(v, by_head_rows(gt[cols : cols + 128, pl.ds(q0, T)])))
            for p in range(pairs):
                one = jnp.concatenate([stats[i, 2 * p : 2 * p + 1, :], stats[i, 2 * p + 1 : 2 * p + 2, :]], 1)
                two = jnp.concatenate([stats[i, 2 * p + 16 : 2 * p + 17, :], stats[i, 2 * p + 17 : 2 * p + 18, :]], 1)
                e = jnp.exp(jnp.where(same, ss[p], -1e30) - one)
                es.append(e.astype(BF16))
                ds.append((e * (ps[p] - two)).astype(BF16))
            a, b, c = [], [], []
            for p in range(pairs):
                cols = p * 128
                a.append(mm(es[p], by_head(do[pl.ds(q0, T), cols : cols + 128])))
                b.append(mm(ds[p], by_head(qkv[pl.ds(q0, T), cols : cols + 128] * BF16(HEAD**-0.5))))
                c.append(mm(kt[cols : cols + 128, pl.ds(k0, W2)], ds[p]))
            for p in range(pairs):
                dv[p] += a[p]
                dk[p] += b[p]
                dq[p, i] += jnp.concatenate([c[p][:HEAD, :T], c[p][HEAD:, T:]], 0)

        @pl.when(mine)
        def _():
            r0 = pl.multiple_of(j * W2 - off * T, W2)
            for p in range(pairs):
                cols = p * 128
                out[pl.ds(r0, W2), width + cols : width + cols + 128] = dk[p].astype(BF16)
                out[pl.ds(r0, W2), 2 * width + cols : 2 * width + cols + 128] = dv[p].astype(BF16)

    @pl.loop(0, own)
    def _(i):
        for p in range(pairs):
            cols = p * 128
            out[pl.ds(pl.multiple_of(i * T, T), T), cols : cols + 128] = (dq[p, off + i] * HEAD**-0.5).T.astype(BF16)

    for n in range(carried):
        carry_out(n).wait()


def attn_backward(ids, qkv, do, stats, *arrays):
    all_rows, columns = qkv.shape
    own_rows = all_rows // 2
    width = columns // 3
    tiles = all_rows // T
    pairs = width // 128
    anywhere = pl.BlockSpec(memory_space=pl.ANY)
    return pl.pallas_call(
        functools.partial(attn_backward_kernel, width, len(arrays)),
        out_shape=[jax.ShapeDtypeStruct((own_rows, columns), BF16)] + [jax.ShapeDtypeStruct(v.shape, v.dtype) for v in arrays],
        in_specs=[SM, VM, anywhere, anywhere, VM] + [anywhere] * len(arrays),
        out_specs=[VM] + [anywhere] * len(arrays),
        scratch_shapes=[
            pltpu.VMEM((pairs, tiles, 128, T), F32),
            pltpu.VMEM((pairs, W2, 128), F32),
            pltpu.VMEM((pairs, W2, 128), F32),
            pltpu.VMEM((width, all_rows), BF16),
            pltpu.VMEM((width, all_rows), BF16),
            pltpu.VMEM((width, all_rows), BF16),
            pltpu.VMEM((all_rows, T), F32),
            pltpu.VMEM((all_rows, columns), BF16),
            pltpu.VMEM((all_rows, width), BF16),
            pltpu.SemaphoreType.DMA((2, tiles)),
            pltpu.SemaphoreType.DMA((2, max(len(arrays), 1))),
        ]
        + [pltpu.VMEM(v.shape, v.dtype) for v in arrays],
        compiler_params=pltpu.CompilerParams(vmem_limit_bytes=56 * 2**20),
        name="attention_backward",
    )(ids, ids, qkv, do, stats, *arrays)


ln_epsilon = 1e-06
drop_scale = 1.0 / 0.9


MESH = pl.DeviceIdType.MESH


class Place:
    def __init__(self):
        self.seq = lax.axis_index("seq")
        self.x = lax.axis_index("hd")
        self.c = lax.rem(self.seq, 2)
        self.y = lax.rem(self.seq // 2, 2)
        self.z = self.seq // 4

    def partner(self, axis):
        if axis == "c":
            return (self.seq + 1 - 2 * self.c, self.x)
        if axis == "y":
            return (self.seq + 2 - 4 * self.y, self.x)
        return (self.seq, 1 - self.x)

    def level(self, step):
        return (lax.rem(self.z + step, 4) * 4 + lax.rem(self.seq, 4), self.x)

    def index(self, axis):
        return {"x": self.x, "y": self.y, "c": self.c}[axis]


def greet(place):
    barrier = pltpu.get_barrier_semaphore()
    for other in [place.partner(a) for a in "cxy"] + [place.level(d) for d in (1, 2, 3)]:
        pl.semaphore_signal(barrier, inc=1, device_id=other, device_id_type=MESH)


def meet():
    pl.semaphore_wait(pltpu.get_barrier_semaphore(), 6)


def send(source, target, send_sem, recv_sem, other):
    copy = pltpu.make_async_remote_copy(
        src_ref=source, dst_ref=target, send_sem=send_sem, recv_sem=recv_sem, device_id=other, device_id_type=MESH
    )
    copy.start()
    return copy


class Flow:
    def __init__(self, place, axes, g, r0, r1, r2, r3, sems, recvs):
        self.place, self.axes, self.g = place, axes, g
        self.r0, self.r1, self.r2, self.r3 = r0, r1, r2, r3
        self.sems, self.recvs = sems, recvs
        self.copies = []

    def start(self):
        p = self.place
        self.copies.append(send(self.g.at[1 - p.c], self.r0, self.sems.at[0], self.recvs.at[0], p.partner("c")))

    def first(self):
        p = self.place
        self.copies[0].wait_recv()
        me = p.index(self.axes[0])

        def add(half):
            @pl.loop(0, 8)
            def _(i):
                b, z = i // 4, lax.rem(i, 4)
                self.r0[half, b, z] = self.r0[half, b, z] + self.g[p.c, half, b, z]

        add(1 - me)
        self.copies.append(
            send(self.r0.at[1 - me], self.r1, self.sems.at[1], self.recvs.at[1], p.partner(self.axes[0]))
        )
        add(me)

    def second(self):
        p = self.place
        self.copies[1].wait_recv()
        me, before = p.index(self.axes[1]), p.index(self.axes[0])

        def add(half):
            @pl.loop(0, 4)
            def _(z):
                self.r1[half, z] = self.r1[half, z] + self.r0[before, half, z]

        add(1 - me)
        self.copies.append(
            send(self.r1.at[1 - me], self.r2, self.sems.at[2], self.recvs.at[2], p.partner(self.axes[1]))
        )
        add(me)

    def third(self):
        p = self.place
        self.copies[2].wait_recv()
        before = p.index(self.axes[1])

        @pl.loop(0, 4)
        def _(z):
            self.r2[z] = self.r2[z] + self.r1[before, z]

        for d in (1, 2, 3):
            target = lax.rem(p.z + d, 4)
            self.copies.append(
                send(self.r2.at[target], self.r3.at[d - 1], self.sems.at[2 + d], self.recvs.at[2 + d], p.level(d))
            )

    def last(self):
        p = self.place
        total = self.r2[p.z].astype(F32)
        for d in (1, 2, 3):
            self.copies[2 + d].wait_recv()
            total = total + self.r3[d - 1].astype(F32)
        return total

    def finish(self):
        for copy in self.copies:
            copy.wait_send()


def flow_scratch(rows, cols, kind=BF16):
    return [
        pltpu.VMEM((2, 2, 4, rows, cols), kind),
        pltpu.VMEM((2, 4, rows, cols), kind),
        pltpu.VMEM((4, rows, cols), kind),
        pltpu.VMEM((3, rows, cols), kind),
        pltpu.SemaphoreType.DMA((6,)),
        pltpu.SemaphoreType.DMA((6,)),
    ]


class ChunkFlow(Flow):
    def __init__(self, place, axes, home, *refs):
        super().__init__(place, axes, *refs)
        self.home = home

    def third(self):
        p = self.place
        self.copies[2].wait_recv()
        self.r2[...] = self.r2[...] + self.r1[p.index(self.axes[1])]
        slot = lax.rem(p.z - self.home + 3, 4)
        self.hop = pltpu.make_async_remote_copy(
            src_ref=self.r2,
            dst_ref=self.r3.at[slot],
            send_sem=self.sems.at[3],
            recv_sem=self.recvs.at[3 + slot],
            device_id=(self.home * 4 + lax.rem(p.seq, 4), p.x),
            device_id_type=MESH,
        )

        @pl.when(p.z != self.home)
        def _():
            self.hop.start()

    def first(self):
        p = self.place
        self.copies[0].wait_recv()
        me = p.index(self.axes[0])

        def add(half):
            for b in range(2):
                self.r0[half, b] = self.r0[half, b] + self.g[p.c, half, b]

        add(1 - me)
        self.copies.append(
            send(self.r0.at[1 - me], self.r1, self.sems.at[1], self.recvs.at[1], p.partner(self.axes[0]))
        )
        add(me)

    def second(self):
        p = self.place
        self.copies[1].wait_recv()
        me, before = p.index(self.axes[1]), p.index(self.axes[0])
        self.r1[1 - me] = self.r1[1 - me] + self.r0[before, 1 - me]
        self.copies.append(
            send(self.r1.at[1 - me], self.r2, self.sems.at[2], self.recvs.at[2], p.partner(self.axes[1]))
        )
        self.r1[me] = self.r1[me] + self.r0[before, me]

    def last_into(self, out):
        p = self.place

        @pl.when(p.z == self.home)
        def _():
            total = self.r2[...].astype(F32)
            for slot in range(3):
                pltpu.make_async_remote_copy(
                    src_ref=self.r2,
                    dst_ref=self.r3.at[slot],
                    send_sem=self.sems.at[3],
                    recv_sem=self.recvs.at[3 + slot],
                    device_id=p.level(1),
                    device_id_type=MESH,
                ).wait_recv()
                total = total + self.r3[slot].astype(F32)
            out[...] = total

    def finish(self):
        super().finish()

        @pl.when(self.place.z != self.home)
        def _():
            self.hop.wait_send()


class LevelFlow(Flow):
    axes = "zxy"

    def __init__(self, place, g, r0, r1, r2, r3, sems, recvs):
        super().__init__(place, "zxy", g, r0, r1, r2, r3, sems, recvs)

    def first(self):
        p = self.place
        self.copies[0].wait_recv()

        @pl.loop(0, 4)
        def _(z):
            for x in range(2):
                for y in range(2):
                    self.r0[z, x, y] = self.r0[z, x, y] + self.g[p.c, z, x, y]

        for d in (1, 2, 3):
            self.copies.append(
                send(self.r0.at[lax.rem(p.z + d, 4)], self.r1.at[d - 1], self.sems.at[d], self.recvs.at[d], p.level(d))
            )

    def second(self):
        p = self.place
        for d in (1, 2, 3):
            self.copies[d].wait_recv()
        for x in range(2):
            for y in range(2):
                total = self.r0[p.z, x, y].astype(F32)
                for d in range(3):
                    total = total + self.r1[d, x, y].astype(F32)
                self.r1[0, x, y] = total.astype(BF16)
        self.copies.append(
            send(self.r1.at[0, 1 - p.x], self.r2, self.sems.at[4], self.recvs.at[4], p.partner("x"))
        )

    def third(self):
        p = self.place
        self.copies[4].wait_recv()
        for y in range(2):
            self.r2[y] = self.r2[y] + self.r1[0, p.x, y]
        self.copies.append(send(self.r2.at[1 - p.y], self.r3, self.sems.at[5], self.recvs.at[5], p.partner("y")))

    def last(self):
        self.copies[5].wait_recv()
        return self.r2[self.place.y].astype(F32) + self.r3[...].astype(F32)


def level_scratch(rows, cols):
    return [
        pltpu.VMEM((4, 2, 2, rows, cols), BF16),
        pltpu.VMEM((3, 2, 2, rows, cols), BF16),
        pltpu.VMEM((2, rows, cols), BF16),
        pltpu.VMEM((rows, cols), BF16),
        pltpu.SemaphoreType.DMA((6,)),
        pltpu.SemaphoreType.DMA((6,)),
    ]


def chunk_scratch(rows, cols):
    return [
        pltpu.VMEM((2, 2, rows, cols), BF16),
        pltpu.VMEM((2, rows, cols), BF16),
        pltpu.VMEM((rows, cols), BF16),
        pltpu.VMEM((3, rows, cols), BF16),
        pltpu.SemaphoreType.DMA((6,)),
        pltpu.SemaphoreType.DMA((6,)),
    ]


def row_norm(x):
    mean = jnp.mean(x, -1, keepdims=True)
    center = x - mean
    rstd = lax.rsqrt(jnp.mean(center * center, -1, keepdims=True) + ln_epsilon)
    return center * rstd, rstd


def norm_back(hat, rstd, gain, grad):
    scaled = grad * gain
    return rstd * (scaled - jnp.mean(scaled, -1, keepdims=True) - hat * jnp.mean(scaled * hat, -1, keepdims=True))


def col_sum(x):
    return jnp.sum(x, 0, keepdims=True)


def put_blocks(product, z, axes, g):
    half = product.shape[1] // 2
    for y in range(2):
        for c in range(2):
            for x in range(2):
                r = ((y * 2 + c) * 2 + x) * 24
                block = jnp.concatenate([product[r : r + 24, :half], product[r : r + 24, half:]], 0)
                at = {"x": x, "y": y}
                if axes == "zxy":
                    g[c, z, x, y] = block.astype(BF16)
                else:
                    g[c, at[axes[0]], at[axes[1]], z] = block.astype(BF16)


def put_chunk(product, y, axes, g):
    for c in range(2):
        for x in range(2):
            r = (c * 2 + x) * 96
            at = {"x": x, "y": y}
            g[c, at[axes[0]], at[axes[1]]] = product[r : r + 96].astype(BF16)


R = 256
HALO = 608
FLOW_REFS = 6
ORDER = (0, 3, 1, 2)
PATHS1 = ("xy", "xy", "zxy", "xy")
PATHS2 = ("yx", "yx", "yx", "yx")


def mlp_kernel(reduce, chunks, *refs):
    o, lse, x, keep, cot, w_out, b_out, gain, bias, w1, b1, w2, b2 = refs[:13]
    mixed_far, dx1_far, do, stats, small, g_far, out1, out2 = refs[13:21]
    v1, v2, x1s, n2s, n2t, dms, gs, dus, das, macc, nacc, load1, load2, halo_sems = refs[21:35]
    mixed, dx1, g_out, near_sems = refs[35:39]
    flow_refs = refs[39:]
    stores = [
        pltpu.make_async_copy(near, far, near_sems.at[n])
        for n, (near, far) in enumerate(((mixed, mixed_far), (dx1, dx1_far), (g_out, g_far)))
    ]
    side = lax.axis_index("hd")
    base = pl.multiple_of(side * o.shape[0], o.shape[0])
    owner = lax.broadcasted_iota(jnp.int32, (16, o.shape[1]), 1) // HEAD
    heads = (owner == lax.broadcasted_iota(jnp.int32, (16, o.shape[1]), 0)).astype(BF16)
    rows, width = o.shape
    tiles = rows // R
    loads = []
    for k in range(chunks):
        cols = pl.ds(k * width, width)
        loads.append(
            (
                pltpu.make_async_copy(w1.at[:, cols], v1.at[k], load1.at[k]),
                pltpu.make_async_copy(w2.at[cols, :], v2.at[k], load2.at[k]),
            )
        )
        loads[k][0].start()
        loads[k][1].start()
    if reduce:
        place = Place()
        greet(place)
        per = 1 + FLOW_REFS
        flows1 = []
        for k in range(chunks):
            mine = flow_refs[2 * per * k : 2 * per * k + per]
            flows1.append(LevelFlow(place, *mine) if PATHS1[k] == "zxy" else Flow(place, PATHS1[k], *mine))
        flows2 = [ChunkFlow(place, PATHS2[k], k, *flow_refs[2 * per * k + per : 2 * per * (k + 1)]) for k in range(chunks)]

    small[...] = jnp.zeros_like(small)

    @pl.loop(0, tiles)
    def _(t):
        r = pl.ds(pl.multiple_of(t * R, R), R)
        x1 = x[r, :].astype(F32) + keep[r, 0:1] * (mm(o[r, :], w_out[...]) + b_out[...])
        x1s[r, :] = x1
        hat, _ = row_norm(x1)
        n2 = (hat * gain[...] + bias[...]).astype(BF16)
        n2s[r, :] = n2
        dm = (cot[r, :].astype(F32) * keep[r, 1:2]).astype(BF16)
        dms[r, :] = dm
        small[7:8, :] += col_sum(dm.astype(F32))

    n2t[...] = n2s[...].T

    def row_tile(k, t, first, slot):
        r = slice(t * R, t * R + R)
        u = mm(n2s[r, :], v1[k]) + b1[k * width : k * width + width]
        dg = mm_nt(dms[r, :], v2[k])
        cdf = 0.5 + 0.5 * lax.erf(u * 0.7071067811865476)
        pdf = jnp.exp(u * u * -0.5) * 0.3989422804014327
        g = (u * cdf).astype(BF16)
        du = (dg * (cdf + u * pdf)).astype(BF16)
        gs[slot, r, :] = g
        dus[slot, r, :] = du
        small[3 + k : 4 + k, :] += col_sum(du.astype(F32))
        if first:
            macc[r, :] = mm(g, v2[k])
            nacc[r, :] = mm_nt(du, v1[k])
        else:
            macc[r, :] += mm(g, v2[k])
            nacc[r, :] += mm_nt(du, v1[k])

    steps = {}
    if reduce:
        for at, k in enumerate(ORDER[:3]):
            for flow, late in ((flows2[k], 0), (flows1[k], 1)):
                steps.setdefault((at + 1, 1 + late), []).append(flow.first)
                if at < 2:
                    steps.setdefault((at + 2, 1 + late), []).append(flow.second)
                    steps.setdefault((2, 5) if at == 0 else (4, 1 + late), []).append(flow.third)

    def point(*at):
        for step in steps.pop(at, []):
            step()

    def gradient2(k, slot):
        @pl.loop(0, 2)
        def _(y):
            product = mm_tn(gs[slot, :, pl.ds(pl.multiple_of(y * 384, 384), 384)], dms[...])
            put_chunk(product, y, flows2[k].axes, flows2[k].g)

        flows2[k].start()

    def gradient1(k, slot):
        @pl.loop(0, 2)
        def _(h):
            product = mm(n2t[pl.ds(pl.multiple_of(h * 384, 128), 384), :], dus[slot])
            for z in range(2):
                put_blocks(product[z * 192 : z * 192 + 192], 2 * h + z, flows1[k].axes, flows1[k].g)

        flows1[k].start()

    for at, k in enumerate(ORDER if reduce else range(chunks)):
        slot = at % 2
        loads[k][0].wait()
        loads[k][1].wait()
        for t in range(tiles):
            row_tile(k, t, at == 0, slot)
            point(at, t + 1)
        if reduce and at == 0:
            meet()
        if reduce and at < 3:
            gradient2(k, slot)
            point(at, 4)
            gradient1(k, slot)
            point(at, 5)
        if not reduce:

            @pl.loop(0, 3)
            def _(t):
                r = pl.ds(pl.multiple_of(t * 256, 256), 256)
                out2[pl.ds(pl.multiple_of(k * width + t * 256, 256), 256), :] = mm_tn(gs[slot, :, r], dms[...]).astype(BF16)
                out1[r, k * width : k * width + width] = mm(n2t[r, :], dus[slot]).astype(BF16)

    apart = rows - HALO
    pad = pl.multiple_of((1 - side) * (2 * rows - apart), 16)
    do[pl.ds(pad, apart), :] = jnp.zeros((apart, width), BF16)
    stat_tiles = pl.cdiv(HALO, T)
    spare = rows // T - stat_tiles
    for s in range(spare):
        stats[(1 - side) * (2 * rows // T - spare) + s] = jnp.zeros((32, T), F32)
    exchange = []

    def exchange_rows(ref, first, count, n):
        part = ref.at[pl.ds(first, count)]
        exchange.append(send(part, part, halo_sems.at[2 * n], halo_sems.at[2 * n + 1], place.partner("x")))

    for t in range(tiles):
        at = lax.rem(t + 1 - side, tiles)
        r = pl.ds(pl.multiple_of(at * R, R), R)
        hat, rstd = row_norm(x1s[r, :])
        dn2 = nacc[r, :]
        dx = cot[r, :].astype(F32) + norm_back(hat, rstd, gain[...], dn2)
        dx1[r, :] = dx
        da = (dx * keep[r, 0:1]).astype(BF16)
        das[r, :] = da
        grad_o = mm_nt(da, w_out[...]).astype(BF16)
        do[pl.ds(pl.multiple_of(base + at * R, R), R), :] = grad_o
        small[0:1, :] += col_sum(da.astype(F32))
        small[1:2, :] += col_sum(dn2 * hat)
        small[2:3, :] += col_sum(dn2)
        prod = grad_o.astype(F32) * o[r, :].astype(F32)
        high = prod.astype(BF16)
        low = (prod - high.astype(F32)).astype(BF16)
        sums = mm_nt(heads, high) + mm_nt(heads, low)
        for s in range(R // T):
            own = at * (R // T) + s
            stats[side * (rows // T) + own, :16] = lse[own]
            stats[side * (rows // T) + own, 16:] = sums[:, s * T : s * T + T]
        point(chunks, t + 1)
        if reduce and t == 0:
            exchange_rows(do, pl.multiple_of(base + at * R, R), R, 0)

    if reduce:
        third, fourth = ORDER[2], ORDER[3]
        exchange_rows(stats, spare + side * stat_tiles, stat_tiles, 3)
        gradient2(fourth, 1)
        gradient1(fourth, 1)

    stores[1].start()
    n2t[...] = o[...].T
    if reduce:

        @pl.loop(0, 2)
        def _(h):
            product = mm(n2t[pl.ds(pl.multiple_of(h * 384, 128), 384), :], das[...])
            for z in range(2):
                put_blocks(product[z * 192 : z * 192 + 192], 2 * h + z, "zxy", g_out)

        flows2[fourth].first()
        flows1[fourth].first()
        flows2[third].second()
        flows1[third].second()
    else:

        @pl.loop(0, 3)
        def _(t):
            r = pl.ds(pl.multiple_of(t * 256, 256), 256)
            g_out[r, :] = mm(n2t[r, :], das[...]).astype(BF16)

    @pl.loop(0, tiles)
    def _(t):
        r = pl.ds(pl.multiple_of(t * R, R), R)
        mixed[r, :] = (x1s[r, :] + keep[r, 1:2] * (macc[r, :] + b2[...])).astype(BF16)

    stores[0].start()
    stores[2].start()

    if reduce:
        half = width // 2

        def keep_share(k):
            total = flows1[k].last()
            out1[:, k * width : k * width + half] = total[:24]
            out1[:, k * width + half : (k + 1) * width] = total[24:]
            flows2[k].last_into(out2)

        for at in sorted(steps):
            point(*at)
        second_tile = 2 - side
        exchange_rows(do, pl.multiple_of(base + second_tile * R, R), R, 1)
        flows2[third].third()
        flows1[third].third()
        flows2[fourth].second()
        exchange_rows(do, pl.multiple_of(base + (1 - side) * apart + side * 2 * R, 16), HALO - 2 * R, 2)
        flows1[fourth].second()
        flows2[fourth].third()
        flows1[fourth].third()
        for k in range(chunks):
            keep_share(k)
        for k in range(chunks):
            flows1[k].finish()
            flows2[k].finish()
        for copy in exchange:
            copy.wait()
    for store in stores:
        store.wait()


def mlp_step(reduce, o, lse, x, keep, cot, w_out, b_out, gain, bias, w1, b1, w2, b2):
    rows, width = o.shape
    chunks = w1.shape[1] // width
    block = lambda dims, kind: jax.ShapeDtypeStruct(dims, kind)
    outs = [
        block((rows, width), BF16),
        block((rows, width), F32),
        block((2 * rows, width), BF16),
        block((2 * rows // T, 32, T), F32),
        block((16, width), F32),
    ]
    if reduce:
        outs += [block((2, 4, 2, 2, 48, width // 2), BF16), block((24, chunks * width), F32), block((96, width), F32)]
    else:
        outs += [block((width, width), BF16), block(w1.shape, BF16), block(w2.shape, BF16)]
    scratch = [
        pltpu.VMEM((chunks, width, width), BF16),
        pltpu.VMEM((chunks, width, width), BF16),
        pltpu.VMEM((rows, width), F32),
        pltpu.VMEM((rows, width), BF16),
        pltpu.VMEM((width, rows), BF16),
        pltpu.VMEM((rows, width), BF16),
        pltpu.VMEM((2, rows, width), BF16),
        pltpu.VMEM((2, rows, width), BF16),
        pltpu.VMEM((rows, width), BF16),
        pltpu.VMEM((rows, width), F32),
        pltpu.VMEM((rows, width), F32),
        pltpu.SemaphoreType.DMA((chunks,)),
        pltpu.SemaphoreType.DMA((chunks,)),
        pltpu.SemaphoreType.DMA((8,)),
        pltpu.VMEM((rows, width), BF16),
        pltpu.VMEM((rows, width), F32),
        pltpu.VMEM(outs[5].shape, BF16),
        pltpu.SemaphoreType.DMA((3,)),
    ]
    params = dict(vmem_limit_bytes=60 * 2**20)
    if reduce:
        for k in range(chunks):
            if PATHS1[k] == "zxy":
                scratch += [pltpu.VMEM((2, 4, 2, 2, 48, width // 2), BF16)] + level_scratch(48, width // 2)
            else:
                scratch += [pltpu.VMEM((2, 2, 2, 4, 48, width // 2), BF16)] + flow_scratch(48, width // 2)
            scratch += [pltpu.VMEM((2, 2, 2, 96, width), BF16)] + chunk_scratch(96, width)
        params.update(collective_id=1, has_side_effects=True)
    anywhere = pl.BlockSpec(memory_space=pl.ANY)
    return pl.pallas_call(
        functools.partial(mlp_kernel, reduce, chunks),
        out_shape=outs,
        in_specs=[VM] * 9 + [anywhere, VM, anywhere, VM],
        out_specs=[anywhere, anywhere, VM, VM, VM, anywhere, VM, VM],
        scratch_shapes=scratch,
        compiler_params=pltpu.CompilerParams(**params),
        name="mlp_step",
    )(o, lse, x, keep, cot, w_out, b_out, gain, bias, w1, b1, w2, b2)


SMALLS = ((8, 1), (9, 1), (10, 2), (0, 1), (1, 1), (2, 1), (3, 4), (7, 1))


def by_owner(sums):
    width = sums.shape[1]
    lane = lax.broadcasted_iota(jnp.int32, (32, width), 1)
    block = lax.broadcasted_iota(jnp.int32, (32, width), 0)
    source = lax.broadcasted_iota(jnp.int32, (width, 128), 0)
    target = lax.broadcasted_iota(jnp.int32, (width, 128), 1)
    parts = []
    for first, rows in SMALLS:
        size = rows * width // 32
        row = block // (32 // rows)
        spread = jnp.zeros((32, width), F32)
        for r in range(rows):
            spread = jnp.where(row == r, sums[first + r : first + r + 1, :], spread)
        spread = jnp.where(lane // size == lax.rem(block, 32 // rows), spread, 0.0)
        pick = (lax.rem(source, size) == target).astype(BF16)
        total = jnp.zeros((32, 128), F32)
        for _ in range(3):
            piece = spread.astype(BF16)
            total = total + mm(piece, pick)
            spread = spread - piece.astype(F32)
        parts.append(total.reshape(32, 1, 128))
    return jnp.concatenate(parts, 1)


def tail_kernel(reduce, *refs):
    dqkv, x, dx1_far, gain, n1t, w_far, g_out, small_in = refs[:8]
    grad_far, grad_w, grad_o, small = refs[8:12]
    dx1, w, near_sems = refs[12:15]
    rest = refs[15:]
    load_w = pltpu.make_async_copy(w_far, w, near_sems.at[0])
    load_x = pltpu.make_async_copy(dx1_far, dx1, near_sems.at[1])
    load_w.start()
    load_x.start()
    rows, width = x.shape
    tiles = rows // R
    if reduce:
        place = Place()
        greet(place)
        out_flow = LevelFlow(place, g_out, *rest[:6])
        flows = [Flow(place, ("yx", "xy", "yx")[i], *rest[6 + 7 * i : 13 + 7 * i]) for i in range(3)]
        sums = Flow(place, "xy", *rest[27:34])

    if reduce:
        meet()
        out_flow.start()
        for i in range(3):

            @pl.loop(0, 2)
            def _(h):
                product = mm(n1t[pl.ds(pl.multiple_of(h * 384, 128), 384), :], dqkv[:, i * width : (i + 1) * width])
                for z in range(2):
                    put_blocks(product[z * 192 : z * 192 + 192], 2 * h + z, flows[i].axes, flows[i].g)

            flows[i].start()
            if i == 0:
                out_flow.first()
            else:
                flows[i - 1].first()
    else:

        @pl.loop(0, 3)
        def _(t):
            r = pl.ds(pl.multiple_of(t * 256, 256), 256)
            for i in range(3):
                grad_w[r, i * width : (i + 1) * width] = mm(n1t[r, :], dqkv[:, i * width : (i + 1) * width]).astype(BF16)

    small_ref = rest[34] if reduce else small
    small_ref[...] = small_in[...]

    def rows_back(t):
        r = pl.ds(pl.multiple_of(t * R, R), R)
        hat, rstd = row_norm(x[r, :].astype(F32))
        dn1 = mm_nt(dqkv[r, :], w[...])
        dx1[r, :] = dx1[r, :] + norm_back(hat, rstd, gain[...], dn1)
        small_ref[8:9, :] += col_sum(dn1 * hat)
        small_ref[9:10, :] += col_sum(dn1)
        small_ref[10:11, :] += col_sum(dqkv[r, :width].astype(F32))
        small_ref[11:12, :] += col_sum(dqkv[r, 2 * width :].astype(F32))

    if reduce:
        flows[2].first()
    load_w.wait()
    load_x.wait()
    pl.loop(0, tiles)(rows_back)
    store_x = pltpu.make_async_copy(dx1, grad_far, near_sems.at[2])
    store_x.start()
    if reduce:
        half = width // 2
        shares = by_owner(small_ref[...])
        for b in range(32):
            sums.g[b // 2 % 2, b % 2, b // 4 % 2, b // 8] = shares[b]
        sums.start()
        flows[0].second()
        sums.first()
        flows[1].second()
        out_flow.second()
        sums.second()
        flows[0].third()
        out_flow.third()
        flows[1].third()
        sums.third()
        flows[2].second()
        flows[2].third()
        total = out_flow.last()
        grad_o[:, :half] = total[:24]
        grad_o[:, half:] = total[24:]
        small[...] = sums.last()
        for i in range(3):
            total = flows[i].last()
            grad_w[:, i * width : i * width + half] = total[:24]
            grad_w[:, i * width + half : (i + 1) * width] = total[24:]
        for flow in (out_flow, *flows, sums):
            flow.finish()
    store_x.wait()


def tail_step(reduce, dqkv, x, dx1, gain, n1t, w, g_out, small):
    rows, width = x.shape
    block = lambda dims, kind: jax.ShapeDtypeStruct(dims, kind)
    outs = [block((rows, width), F32)]
    scratch = [
        pltpu.VMEM((rows, width), F32),
        pltpu.VMEM(w.shape, BF16),
        pltpu.SemaphoreType.DMA((3,)),
    ]
    anywhere = pl.BlockSpec(memory_space=pl.ANY)
    params = dict(vmem_limit_bytes=60 * 2**20)
    args = [dqkv, x, dx1, gain, n1t, w, g_out, small]
    if reduce:
        outs += [block((24, 3 * width), F32), block((24, width), F32), block((8, 128), F32)]
        scratch += level_scratch(48, width // 2)
        for _ in range(3):
            scratch += [pltpu.VMEM((2, 2, 2, 4, 48, width // 2), BF16)] + flow_scratch(48, width // 2)
        scratch += [pltpu.VMEM((2, 2, 2, 4, 8, 128), F32)] + flow_scratch(8, 128, F32)
        scratch += [pltpu.VMEM((16, width), F32)]
        params.update(collective_id=2, has_side_effects=True)
    else:
        outs += [block(w.shape, BF16), block((8, 128), F32), block((16, width), F32)]
    return pl.pallas_call(
        functools.partial(tail_kernel, reduce),
        out_shape=outs,
        in_specs=[VM, VM, anywhere, VM, VM, anywhere, VM, VM],
        out_specs=[anywhere, VM, VM, VM],
        scratch_shapes=scratch,
        compiler_params=pltpu.CompilerParams(**params),
        name="tail_step",
    )(*args)


def project_kernel(x, gain, bias, w, b, out, turned):
    @pl.loop(0, x.shape[0] // T)
    def _(t):
        r = pl.ds(pl.multiple_of(t * T, T), T)
        hat, _ = row_norm(x[r, :].astype(F32))
        n1 = (hat * gain[...] + bias[...]).astype(BF16)
        out[r, :] = (mm(n1, w[...]) + b[...]).astype(BF16)
        turned[:, r] = n1.T


def project(x, gain, bias, w, b):
    return pl.pallas_call(
        project_kernel,
        out_shape=(
            jax.ShapeDtypeStruct((x.shape[0], w.shape[1]), BF16),
            jax.ShapeDtypeStruct((x.shape[1], x.shape[0]), BF16),
        ),
        in_specs=[VM] * 5,
        out_specs=(VM, VM),
        compiler_params=pltpu.CompilerParams(vmem_limit_bytes=32 * 2**20),
        cost_estimate=pl.CostEstimate(flops=2 * x.shape[0] * w.shape[0] * w.shape[1], bytes_accessed=9 * 2**20, transcendentals=0),
        name="project",
    )(x, gain, bias, w, b)


def finish_kernel(small, far, *refs):
    near, sems = refs[-2:]
    copied = (len(refs) - 3 - len(SMALLS)) // 2
    loads, stores = [], []
    for n in range(4):
        rows = pl.ds(n * (near.shape[0] // 4), near.shape[0] // 4)
        loads.append(pltpu.make_async_copy(far.at[rows, :], near.at[rows, :], sems.at[0, n]))
        stores.append(pltpu.make_async_copy(near.at[rows, :], refs[copied].at[rows, :], sems.at[1, n]))
        loads[n].start()
    for source, target in zip(refs[:copied], refs[copied + 1 : 2 * copied + 1]):
        target[...] = source[...]
    for row, out in enumerate(refs[2 * copied + 1 : -2]):
        out[...] = small[row, : out.shape[0]]
    for load, store in zip(loads, stores):
        load.wait()
        store.start()
    for store in stores:
        store.wait()


def finish(shards, small, large, *arrays):
    width = large.shape[1]
    anywhere = pl.BlockSpec(memory_space=pl.ANY)
    outs = [jax.ShapeDtypeStruct(a.shape, a.dtype) for a in (large, *arrays)]
    outs += [jax.ShapeDtypeStruct((rows * width // shards,), F32) for _, rows in SMALLS]
    return pl.pallas_call(
        finish_kernel,
        out_shape=outs,
        in_specs=[VM, anywhere] + [VM] * len(arrays),
        out_specs=[anywhere] + [VM] * (len(outs) - 1),
        scratch_shapes=[pltpu.VMEM(large.shape, large.dtype), pltpu.SemaphoreType.DMA((2, 4))],
        name="finish",
    )(small, large, *arrays)


def halo_of(rows, halo, side):
    mine = jnp.where(side == 0, rows[rows.shape[0] - halo :], rows[:halo])
    return lax.ppermute(mine, "hd", [(0, 1), (1, 0)])


def in_pack_order(own, halo, side, before=0, after=0):
    dims = (own.shape[0] - halo.shape[0], *own.shape[1:])
    late, early = jnp.full(dims, after, own.dtype), jnp.full(dims, before, own.dtype)
    return jnp.where(side == 0, jnp.concatenate([own, halo, late], 0), jnp.concatenate([early, halo, own], 0))


def per_device(tokens, image_ids, keep_masks, ln1_gain, ln1_bias, w_qkv, qv_bias, w_out, b_out,
               ln2_gain, ln2_bias, w_fc1, b_fc1, w_fc2, b_fc2, cotangent):
    rows, width = tokens.shape
    halo = HALO
    both = ("seq", "hd")
    side = lax.axis_index("hd")
    reduce = lax.axis_size("seq") == 16 and lax.axis_size("hd") == 2
    halo_tiles = pl.cdiv(halo, T)
    tok_halo = halo_of(tokens, halo, side)
    id_halo = halo_of(image_ids, halo, side)
    id_all = in_pack_order(image_ids, id_halo, side, -1, 1 << 20)
    ids = id_all.reshape(-1, T)
    one_hot = (image_ids[:, None] == jnp.arange(keep_masks.shape[1], dtype=jnp.int32)[None, :]).astype(F32)
    keep_rows = jnp.dot(one_hot, keep_masks[0].astype(F32)) * drop_scale
    bias_all = jnp.concatenate([qv_bias[:width], jnp.zeros((width,), F32), qv_bias[width:]])

    norm1 = (ln1_gain, ln1_bias, w_qkv, bias_all)
    qkv_own, n1t = project(tokens, *norm1)
    heads_out, lse, qkv_all = attn_forward(ids, qkv_own, tok_halo, *norm1)
    mixed, dx1, do_all, stats_all, small, g_out, grad_fc1, grad_fc2 = mlp_step(
        reduce, heads_out, lse, tokens, keep_rows, cotangent, w_out, b_out, ln2_gain, ln2_bias,
        w_fc1, b_fc1, w_fc2, b_fc2)
    if not reduce:
        first = side * rows
        do_own = lax.dynamic_slice_in_dim(do_all, first, rows, 0)
        stats_own = lax.dynamic_slice_in_dim(stats_all, first // T, rows // T, 0)
        do_all = in_pack_order(do_own, halo_of(do_own, halo, side), side)
        stats_all = in_pack_order(stats_own, halo_of(stats_own, halo_tiles, side), side)
    dqkv, *carried = attn_backward(ids, qkv_all, do_all, stats_all, *((mixed, grad_fc1, grad_fc2) if reduce else ()))
    if reduce:
        mixed, grad_fc1, grad_fc2 = carried
    grad_x, grad_qkv, grad_out, small = tail_step(
        reduce, dqkv, tokens, dx1, ln1_gain, n1t, w_qkv, g_out, small)
    if not reduce:
        grad_out = g_out

        def scatter(v):
            return lax.psum_scatter(v, both, scatter_dimension=0, tiled=True).astype(F32)

        grad_fc1, grad_fc2, grad_qkv, grad_out = map(scatter, (grad_fc1, grad_fc2, grad_qkv, grad_out))
        small = lax.psum(small, both)
    shards = lax.axis_size("seq") * lax.axis_size("hd")
    if reduce:
        grad_x, grad_qkv, grad_out, *vectors = finish(shards, small, grad_x, grad_qkv, grad_out)
    else:
        place = lax.axis_index("seq") * lax.axis_size("hd") + side
        vectors = []
        for first, count in SMALLS:
            size = count * width // shards
            vectors.append(lax.dynamic_slice(small[first : first + count].reshape(-1), (place * size,), (size,)))
    g1, b1, qv, bo, g2, b2, bf1, bf2 = vectors
    return mixed, grad_x, g1, b1, grad_qkv, qv, grad_out, bo, g2, b2, grad_fc1, bf1, grad_fc2, bf2


def solution(mesh):
    both = P(("seq", "hd"))
    split = P(("seq", "hd"), None)
    return jax.shard_map(
        per_device,
        mesh=mesh,
        in_specs=(split, both, P("seq", None, None)) + (P(),) * 12 + (split,),
        out_specs=(split, split, both, both, split, both, split, both, both, both, split, both, split, both),
        check_vma=False,
    )
```

```python
import functools
import jax, jax.numpy as jnp
from jax import lax
from jax.experimental import pallas as pl
from jax.experimental.pallas import tpu as pltpu
from jax.sharding import PartitionSpec as P

HEADS, HEAD = 12, 64
T = 128
W2 = 256
VM = pl.BlockSpec(memory_space=pltpu.VMEM)
SM = pl.BlockSpec(memory_space=pltpu.SMEM)
F32, BF16 = jnp.float32, jnp.bfloat16
NT = (((1,), (1,)), ((), ()))
TN = (((0,), (0,)), ((), ()))


def mm(a, b):
    return jnp.dot(a, b, preferred_element_type=F32)


def mm_nt(a, b):
    return lax.dot_general(a, b, NT, preferred_element_type=F32)


def mm_tn(a, b):
    return lax.dot_general(a, b, TN, preferred_element_type=F32)


def by_head(pair):
    lane = lax.broadcasted_iota(jnp.int32, pair.shape, 1)
    zero = jnp.zeros_like(pair)
    return jnp.concatenate(
        [jnp.where(lane < HEAD, pair, zero), jnp.where(lane < HEAD, zero, pair)], 0
    )


def by_head_rows(pair):
    row = lax.broadcasted_iota(jnp.int32, pair.shape, 0)
    zero = jnp.zeros_like(pair)
    return jnp.concatenate([jnp.where(row < HEAD, pair, zero), jnp.where(row < HEAD, zero, pair)], 1)


def tile_span(ids, first_tile, last_tile):
    low, high = 0, 0
    for u in range(ids.shape[0]):
        low += (ids[u, T - 1] < ids[first_tile, 0]).astype(jnp.int32)
        high += (ids[u, 0] <= ids[last_tile, T - 1]).astype(jnp.int32)
    return low, high


def id_columns(id_row, id_col):
    @pl.loop(0, id_row.shape[0])
    def _(j):
        line = jnp.broadcast_to(id_row[pl.ds(j, 1), :].astype(F32), (T, T))
        id_col[pl.ds(pl.multiple_of(j * T, T), T), :] = line.T


def same_image(id_col, rows, id_row, tile):
    left = id_col[rows, :]
    right = id_row[pl.ds(tile, 1), :].astype(F32)
    return jnp.concatenate([left, left], 1) == jnp.concatenate([right, right], 1)


HALO_ROWS = 304


def attn_forward_kernel(width, ids, id_row, own_qkv, halo, gain, bias, w, b, out, lse, all_qkv, qkv, sc, vt, acc, id_col, sems):
    pairs = width // 128
    rows, tiles = out.shape[0], id_row.shape[0]
    own = rows // T
    side = lax.axis_index("hd")
    off = side * own
    apart = rows - halo.shape[0]
    fetch = pltpu.make_async_copy(own_qkv, qkv.at[pl.ds(pl.multiple_of(side * rows, rows), rows), :], sems.at[0])
    fetch.start()
    id_columns(id_row, id_col)
    qkv[pl.ds(pl.multiple_of((1 - side) * (2 * rows - apart), 16), apart), :] = jnp.zeros((apart, 3 * width), BF16)

    @pl.loop(0, halo.shape[0] // HALO_ROWS)
    def _(t):
        r = pl.ds(pl.multiple_of(t * HALO_ROWS, 16), HALO_ROWS)
        hat, _ = row_norm(halo[r, :].astype(F32))
        n1 = (hat * gain[...] + bias[...]).astype(BF16)
        first = pl.multiple_of((1 - side) * rows + side * apart + t * HALO_ROWS, 16)
        qkv[pl.ds(first, HALO_ROWS), :] = (mm(n1, w[...]) + b[...]).astype(BF16)

    used_low, used_high = tile_span(ids, off, off + own - 1)
    fetch.wait()
    store = pltpu.make_async_copy(qkv, all_qkv, sems.at[1])
    store.start()

    @pl.loop(0, tiles)
    def _(j):
        rows = pl.ds(pl.multiple_of(j * T, T), T)

        @pl.when(jnp.logical_and(j >= used_low - 1, j <= used_high))
        def _():
            vt[:, rows] = qkv[rows, 2 * width :].T

    @pl.loop(0, own)
    def _(i):
        tile = off + i
        q0 = pl.multiple_of(tile * T, T)
        low, high = tile_span(ids, tile, tile)
        low = jnp.where(jnp.logical_and(lax.rem(high - low, 2) == 1, low > 0), low - 1, low)
        count = (high - low + 1) // 2
        turned = (qkv[pl.ds(q0, T), :width] * BF16(HEAD**-0.5)).T
        stacks = [by_head_rows(turned[p * 128 : p * 128 + 128]) for p in range(pairs)]

        def scores(j, peaks):
            k0 = pl.multiple_of((low + 2 * j) * T, T)
            same = same_image(id_col, pl.ds(k0, W2), id_row, tile)
            held = [mm(qkv[pl.ds(k0, W2), width + p * 128 : width + p * 128 + 128], stacks[p]) for p in range(pairs)]
            news = []
            for p, s in enumerate(held):
                s = jnp.where(same, s, -1e30)
                sc[p, j] = s
                news.append(jnp.maximum(peaks[p], jnp.max(s.reshape(W2 // 8, 8, 2 * T), 0)))
            return tuple(news)

        start = tuple(jnp.full((8, 2 * T), -jnp.inf, F32) for _ in range(pairs))
        peaks = lax.fori_loop(0, count, scores, start)
        peaks = [jnp.max(m, 0, keepdims=True) for m in peaks]
        for p in range(pairs):
            acc[p] = jnp.zeros((128, 2 * T), F32)

        def outputs(j, totals):
            k0 = pl.multiple_of((low + 2 * j) * T, T)
            es, news = [], []
            for p in range(pairs):
                e = jnp.exp(sc[p, j] - peaks[p])
                news.append(totals[p] + jnp.sum(e.reshape(W2 // 8, 8, 2 * T), 0))
                es.append(e.astype(BF16))
            held = [mm(vt[p * 128 : p * 128 + 128, pl.ds(k0, W2)], es[p]) for p in range(pairs)]
            for p in range(pairs):
                acc[p] += held[p]
            return tuple(news)

        totals = lax.fori_loop(0, count, outputs, tuple(jnp.zeros((8, 2 * T), F32) for _ in range(pairs)))
        stats = []
        for p in range(pairs):
            total = jnp.sum(totals[p], 0, keepdims=True)
            scaled = acc[p] * (1.0 / total)
            o = jnp.concatenate([scaled[:HEAD, :T], scaled[HEAD:, T:]], 0)
            out[pl.ds(pl.multiple_of(i * T, T), T), p * 128 : p * 128 + 128] = o.T.astype(BF16)
            stat = peaks[p] + jnp.log(total)
            stats += [stat[:, :T], stat[:, T:]]
        lse[i] = jnp.concatenate(stats + [jnp.zeros((4, T), F32)], 0)

    store.wait()


def attn_forward(ids, own_qkv, halo, gain, bias, w, b):
    rows, width = own_qkv.shape[0], own_qkv.shape[1] // 3
    tiles = ids.shape[0]
    pairs = width // 128
    anywhere = pl.BlockSpec(memory_space=pl.ANY)
    return pl.pallas_call(
        functools.partial(attn_forward_kernel, width),
        out_shape=(
            jax.ShapeDtypeStruct((rows, width), BF16),
            jax.ShapeDtypeStruct((rows // T, 16, T), F32),
            jax.ShapeDtypeStruct((2 * rows, 3 * width), BF16),
        ),
        in_specs=[SM, VM, anywhere] + [VM] * 5,
        out_specs=(VM, VM, anywhere),
        scratch_shapes=[
            pltpu.VMEM((2 * rows, 3 * width), BF16),
            pltpu.VMEM((pairs, tiles // 2, W2, 2 * T), F32),
            pltpu.VMEM((width, 2 * rows), BF16),
            pltpu.VMEM((pairs, 128, 2 * T), F32),
            pltpu.VMEM((2 * rows, T), F32),
            pltpu.SemaphoreType.DMA((2,)),
        ],
        compiler_params=pltpu.CompilerParams(vmem_limit_bytes=56 * 2**20),
        name="attention_forward",
    )(ids, ids, own_qkv, halo, gain, bias, w, b)


def attn_backward_kernel(width, carried, ids, id_row, qkv_far, do_far, stats, *refs):
    sources, (out, *targets) = refs[:carried], refs[carried : 2 * carried + 1]
    dq, dk, dv, qt, kt, gt, id_col, qkv, do, sems, carry_sems, *held = refs[2 * carried + 1 :]
    pairs = width // 128
    own = out.shape[0] // T
    off = lax.axis_index("hd") * own
    tiles = id_row.shape[0]
    used_low, used_high = tile_span(ids, off, off + own - 1)

    def carry_in(n):
        return pltpu.make_async_copy(sources[n], held[n], carry_sems.at[0, n])

    def carry_out(n):
        return pltpu.make_async_copy(held[n], targets[n], carry_sems.at[1, n])

    def loads(j):
        rows = pl.ds(pl.multiple_of(j * T, T), T)
        return (
            pltpu.make_async_copy(qkv_far.at[rows, :], qkv.at[rows, :], sems.at[0, j]),
            pltpu.make_async_copy(do_far.at[rows, :], do.at[rows, :], sems.at[1, j]),
        )

    @pl.loop(0, tiles)
    def _(j):
        for load in loads(j):
            load.start()

    for n in range(carried):
        carry_in(n).start()
    id_columns(id_row, id_col)
    dq[...] = jnp.zeros_like(dq)

    @pl.loop(0, tiles)
    def _(j):
        for load in loads(j):
            load.wait()
        rows = pl.ds(pl.multiple_of(j * T, T), T)

        @pl.when(jnp.logical_and(j // 2 >= used_low // 2, j // 2 <= (used_high - 1) // 2))
        def _():
            qt[:, rows] = (qkv[rows, :width] * BF16(HEAD**-0.5)).T
            kt[:, rows] = qkv[rows, width : 2 * width].T
            gt[:, rows] = do[rows, :].T

    for n in range(carried):
        carry_in(n).wait()
        carry_out(n).start()

    @pl.loop(0, tiles // 2)
    def _(j):
        k0 = pl.multiple_of(j * W2, W2)
        mine = jnp.logical_and(2 * j >= off, 2 * j < off + own)
        low, high = tile_span(ids, 2 * j, 2 * j + 1)
        low = jnp.where(mine, low, jnp.maximum(low, off))
        high = jnp.where(mine, high, jnp.minimum(high, off + own))
        for p in range(pairs):
            dk[p] = jnp.zeros((W2, 128), F32)
            dv[p] = jnp.zeros((W2, 128), F32)

        @pl.loop(low, high)
        def _(i):
            q0 = pl.multiple_of(i * T, T)
            same = same_image(id_col, pl.ds(k0, W2), id_row, i)
            qs, gs, ss, ps, es, ds = [], [], [], [], [], []
            for p in range(pairs):
                cols = p * 128
                k = qkv[pl.ds(k0, W2), width + cols : width + cols + 128]
                v = qkv[pl.ds(k0, W2), 2 * width + cols : 2 * width + cols + 128]
                ss.append(mm(k, by_head_rows(qt[cols : cols + 128, pl.ds(q0, T)])))
                ps.append(mm(v, by_head_rows(gt[cols : cols + 128, pl.ds(q0, T)])))
            for p in range(pairs):
                one = jnp.concatenate([stats[i, 2 * p : 2 * p + 1, :], stats[i, 2 * p + 1 : 2 * p + 2, :]], 1)
                two = jnp.concatenate([stats[i, 2 * p + 16 : 2 * p + 17, :], stats[i, 2 * p + 17 : 2 * p + 18, :]], 1)
                e = jnp.exp(jnp.where(same, ss[p], -1e30) - one)
                es.append(e.astype(BF16))
                ds.append((e * (ps[p] - two)).astype(BF16))
            a, b, c = [], [], []
            for p in range(pairs):
                cols = p * 128
                a.append(mm(es[p], by_head(do[pl.ds(q0, T), cols : cols + 128])))
                b.append(mm(ds[p], by_head(qkv[pl.ds(q0, T), cols : cols + 128] * BF16(HEAD**-0.5))))
                c.append(mm(kt[cols : cols + 128, pl.ds(k0, W2)], ds[p]))
            for p in range(pairs):
                dv[p] += a[p]
                dk[p] += b[p]
                dq[p, i] += jnp.concatenate([c[p][:HEAD, :T], c[p][HEAD:, T:]], 0)

        @pl.when(mine)
        def _():
            r0 = pl.multiple_of(j * W2 - off * T, W2)
            for p in range(pairs):
                cols = p * 128
                out[pl.ds(r0, W2), width + cols : width + cols + 128] = dk[p].astype(BF16)
                out[pl.ds(r0, W2), 2 * width + cols : 2 * width + cols + 128] = dv[p].astype(BF16)

    @pl.loop(0, own)
    def _(i):
        for p in range(pairs):
            cols = p * 128
            out[pl.ds(pl.multiple_of(i * T, T), T), cols : cols + 128] = (dq[p, off + i] * HEAD**-0.5).T.astype(BF16)

    for n in range(carried):
        carry_out(n).wait()


def attn_backward(ids, qkv, do, stats, *arrays):
    all_rows, columns = qkv.shape
    own_rows = all_rows // 2
    width = columns // 3
    tiles = all_rows // T
    pairs = width // 128
    anywhere = pl.BlockSpec(memory_space=pl.ANY)
    return pl.pallas_call(
        functools.partial(attn_backward_kernel, width, len(arrays)),
        out_shape=[jax.ShapeDtypeStruct((own_rows, columns), BF16)] + [jax.ShapeDtypeStruct(v.shape, v.dtype) for v in arrays],
        in_specs=[SM, VM, anywhere, anywhere, VM] + [anywhere] * len(arrays),
        out_specs=[VM] + [anywhere] * len(arrays),
        scratch_shapes=[
            pltpu.VMEM((pairs, tiles, 128, T), F32),
            pltpu.VMEM((pairs, W2, 128), F32),
            pltpu.VMEM((pairs, W2, 128), F32),
            pltpu.VMEM((width, all_rows), BF16),
            pltpu.VMEM((width, all_rows), BF16),
            pltpu.VMEM((width, all_rows), BF16),
            pltpu.VMEM((all_rows, T), F32),
            pltpu.VMEM((all_rows, columns), BF16),
            pltpu.VMEM((all_rows, width), BF16),
            pltpu.SemaphoreType.DMA((2, tiles)),
            pltpu.SemaphoreType.DMA((2, max(len(arrays), 1))),
        ]
        + [pltpu.VMEM(v.shape, v.dtype) for v in arrays],
        compiler_params=pltpu.CompilerParams(vmem_limit_bytes=56 * 2**20),
        name="attention_backward",
    )(ids, ids, qkv, do, stats, *arrays)


ln_epsilon = 1e-06
drop_scale = 1.0 / 0.9


MESH = pl.DeviceIdType.MESH


class Place:
    def __init__(self):
        self.seq = lax.axis_index("seq")
        self.x = lax.axis_index("hd")
        self.c = lax.rem(self.seq, 2)
        self.y = lax.rem(self.seq // 2, 2)
        self.z = self.seq // 4

    def partner(self, axis):
        if axis == "c":
            return (self.seq + 1 - 2 * self.c, self.x)
        if axis == "y":
            return (self.seq + 2 - 4 * self.y, self.x)
        return (self.seq, 1 - self.x)

    def level(self, step):
        return (lax.rem(self.z + step, 4) * 4 + lax.rem(self.seq, 4), self.x)

    def index(self, axis):
        return {"x": self.x, "y": self.y, "c": self.c}[axis]


def greet(place):
    barrier = pltpu.get_barrier_semaphore()
    for other in [place.partner(a) for a in "cxy"] + [place.level(d) for d in (1, 2, 3)]:
        pl.semaphore_signal(barrier, inc=1, device_id=other, device_id_type=MESH)


def meet():
    pl.semaphore_wait(pltpu.get_barrier_semaphore(), 6)


def send(source, target, send_sem, recv_sem, other):
    copy = pltpu.make_async_remote_copy(
        src_ref=source, dst_ref=target, send_sem=send_sem, recv_sem=recv_sem, device_id=other, device_id_type=MESH
    )
    copy.start()
    return copy


class Flow:
    def __init__(self, place, axes, g, r0, r1, r2, r3, sems, recvs):
        self.place, self.axes, self.g = place, axes, g
        self.r0, self.r1, self.r2, self.r3 = r0, r1, r2, r3
        self.sems, self.recvs = sems, recvs
        self.copies = []

    def start(self):
        p = self.place
        self.copies.append(send(self.g.at[1 - p.c], self.r0, self.sems.at[0], self.recvs.at[0], p.partner("c")))

    def first(self):
        p = self.place
        self.copies[0].wait_recv()
        me = p.index(self.axes[0])

        def add(half):
            @pl.loop(0, 8)
            def _(i):
                b, z = i // 4, lax.rem(i, 4)
                self.r0[half, b, z] = self.r0[half, b, z] + self.g[p.c, half, b, z]

        add(1 - me)
        self.copies.append(
            send(self.r0.at[1 - me], self.r1, self.sems.at[1], self.recvs.at[1], p.partner(self.axes[0]))
        )
        add(me)

    def second(self):
        p = self.place
        self.copies[1].wait_recv()
        me, before = p.index(self.axes[1]), p.index(self.axes[0])

        def add(half):
            @pl.loop(0, 4)
            def _(z):
                self.r1[half, z] = self.r1[half, z] + self.r0[before, half, z]

        add(1 - me)
        self.copies.append(
            send(self.r1.at[1 - me], self.r2, self.sems.at[2], self.recvs.at[2], p.partner(self.axes[1]))
        )
        add(me)

    def third(self):
        p = self.place
        self.copies[2].wait_recv()
        before = p.index(self.axes[1])

        @pl.loop(0, 4)
        def _(z):
            self.r2[z] = self.r2[z] + self.r1[before, z]

        for d in (1, 2, 3):
            target = lax.rem(p.z + d, 4)
            self.copies.append(
                send(self.r2.at[target], self.r3.at[d - 1], self.sems.at[2 + d], self.recvs.at[2 + d], p.level(d))
            )

    def last(self):
        p = self.place
        total = self.r2[p.z].astype(F32)
        for d in (1, 2, 3):
            self.copies[2 + d].wait_recv()
            total = total + self.r3[d - 1].astype(F32)
        return total

    def finish(self):
        for copy in self.copies:
            copy.wait_send()


def flow_scratch(rows, cols, kind=BF16):
    return [
        pltpu.VMEM((2, 2, 4, rows, cols), kind),
        pltpu.VMEM((2, 4, rows, cols), kind),
        pltpu.VMEM((4, rows, cols), kind),
        pltpu.VMEM((3, rows, cols), kind),
        pltpu.SemaphoreType.DMA((6,)),
        pltpu.SemaphoreType.DMA((6,)),
    ]


class ChunkFlow(Flow):
    def __init__(self, place, axes, home, *refs):
        super().__init__(place, axes, *refs)
        self.home = home

    def third(self):
        p = self.place
        self.copies[2].wait_recv()
        self.r2[...] = self.r2[...] + self.r1[p.index(self.axes[1])]
        slot = lax.rem(p.z - self.home + 3, 4)
        self.hop = pltpu.make_async_remote_copy(
            src_ref=self.r2,
            dst_ref=self.r3.at[slot],
            send_sem=self.sems.at[3],
            recv_sem=self.recvs.at[3 + slot],
            device_id=(self.home * 4 + lax.rem(p.seq, 4), p.x),
            device_id_type=MESH,
        )

        @pl.when(p.z != self.home)
        def _():
            self.hop.start()

    def first(self):
        p = self.place
        self.copies[0].wait_recv()
        me = p.index(self.axes[0])

        def add(half):
            for b in range(2):
                self.r0[half, b] = self.r0[half, b] + self.g[p.c, half, b]

        add(1 - me)
        self.copies.append(
            send(self.r0.at[1 - me], self.r1, self.sems.at[1], self.recvs.at[1], p.partner(self.axes[0]))
        )
        add(me)

    def second(self):
        p = self.place
        self.copies[1].wait_recv()
        me, before = p.index(self.axes[1]), p.index(self.axes[0])
        self.r1[1 - me] = self.r1[1 - me] + self.r0[before, 1 - me]
        self.copies.append(
            send(self.r1.at[1 - me], self.r2, self.sems.at[2], self.recvs.at[2], p.partner(self.axes[1]))
        )
        self.r1[me] = self.r1[me] + self.r0[before, me]

    def last_into(self, out):
        p = self.place

        @pl.when(p.z == self.home)
        def _():
            total = self.r2[...].astype(F32)
            for slot in range(3):
                pltpu.make_async_remote_copy(
                    src_ref=self.r2,
                    dst_ref=self.r3.at[slot],
                    send_sem=self.sems.at[3],
                    recv_sem=self.recvs.at[3 + slot],
                    device_id=p.level(1),
                    device_id_type=MESH,
                ).wait_recv()
                total = total + self.r3[slot].astype(F32)
            out[...] = total

    def finish(self):
        super().finish()

        @pl.when(self.place.z != self.home)
        def _():
            self.hop.wait_send()


class LevelFlow(Flow):
    axes = "zxy"

    def __init__(self, place, g, r0, r1, r2, r3, sems, recvs):
        super().__init__(place, "zxy", g, r0, r1, r2, r3, sems, recvs)

    def first(self):
        p = self.place
        self.copies[0].wait_recv()

        @pl.loop(0, 4)
        def _(z):
            for x in range(2):
                for y in range(2):
                    self.r0[z, x, y] = self.r0[z, x, y] + self.g[p.c, z, x, y]

        for d in (1, 2, 3):
            self.copies.append(
                send(self.r0.at[lax.rem(p.z + d, 4)], self.r1.at[d - 1], self.sems.at[d], self.recvs.at[d], p.level(d))
            )

    def second(self):
        p = self.place
        for d in (1, 2, 3):
            self.copies[d].wait_recv()
        for x in range(2):
            for y in range(2):
                total = self.r0[p.z, x, y].astype(F32)
                for d in range(3):
                    total = total + self.r1[d, x, y].astype(F32)
                self.r1[0, x, y] = total.astype(BF16)
        self.copies.append(
            send(self.r1.at[0, 1 - p.x], self.r2, self.sems.at[4], self.recvs.at[4], p.partner("x"))
        )

    def third(self):
        p = self.place
        self.copies[4].wait_recv()
        for y in range(2):
            self.r2[y] = self.r2[y] + self.r1[0, p.x, y]
        self.copies.append(send(self.r2.at[1 - p.y], self.r3, self.sems.at[5], self.recvs.at[5], p.partner("y")))

    def last(self):
        self.copies[5].wait_recv()
        return self.r2[self.place.y].astype(F32) + self.r3[...].astype(F32)


def level_scratch(rows, cols):
    return [
        pltpu.VMEM((4, 2, 2, rows, cols), BF16),
        pltpu.VMEM((3, 2, 2, rows, cols), BF16),
        pltpu.VMEM((2, rows, cols), BF16),
        pltpu.VMEM((rows, cols), BF16),
        pltpu.SemaphoreType.DMA((6,)),
        pltpu.SemaphoreType.DMA((6,)),
    ]


def chunk_scratch(rows, cols):
    return [
        pltpu.VMEM((2, 2, rows, cols), BF16),
        pltpu.VMEM((2, rows, cols), BF16),
        pltpu.VMEM((rows, cols), BF16),
        pltpu.VMEM((3, rows, cols), BF16),
        pltpu.SemaphoreType.DMA((6,)),
        pltpu.SemaphoreType.DMA((6,)),
    ]


def row_norm(x):
    mean = jnp.mean(x, -1, keepdims=True)
    center = x - mean
    rstd = lax.rsqrt(jnp.mean(center * center, -1, keepdims=True) + ln_epsilon)
    return center * rstd, rstd


def norm_back(hat, rstd, gain, grad):
    scaled = grad * gain
    return rstd * (scaled - jnp.mean(scaled, -1, keepdims=True) - hat * jnp.mean(scaled * hat, -1, keepdims=True))


def col_sum(x):
    return jnp.sum(x, 0, keepdims=True)


def put_blocks(product, z, axes, g):
    half = product.shape[1] // 2
    for y in range(2):
        for c in range(2):
            for x in range(2):
                r = ((y * 2 + c) * 2 + x) * 24
                block = jnp.concatenate([product[r : r + 24, :half], product[r : r + 24, half:]], 0)
                at = {"x": x, "y": y}
                if axes == "zxy":
                    g[c, z, x, y] = block.astype(BF16)
                else:
                    g[c, at[axes[0]], at[axes[1]], z] = block.astype(BF16)


def put_chunk(product, y, axes, g):
    for c in range(2):
        for x in range(2):
            r = (c * 2 + x) * 96
            at = {"x": x, "y": y}
            g[c, at[axes[0]], at[axes[1]]] = product[r : r + 96].astype(BF16)


R = 256
HALO = 608
FLOW_REFS = 6
ORDER = (0, 3, 1, 2)
PATHS1 = ("xy", "xy", "zxy", "xy")
PATHS2 = ("yx", "yx", "yx", "yx")


def mlp_kernel(reduce, chunks, *refs):
    o, lse, x, keep, cot, w_out, b_out, gain, bias, w1, b1, w2, b2 = refs[:13]
    mixed_far, dx1_far, do, stats, small, g_far, out1, out2 = refs[13:21]
    v1, v2, x1s, n2s, n2t, dms, gs, dus, das, macc, nacc, load1, load2, halo_sems = refs[21:35]
    mixed, dx1, g_out, near_sems = refs[35:39]
    flow_refs = refs[39:]
    stores = [
        pltpu.make_async_copy(near, far, near_sems.at[n])
        for n, (near, far) in enumerate(((mixed, mixed_far), (dx1, dx1_far), (g_out, g_far)))
    ]
    side = lax.axis_index("hd")
    base = pl.multiple_of(side * o.shape[0], o.shape[0])
    owner = lax.broadcasted_iota(jnp.int32, (16, o.shape[1]), 1) // HEAD
    heads = (owner == lax.broadcasted_iota(jnp.int32, (16, o.shape[1]), 0)).astype(BF16)
    rows, width = o.shape
    tiles = rows // R
    loads = []
    for k in range(chunks):
        cols = pl.ds(k * width, width)
        loads.append(
            (
                pltpu.make_async_copy(w1.at[:, cols], v1.at[k], load1.at[k]),
                pltpu.make_async_copy(w2.at[cols, :], v2.at[k], load2.at[k]),
            )
        )
        loads[k][0].start()
        loads[k][1].start()
    if reduce:
        place = Place()
        greet(place)
        per = 1 + FLOW_REFS
        flows1 = []
        for k in range(chunks):
            mine = flow_refs[2 * per * k : 2 * per * k + per]
            flows1.append(LevelFlow(place, *mine) if PATHS1[k] == "zxy" else Flow(place, PATHS1[k], *mine))
        flows2 = [ChunkFlow(place, PATHS2[k], k, *flow_refs[2 * per * k + per : 2 * per * (k + 1)]) for k in range(chunks)]

    small[...] = jnp.zeros_like(small)

    @pl.loop(0, tiles)
    def _(t):
        r = pl.ds(pl.multiple_of(t * R, R), R)
        x1 = x[r, :].astype(F32) + keep[r, 0:1] * (mm(o[r, :], w_out[...]) + b_out[...])
        x1s[r, :] = x1
        hat, _ = row_norm(x1)
        n2 = (hat * gain[...] + bias[...]).astype(BF16)
        n2s[r, :] = n2
        dm = (cot[r, :].astype(F32) * keep[r, 1:2]).astype(BF16)
        dms[r, :] = dm
        small[7:8, :] += col_sum(dm.astype(F32))

    n2t[...] = n2s[...].T

    def row_tile(k, t, first, slot):
        r = slice(t * R, t * R + R)
        u = mm(n2s[r, :], v1[k]) + b1[k * width : k * width + width]
        dg = mm_nt(dms[r, :], v2[k])
        cdf = 0.5 + 0.5 * lax.erf(u * 0.7071067811865476)
        pdf = jnp.exp(u * u * -0.5) * 0.3989422804014327
        g = (u * cdf).astype(BF16)
        du = (dg * (cdf + u * pdf)).astype(BF16)
        gs[slot, r, :] = g
        dus[slot, r, :] = du
        small[3 + k : 4 + k, :] += col_sum(du.astype(F32))
        if first:
            macc[r, :] = mm(g, v2[k])
            nacc[r, :] = mm_nt(du, v1[k])
        else:
            macc[r, :] += mm(g, v2[k])
            nacc[r, :] += mm_nt(du, v1[k])

    steps = {}
    if reduce:
        for at, k in enumerate(ORDER[:3]):
            for flow, late in ((flows2[k], 0), (flows1[k], 1)):
                steps.setdefault((at + 1, 1 + late), []).append(flow.first)
                if at < 2:
                    steps.setdefault((at + 2, 1 + late), []).append(flow.second)
                    steps.setdefault((2, 5) if at == 0 else (4, 1 + late), []).append(flow.third)

    def point(*at):
        for step in steps.pop(at, []):
            step()

    def gradient2(k, slot):
        @pl.loop(0, 2)
        def _(y):
            product = mm_tn(gs[slot, :, pl.ds(pl.multiple_of(y * 384, 384), 384)], dms[...])
            put_chunk(product, y, flows2[k].axes, flows2[k].g)

        flows2[k].start()

    def gradient1(k, slot):
        @pl.loop(0, 2)
        def _(h):
            product = mm(n2t[pl.ds(pl.multiple_of(h * 384, 128), 384), :], dus[slot])
            for z in range(2):
                put_blocks(product[z * 192 : z * 192 + 192], 2 * h + z, flows1[k].axes, flows1[k].g)

        flows1[k].start()

    for at, k in enumerate(ORDER if reduce else range(chunks)):
        slot = at % 2
        loads[k][0].wait()
        loads[k][1].wait()
        for t in range(tiles):
            row_tile(k, t, at == 0, slot)
            point(at, t + 1)
        if reduce and at == 0:
            meet()
        if reduce and at < 3:
            gradient2(k, slot)
            point(at, 4)
            gradient1(k, slot)
            point(at, 5)
        if not reduce:

            @pl.loop(0, 3)
            def _(t):
                r = pl.ds(pl.multiple_of(t * 256, 256), 256)
                out2[pl.ds(pl.multiple_of(k * width + t * 256, 256), 256), :] = mm_tn(gs[slot, :, r], dms[...]).astype(BF16)
                out1[r, k * width : k * width + width] = mm(n2t[r, :], dus[slot]).astype(BF16)

    apart = rows - HALO
    pad = pl.multiple_of((1 - side) * (2 * rows - apart), 16)
    do[pl.ds(pad, apart), :] = jnp.zeros((apart, width), BF16)
    stat_tiles = pl.cdiv(HALO, T)
    spare = rows // T - stat_tiles
    for s in range(spare):
        stats[(1 - side) * (2 * rows // T - spare) + s] = jnp.zeros((32, T), F32)
    exchange = []

    def exchange_rows(ref, first, count, n):
        part = ref.at[pl.ds(first, count)]
        exchange.append(send(part, part, halo_sems.at[2 * n], halo_sems.at[2 * n + 1], place.partner("x")))

    for t in range(tiles):
        at = lax.rem(t + 1 - side, tiles)
        r = pl.ds(pl.multiple_of(at * R, R), R)
        hat, rstd = row_norm(x1s[r, :])
        dn2 = nacc[r, :]
        dx = cot[r, :].astype(F32) + norm_back(hat, rstd, gain[...], dn2)
        dx1[r, :] = dx
        da = (dx * keep[r, 0:1]).astype(BF16)
        das[r, :] = da
        grad_o = mm_nt(da, w_out[...]).astype(BF16)
        do[pl.ds(pl.multiple_of(base + at * R, R), R), :] = grad_o
        small[0:1, :] += col_sum(da.astype(F32))
        small[1:2, :] += col_sum(dn2 * hat)
        small[2:3, :] += col_sum(dn2)
        prod = grad_o.astype(F32) * o[r, :].astype(F32)
        high = prod.astype(BF16)
        low = (prod - high.astype(F32)).astype(BF16)
        sums = mm_nt(heads, high) + mm_nt(heads, low)
        for s in range(R // T):
            own = at * (R // T) + s
            stats[side * (rows // T) + own, :16] = lse[own]
            stats[side * (rows // T) + own, 16:] = sums[:, s * T : s * T + T]
        point(chunks, t + 1)
        if reduce and t == 0:
            exchange_rows(do, pl.multiple_of(base + at * R, R), R, 0)

    if reduce:
        third, fourth = ORDER[2], ORDER[3]
        exchange_rows(stats, spare + side * stat_tiles, stat_tiles, 3)
        gradient2(fourth, 1)
        gradient1(fourth, 1)

    stores[1].start()
    n2t[...] = o[...].T
    if reduce:

        @pl.loop(0, 2)
        def _(h):
            product = mm(n2t[pl.ds(pl.multiple_of(h * 384, 128), 384), :], das[...])
            for z in range(2):
                put_blocks(product[z * 192 : z * 192 + 192], 2 * h + z, "zxy", g_out)

        flows2[fourth].first()
        flows1[fourth].first()
        flows2[third].second()
        flows1[third].second()
    else:

        @pl.loop(0, 3)
        def _(t):
            r = pl.ds(pl.multiple_of(t * 256, 256), 256)
            g_out[r, :] = mm(n2t[r, :], das[...]).astype(BF16)

    @pl.loop(0, tiles)
    def _(t):
        r = pl.ds(pl.multiple_of(t * R, R), R)
        mixed[r, :] = (x1s[r, :] + keep[r, 1:2] * (macc[r, :] + b2[...])).astype(BF16)

    stores[0].start()
    stores[2].start()

    if reduce:
        half = width // 2

        def keep_share(k):
            total = flows1[k].last()
            out1[:, k * width : k * width + half] = total[:24]
            out1[:, k * width + half : (k + 1) * width] = total[24:]
            flows2[k].last_into(out2)

        for at in sorted(steps):
            point(*at)
        second_tile = 2 - side
        exchange_rows(do, pl.multiple_of(base + second_tile * R, R), R, 1)
        flows2[third].third()
        flows1[third].third()
        flows2[fourth].second()
        exchange_rows(do, pl.multiple_of(base + (1 - side) * apart + side * 2 * R, 16), HALO - 2 * R, 2)
        flows1[fourth].second()
        flows2[fourth].third()
        flows1[fourth].third()
        for k in range(chunks):
            keep_share(k)
        for k in range(chunks):
            flows1[k].finish()
            flows2[k].finish()
        for copy in exchange:
            copy.wait()
    for store in stores:
        store.wait()


def mlp_step(reduce, o, lse, x, keep, cot, w_out, b_out, gain, bias, w1, b1, w2, b2):
    rows, width = o.shape
    chunks = w1.shape[1] // width
    block = lambda dims, kind: jax.ShapeDtypeStruct(dims, kind)
    outs = [
        block((rows, width), BF16),
        block((rows, width), F32),
        block((2 * rows, width), BF16),
        block((2 * rows // T, 32, T), F32),
        block((16, width), F32),
    ]
    if reduce:
        outs += [block((2, 4, 2, 2, 48, width // 2), BF16), block((24, chunks * width), F32), block((96, width), F32)]
    else:
        outs += [block((width, width), BF16), block(w1.shape, BF16), block(w2.shape, BF16)]
    scratch = [
        pltpu.VMEM((chunks, width, width), BF16),
        pltpu.VMEM((chunks, width, width), BF16),
        pltpu.VMEM((rows, width), F32),
        pltpu.VMEM((rows, width), BF16),
        pltpu.VMEM((width, rows), BF16),
        pltpu.VMEM((rows, width), BF16),
        pltpu.VMEM((2, rows, width), BF16),
        pltpu.VMEM((2, rows, width), BF16),
        pltpu.VMEM((rows, width), BF16),
        pltpu.VMEM((rows, width), F32),
        pltpu.VMEM((rows, width), F32),
        pltpu.SemaphoreType.DMA((chunks,)),
        pltpu.SemaphoreType.DMA((chunks,)),
        pltpu.SemaphoreType.DMA((8,)),
        pltpu.VMEM((rows, width), BF16),
        pltpu.VMEM((rows, width), F32),
        pltpu.VMEM(outs[5].shape, BF16),
        pltpu.SemaphoreType.DMA((3,)),
    ]
    params = dict(vmem_limit_bytes=60 * 2**20)
    if reduce:
        for k in range(chunks):
            if PATHS1[k] == "zxy":
                scratch += [pltpu.VMEM((2, 4, 2, 2, 48, width // 2), BF16)] + level_scratch(48, width // 2)
            else:
                scratch += [pltpu.VMEM((2, 2, 2, 4, 48, width // 2), BF16)] + flow_scratch(48, width // 2)
            scratch += [pltpu.VMEM((2, 2, 2, 96, width), BF16)] + chunk_scratch(96, width)
        params.update(collective_id=1, has_side_effects=True)
    anywhere = pl.BlockSpec(memory_space=pl.ANY)
    return pl.pallas_call(
        functools.partial(mlp_kernel, reduce, chunks),
        out_shape=outs,
        in_specs=[VM] * 9 + [anywhere, VM, anywhere, VM],
        out_specs=[anywhere, anywhere, VM, VM, VM, anywhere, VM, VM],
        scratch_shapes=scratch,
        compiler_params=pltpu.CompilerParams(**params),
        name="mlp_step",
    )(o, lse, x, keep, cot, w_out, b_out, gain, bias, w1, b1, w2, b2)


SMALLS = ((8, 1), (9, 1), (10, 2), (0, 1), (1, 1), (2, 1), (3, 4), (7, 1))


def by_owner(sums):
    width = sums.shape[1]
    lane = lax.broadcasted_iota(jnp.int32, (32, width), 1)
    block = lax.broadcasted_iota(jnp.int32, (32, width), 0)
    source = lax.broadcasted_iota(jnp.int32, (width, 128), 0)
    target = lax.broadcasted_iota(jnp.int32, (width, 128), 1)
    parts = []
    for first, rows in SMALLS:
        size = rows * width // 32
        row = block // (32 // rows)
        spread = jnp.zeros((32, width), F32)
        for r in range(rows):
            spread = jnp.where(row == r, sums[first + r : first + r + 1, :], spread)
        spread = jnp.where(lane // size == lax.rem(block, 32 // rows), spread, 0.0)
        pick = (lax.rem(source, size) == target).astype(BF16)
        total = jnp.zeros((32, 128), F32)
        for _ in range(3):
            piece = spread.astype(BF16)
            total = total + mm(piece, pick)
            spread = spread - piece.astype(F32)
        parts.append(total.reshape(32, 1, 128))
    return jnp.concatenate(parts, 1)


def tail_kernel(reduce, *refs):
    dqkv, x, dx1_far, gain, n1t, w_far, g_out, small_in = refs[:8]
    grad_far, grad_w, grad_o, small = refs[8:12]
    dx1, w, near_sems = refs[12:15]
    rest = refs[15:]
    load_w = pltpu.make_async_copy(w_far, w, near_sems.at[0])
    load_x = pltpu.make_async_copy(dx1_far, dx1, near_sems.at[1])
    load_w.start()
    load_x.start()
    rows, width = x.shape
    tiles = rows // R
    if reduce:
        place = Place()
        greet(place)
        out_flow = LevelFlow(place, g_out, *rest[:6])
        flows = [Flow(place, ("yx", "xy", "yx")[i], *rest[6 + 7 * i : 13 + 7 * i]) for i in range(3)]
        sums = Flow(place, "xy", *rest[27:34])

    if reduce:
        meet()
        out_flow.start()
        for i in range(3):

            @pl.loop(0, 2)
            def _(h):
                product = mm(n1t[pl.ds(pl.multiple_of(h * 384, 128), 384), :], dqkv[:, i * width : (i + 1) * width])
                for z in range(2):
                    put_blocks(product[z * 192 : z * 192 + 192], 2 * h + z, flows[i].axes, flows[i].g)

            flows[i].start()
            if i == 0:
                out_flow.first()
            else:
                flows[i - 1].first()
    else:

        @pl.loop(0, 3)
        def _(t):
            r = pl.ds(pl.multiple_of(t * 256, 256), 256)
            for i in range(3):
                grad_w[r, i * width : (i + 1) * width] = mm(n1t[r, :], dqkv[:, i * width : (i + 1) * width]).astype(BF16)

    small_ref = rest[34] if reduce else small
    small_ref[...] = small_in[...]

    def rows_back(t):
        r = pl.ds(pl.multiple_of(t * R, R), R)
        hat, rstd = row_norm(x[r, :].astype(F32))
        dn1 = mm_nt(dqkv[r, :], w[...])
        dx1[r, :] = dx1[r, :] + norm_back(hat, rstd, gain[...], dn1)
        small_ref[8:9, :] += col_sum(dn1 * hat)
        small_ref[9:10, :] += col_sum(dn1)
        small_ref[10:11, :] += col_sum(dqkv[r, :width].astype(F32))
        small_ref[11:12, :] += col_sum(dqkv[r, 2 * width :].astype(F32))

    if reduce:
        flows[2].first()
    load_w.wait()
    load_x.wait()
    pl.loop(0, tiles)(rows_back)
    store_x = pltpu.make_async_copy(dx1, grad_far, near_sems.at[2])
    store_x.start()
    if reduce:
        half = width // 2
        shares = by_owner(small_ref[...])
        for b in range(32):
            sums.g[b // 2 % 2, b % 2, b // 4 % 2, b // 8] = shares[b]
        sums.start()
        flows[0].second()
        sums.first()
        flows[1].second()
        out_flow.second()
        sums.second()
        flows[0].third()
        out_flow.third()
        flows[1].third()
        sums.third()
        flows[2].second()
        flows[2].third()
        total = out_flow.last()
        grad_o[:, :half] = total[:24]
        grad_o[:, half:] = total[24:]
        small[...] = sums.last()
        for i in range(3):
            total = flows[i].last()
            grad_w[:, i * width : i * width + half] = total[:24]
            grad_w[:, i * width + half : (i + 1) * width] = total[24:]
        for flow in (out_flow, *flows, sums):
            flow.finish()
    store_x.wait()


def tail_step(reduce, dqkv, x, dx1, gain, n1t, w, g_out, small):
    rows, width = x.shape
    block = lambda dims, kind: jax.ShapeDtypeStruct(dims, kind)
    outs = [block((rows, width), F32)]
    scratch = [
        pltpu.VMEM((rows, width), F32),
        pltpu.VMEM(w.shape, BF16),
        pltpu.SemaphoreType.DMA((3,)),
    ]
    anywhere = pl.BlockSpec(memory_space=pl.ANY)
    params = dict(vmem_limit_bytes=60 * 2**20)
    args = [dqkv, x, dx1, gain, n1t, w, g_out, small]
    if reduce:
        outs += [block((24, 3 * width), F32), block((24, width), F32), block((8, 128), F32)]
        scratch += level_scratch(48, width // 2)
        for _ in range(3):
            scratch += [pltpu.VMEM((2, 2, 2, 4, 48, width // 2), BF16)] + flow_scratch(48, width // 2)
        scratch += [pltpu.VMEM((2, 2, 2, 4, 8, 128), F32)] + flow_scratch(8, 128, F32)
        scratch += [pltpu.VMEM((16, width), F32)]
        params.update(collective_id=2, has_side_effects=True)
    else:
        outs += [block(w.shape, BF16), block((8, 128), F32), block((16, width), F32)]
    return pl.pallas_call(
        functools.partial(tail_kernel, reduce),
        out_shape=outs,
        in_specs=[VM, VM, anywhere, VM, VM, anywhere, VM, VM],
        out_specs=[anywhere, VM, VM, VM],
        scratch_shapes=scratch,
        compiler_params=pltpu.CompilerParams(**params),
        name="tail_step",
    )(*args)


def project_kernel(x, gain, bias, w, b, out, turned):
    @pl.loop(0, x.shape[0] // T)
    def _(t):
        r = pl.ds(pl.multiple_of(t * T, T), T)
        hat, _ = row_norm(x[r, :].astype(F32))
        n1 = (hat * gain[...] + bias[...]).astype(BF16)
        out[r, :] = (mm(n1, w[...]) + b[...]).astype(BF16)
        turned[:, r] = n1.T


def project(x, gain, bias, w, b):
    return pl.pallas_call(
        project_kernel,
        out_shape=(
            jax.ShapeDtypeStruct((x.shape[0], w.shape[1]), BF16),
            jax.ShapeDtypeStruct((x.shape[1], x.shape[0]), BF16),
        ),
        in_specs=[VM] * 5,
        out_specs=(VM, VM),
        compiler_params=pltpu.CompilerParams(vmem_limit_bytes=32 * 2**20),
        cost_estimate=pl.CostEstimate(flops=2 * x.shape[0] * w.shape[0] * w.shape[1], bytes_accessed=9 * 2**20, transcendentals=0),
        name="project",
    )(x, gain, bias, w, b)


def finish_kernel(small, far, *refs):
    near, sems = refs[-2:]
    copied = (len(refs) - 3 - len(SMALLS)) // 2
    loads, stores = [], []
    for n in range(4):
        rows = pl.ds(n * (near.shape[0] // 4), near.shape[0] // 4)
        loads.append(pltpu.make_async_copy(far.at[rows, :], near.at[rows, :], sems.at[0, n]))
        stores.append(pltpu.make_async_copy(near.at[rows, :], refs[copied].at[rows, :], sems.at[1, n]))
        loads[n].start()
    for source, target in zip(refs[:copied], refs[copied + 1 : 2 * copied + 1]):
        target[...] = source[...]
    for row, out in enumerate(refs[2 * copied + 1 : -2]):
        out[...] = small[row, : out.shape[0]]
    for load, store in zip(loads, stores):
        load.wait()
        store.start()
    for store in stores:
        store.wait()


def finish(shards, small, large, *arrays):
    width = large.shape[1]
    anywhere = pl.BlockSpec(memory_space=pl.ANY)
    outs = [jax.ShapeDtypeStruct(a.shape, a.dtype) for a in (large, *arrays)]
    outs += [jax.ShapeDtypeStruct((rows * width // shards,), F32) for _, rows in SMALLS]
    return pl.pallas_call(
        finish_kernel,
        out_shape=outs,
        in_specs=[VM, anywhere] + [VM] * len(arrays),
        out_specs=[anywhere] + [VM] * (len(outs) - 1),
        scratch_shapes=[pltpu.VMEM(large.shape, large.dtype), pltpu.SemaphoreType.DMA((2, 4))],
        name="finish",
    )(small, large, *arrays)


def halo_of(rows, halo, side):
    mine = jnp.where(side == 0, rows[rows.shape[0] - halo :], rows[:halo])
    return lax.ppermute(mine, "hd", [(0, 1), (1, 0)])


def in_pack_order(own, halo, side, before=0, after=0):
    dims = (own.shape[0] - halo.shape[0], *own.shape[1:])
    late, early = jnp.full(dims, after, own.dtype), jnp.full(dims, before, own.dtype)
    return jnp.where(side == 0, jnp.concatenate([own, halo, late], 0), jnp.concatenate([early, halo, own], 0))


def per_device(tokens, image_ids, keep_masks, ln1_gain, ln1_bias, w_qkv, qv_bias, w_out, b_out,
               ln2_gain, ln2_bias, w_fc1, b_fc1, w_fc2, b_fc2, cotangent):
    rows, width = tokens.shape
    halo = HALO
    both = ("seq", "hd")
    side = lax.axis_index("hd")
    reduce = lax.axis_size("seq") == 16 and lax.axis_size("hd") == 2
    halo_tiles = pl.cdiv(halo, T)
    tok_halo = halo_of(tokens, halo, side)
    id_halo = halo_of(image_ids, halo, side)
    id_all = in_pack_order(image_ids, id_halo, side, -1, 1 << 20)
    ids = id_all.reshape(-1, T)
    one_hot = (image_ids[:, None] == jnp.arange(keep_masks.shape[1], dtype=jnp.int32)[None, :]).astype(F32)
    keep_rows = jnp.dot(one_hot, keep_masks[0].astype(F32)) * drop_scale
    bias_all = jnp.concatenate([qv_bias[:width], jnp.zeros((width,), F32), qv_bias[width:]])

    norm1 = (ln1_gain, ln1_bias, w_qkv, bias_all)
    qkv_own, n1t = project(tokens, *norm1)
    heads_out, lse, qkv_all = attn_forward(ids, qkv_own, tok_halo, *norm1)
    mixed, dx1, do_all, stats_all, small, g_out, grad_fc1, grad_fc2 = mlp_step(
        reduce, heads_out, lse, tokens, keep_rows, cotangent, w_out, b_out, ln2_gain, ln2_bias,
        w_fc1, b_fc1, w_fc2, b_fc2)
    if not reduce:
        first = side * rows
        do_own = lax.dynamic_slice_in_dim(do_all, first, rows, 0)
        stats_own = lax.dynamic_slice_in_dim(stats_all, first // T, rows // T, 0)
        do_all = in_pack_order(do_own, halo_of(do_own, halo, side), side)
        stats_all = in_pack_order(stats_own, halo_of(stats_own, halo_tiles, side), side)
    dqkv, *carried = attn_backward(ids, qkv_all, do_all, stats_all, *((mixed, grad_fc1, grad_fc2) if reduce else ()))
    if reduce:
        mixed, grad_fc1, grad_fc2 = carried
    grad_x, grad_qkv, grad_out, small = tail_step(
        reduce, dqkv, tokens, dx1, ln1_gain, n1t, w_qkv, g_out, small)
    if not reduce:
        grad_out = g_out

        def scatter(v):
            return lax.psum_scatter(v, both, scatter_dimension=0, tiled=True).astype(F32)

        grad_fc1, grad_fc2, grad_qkv, grad_out = map(scatter, (grad_fc1, grad_fc2, grad_qkv, grad_out))
        small = lax.psum(small, both)
    shards = lax.axis_size("seq") * lax.axis_size("hd")
    if reduce:
        grad_x, grad_qkv, grad_out, *vectors = finish(shards, small, grad_x, grad_qkv, grad_out)
    else:
        place = lax.axis_index("seq") * lax.axis_size("hd") + side
        vectors = []
        for first, count in SMALLS:
            size = count * width // shards
            vectors.append(lax.dynamic_slice(small[first : first + count].reshape(-1), (place * size,), (size,)))
    g1, b1, qv, bo, g2, b2, bf1, bf2 = vectors
    return mixed, grad_x, g1, b1, grad_qkv, qv, grad_out, bo, g2, b2, grad_fc1, bf1, grad_fc2, bf2


def solution(mesh):
    both = P(("seq", "hd"))
    split = P(("seq", "hd"), None)
    return jax.shard_map(
        per_device,
        mesh=mesh,
        in_specs=(split, both, P("seq", None, None)) + (P(),) * 12 + (split,),
        out_specs=(split, split, both, both, split, both, split, both, both, both, split, both, split, both),
        check_vma=False,
    )
```
